32 devices in a mesh: shard: 4 (over y, core), ctx: 2 (over x), tp: 4 (over z).
Axes of the slice: x: 2, y: 2, z: 4, core: 2. Of those that a mesh axis runs over, the one named last changes fastest.
Arguments:
- tokens: bfloat16 [16, 788, 768], P(('shard', 'tp'), 'ctx'), may hold values from -6 to 6
- cotangent: bfloat16 [16, 788, 768], P(('shard', 'tp'), 'ctx'), may hold values from -6 to 6
- routing: int32 [16, 788, 2], P(('shard', 'tp'), 'ctx'), may hold values from 0 to 7, all different within a row; in each aligned block of 394 rows (0 to 393, 394 to 787, ..., all dimensions but the last counted through in order) at most 197 rows name the same one
- gating: float32 [16, 788, 2], P(('shard', 'tp'), 'ctx'), may hold values from 0.2 to 0.8
- inward: bfloat16 [3, 768, 768], P(None, ('shard', 'ctx', 'tp')), may hold values from -0.21875 to 0.21875
- outward: bfloat16 [768, 768], P(('shard', 'ctx', 'tp')), may hold values from -1.25 to 1.25
- scales: bfloat16 [2, 768], P(None, ('shard', 'ctx', 'tp')), may hold values from 0.5 to 1.5
- shifts: bfloat16 [2, 768], P(None, ('shard', 'ctx', 'tp')), may hold values from -1.5 to 1.5
- upward: bfloat16 [8, 768, 3072], P(None, ('shard', 'ctx'), 'tp'), may hold values from -0.21875 to 0.21875
- downward: bfloat16 [8, 768, 3072], P(None, ('shard', 'ctx'), 'tp'), may hold values from -0.21875 to 0.21875
- inward_moment: float32 [3, 768, 768], P(None, ('shard', 'ctx', 'tp')), may hold values from -12 to 12
- outward_moment: float32 [768, 768], P(('shard', 'ctx', 'tp')), may hold values from -12 to 12
- scales_moment: float32 [2, 768], P(None, ('shard', 'ctx', 'tp')), may hold values from -12 to 12
- shifts_moment: float32 [2, 768], P(None, ('shard', 'ctx', 'tp')), may hold values from -12 to 12
- upward_moment: float32 [8, 768, 3072], P(None, ('shard', 'ctx'), 'tp'), may hold values from -24 to 24
- downward_moment: float32 [8, 768, 3072], P(None, ('shard', 'ctx'), 'tp'), may hold values from -24 to 24
Outputs:
- result: bfloat16 [16, 788, 768], P(('shard', 'tp'), 'ctx')
- input_grad: float32 [16, 788, 768], P(('shard', 'tp'), 'ctx')
- inward_grad: float32 [3, 768, 768], P(None, ('shard', 'ctx', 'tp'))
- outward_grad: float32 [768, 768], P(('shard', 'ctx', 'tp'))
- scales_grad: float32 [2, 768], P(None, ('shard', 'ctx', 'tp'))
- shifts_grad: float32 [2, 768], P(None, ('shard', 'ctx', 'tp'))
- upward_grad: float32 [8, 768, 3072], P(None, ('shard', 'ctx'), 'tp')
- downward_grad: float32 [8, 768, 3072], P(None, ('shard', 'ctx'), 'tp')
- inward_state: float32 [3, 768, 768], P(None, ('shard', 'ctx', 'tp'))
- outward_state: float32 [768, 768], P(('shard', 'ctx', 'tp'))
- scales_state: float32 [2, 768], P(None, ('shard', 'ctx', 'tp'))
- shifts_state: float32 [2, 768], P(None, ('shard', 'ctx', 'tp'))
- upward_state: float32 [8, 768, 3072], P(None, ('shard', 'ctx'), 'tp')
- downward_state: float32 [8, 768, 3072], P(None, ('shard', 'ctx'), 'tp')
- inward_new: float32 [3, 768, 768], P(None, ('shard', 'ctx', 'tp'))
- outward_new: float32 [768, 768], P(('shard', 'ctx', 'tp'))
- scales_new: float32 [2, 768], P(None, ('shard', 'ctx', 'tp'))
- shifts_new: float32 [2, 768], P(None, ('shard', 'ctx', 'tp'))
- upward_new: float32 [8, 768, 3072], P(None, ('shard', 'ctx'), 'tp')
- downward_new: float32 [8, 768, 3072], P(None, ('shard', 'ctx'), 'tp')
The draws below stay inside these ranges and needn't reach their ends.
Inputs may be any that keep to these rules, and one draw needn't show every extreme that they name: `routing`: in each aligned block of 394 rows (the rows of one device) no expert is named by more than 197 of them; the 2 experts of a row differ.
All inputs are finite; a program needn't handle non-finite values.
Results may differ from the reference program's by a relative error of at most 0.022.
Values may be sent and summed in bfloat16 or wider, within the bound.
A program may use at most 320 MiB of HBM per device.

```python
import math
import jax
import jax.numpy as jnp
import numpy as np
from jax import lax

D = 768
HEADS = 12
HEAD_DIM = 64
F = 3072
LEN = 197
EXPERTS = 8
TOP = 2
SEQS = 4
ROWS = 788
TOK_DEV = 394
GROUPS = 16
TOKENS = 12608
CAP = 197


def block_scale(own_key, extent, cuts, low, high):
    loudness, own = 1.0, jax.random.fold_in(own_key, 6)
    for dim, shards_of in cuts:
        steps = jnp.exp(jax.random.uniform(jax.random.fold_in(own, dim), (shards_of,), jnp.float32, low / len(cuts), high / len(cuts)))
        loudness = loudness * jnp.repeat(steps, extent[dim] // shards_of).reshape([-1 if axis == dim else 1 for axis in range(len(extent))])
    return loudness


def shared_out(own_key, own, number, rows, count, top, most, skew):
    sequence = jax.random.permutation(own_key, count)
    crowded, common = load_shares(count, rows * top, most, skew, True), load_shares(count, rows * top, most, skew, False)
    places = jnp.arange(count)

    def named(sizes, offset_by):
        used = int((sizes > 0).sum())
        fixed = max(1, used // 4)
        passed = fixed + (places - fixed + offset_by * (used - fixed)) % max(1, count - fixed)
        return jnp.zeros((count,), jnp.int32).at[sequence[jnp.where(places < fixed, places, passed)]].set(jnp.asarray(sizes, jnp.int32))

    sizes = jnp.where(number % 4 == 0, named(crowded, number // 4), named(common, number - number // 4 - 1))
    mixed = jax.random.permutation(jax.random.fold_in(own, 3), count)
    donor, taker = mixed[0:count // 2 * 2:2], mixed[1:count // 2 * 2:2]
    room = jnp.minimum(sizes[donor] - 1, most - sizes[taker]) // 2
    room = jnp.where((donor == sequence[0]) | (taker == sequence[0]) | (sizes[taker] == 0), 0, jnp.maximum(room, 0))
    passed = jax.random.randint(jax.random.fold_in(own, 4), (count // 2,), 0, 1 << 20) % (room + 1)
    sizes = sizes.at[donor].add(-passed).at[taker].add(passed)
    labels = jnp.searchsorted(jnp.cumsum(sizes), jnp.arange(rows * top), side="right").astype(jnp.int32)
    table = labels.reshape(top, rows).T
    table = table[jax.random.permutation(jax.random.fold_in(own, 1), rows)]
    offset_by = jax.random.randint(jax.random.fold_in(own, 2), (rows, 1), 0, top)
    return jnp.take_along_axis(table, (jnp.arange(top)[None, :] + offset_by) % top, axis=1)


def load_shares(amount, total, reach, skew, full):
    portions = [(1 << 20) // math.isqrt(standing ** skew) + 1 for standing in range(1, amount + 1)]
    largest = reach if full else min(reach, max(-(-total // amount), total * portions[0] // sum(portions)))
    least = 1 if total - largest >= amount - 1 else 0
    counts, surplus = [largest] + [least] * (amount - 1), total - largest - least * (amount - 1)
    while surplus > 0:
        free = [i for i in range(1, amount) if counts[i] < largest] or [i for i in range(1, amount) if counts[i] < reach]
        mass, left = sum([portions[i] for i in free]), surplus
        for i in free:
            more = min(reach - counts[i], max(1, left * portions[i] // mass), surplus)
            counts[i] = counts[i] + more
            surplus = surplus - more
    return np.array(counts)


def scatter_about(rng, dims, scale, reach, pieces=(), held_as=jnp.bfloat16):
    factor_of = block_scale(rng, dims, pieces, -0.22, 0.18) if pieces else 1.0
    drawn = jax.random.normal(rng, dims, jnp.float32) * scale * factor_of
    return jnp.minimum(jnp.maximum(drawn, -reach), reach).astype(held_as)


def setup_inputs(seed: int = 0) -> dict:
    seeds = jax.random.split(jax.random.key(seed), 17)
    tokens = scatter_about(seeds[0], (GROUPS, ROWS, D), 1.0, 6.0, ((0, 16), (1, 2)))
    cotangent = scatter_about(seeds[1], (GROUPS, ROWS, D), 1.0, 6.0, ((0, 16), (1, 2)))
    routing_keys = jax.random.split(jax.random.fold_in(seeds[2], 1), GROUPS * ROWS // TOK_DEV)
    routing_turns = jax.random.permutation(jax.random.fold_in(seeds[2], 3), GROUPS * ROWS // TOK_DEV)
    routing = jax.vmap(lambda own, number: shared_out(jax.random.fold_in(seeds[2], 2), own, number, TOK_DEV, EXPERTS, TOP, CAP, 2))(routing_keys, routing_turns).reshape((GROUPS, ROWS, TOP))
    gating = jnp.clip(0.2 + 0.6 * jax.random.uniform(seeds[3], (GROUPS, ROWS, TOP), jnp.float32) ** block_scale(seeds[3], (GROUPS, ROWS, TOP), ((0, 16), (1, 2)), -0.2, 0.2), 0.2, 0.8)
    inward = scatter_about(seeds[4], (3, D, D), D ** -0.5, 0.21875, ((1, 32),))
    outward = scatter_about(seeds[5], (D, D), (D // 32) ** -0.5, 1.25, ((0, 32),))
    scales = jnp.clip(1.0 + 0.1 * jax.random.normal(seeds[6], (2, D), jnp.float32), 0.5, 1.5).astype(jnp.bfloat16)
    shifts = scatter_about(seeds[7], (2, D), 0.3, 1.5, ((1, 32),))
    upward = scatter_about(seeds[8], (EXPERTS, D, F), D ** -0.5, 0.21875, ((1, 8), (2, 4)))
    downward = scatter_about(seeds[9], (EXPERTS, D, F), (F // 4) ** -0.5, 0.21875, ((1, 8), (2, 4)))
    inward_moment = scatter_about(seeds[10], (3, D, D), 2.0, 12.0, ((1, 32),), jnp.float32)
    outward_moment = scatter_about(seeds[11], (D, D), 2.0, 12.0, ((0, 32),), jnp.float32)
    scales_moment = scatter_about(seeds[12], (2, D), 2.0, 12.0, ((1, 32),), jnp.float32)
    shifts_moment = scatter_about(seeds[13], (2, D), 2.0, 12.0, ((1, 32),), jnp.float32)
    upward_moment = scatter_about(seeds[14], (EXPERTS, D, F), 4.0, 24.0, ((1, 8), (2, 4)), jnp.float32)
    downward_moment = scatter_about(seeds[15], (EXPERTS, D, F), 4.0, 24.0, ((1, 8), (2, 4)), jnp.float32)
    return dict(tokens=tokens, cotangent=cotangent, routing=routing, gating=gating, inward=inward, outward=outward, scales=scales, shifts=shifts, upward=upward, downward=downward, inward_moment=inward_moment, outward_moment=outward_moment, scales_moment=scales_moment, shifts_moment=shifts_moment, upward_moment=upward_moment, downward_moment=downward_moment)


@jax.custom_vjp
def low(v):
    return lax.optimization_barrier(v.astype(jnp.bfloat16)).astype(jnp.float32)

@jax.custom_vjp
def low_back(v):
    return v

def low_keep(v):
    return (low(v), None)

def low_pass(kept, grad):
    return (grad,)

def back_keep(v):
    return (v, None)

def back_low(kept, grad):
    return (low(grad),)
low.defvjp(low_keep, low_pass)
low_back.defvjp(back_keep, back_low)
highest = lax.Precision.HIGHEST
first_coef = 3.4445
second_coef = -4.775
third_coef = 2.0315
momentum_decay = 0.9

def both_ways(value):
    return low_back(low(value))

def normalize(values, factor, offset):
    average = lax.optimization_barrier(jnp.mean(values, axis=-1, keepdims=True))
    centred = values - average
    spread = lax.optimization_barrier(jnp.mean(centred * centred, axis=-1, keepdims=True))
    return centred * lax.rsqrt(spread + 1e-06) * factor + offset

def slot_sources(routes, experts, capacity):
    pairs = routes.shape[0] * routes.shape[1]
    chosen = routes.reshape(pairs).astype(jnp.int32)
    onehot = (chosen[:, None] == jnp.arange(experts, dtype=jnp.int32)[None, :]).astype(jnp.int32)
    earlier = (jnp.cumsum(onehot, axis=0) - onehot).astype(jnp.int32)
    placed = (lax.optimization_barrier(jnp.sum(earlier * onehot, axis=1)) + chosen * capacity).astype(jnp.int32)
    matches = placed[None, :] == jnp.arange(experts * capacity, dtype=jnp.int32)[:, None]
    source = lax.optimization_barrier(jnp.sum(jnp.where(matches, jnp.arange(pairs, dtype=jnp.int32)[None, :], 0), axis=1)).astype(jnp.int32)
    filled = jnp.any(matches, axis=1)
    return (placed, source, filled)

def attend(members):
    queries, keys_all, values_all = members
    scores = low_back(jnp.einsum('sqhd,skhd->shqk', queries, keys_all, precision=highest) * HEAD_DIM ** (-0.5))
    probabilities = low(jax.nn.softmax(scores, axis=-1))
    blended = jnp.einsum('shqk,skhd->sqhd', probabilities, values_all, precision=highest)
    return both_ways(blended)

def expert_pass(members):
    inputs, upper, lower = members
    before = low_back(jnp.dot(inputs, upper, precision=highest))
    hidden = low(jax.nn.gelu(before))
    return low_back(jnp.einsum('cf,df->cd', hidden, lower, precision=highest))

def orthogonal(update):
    summed = jnp.sqrt(jnp.sum(update * update))
    current = update / (summed + 1e-07)
    for repeat in range(5):
        square = jnp.dot(current, current.T, precision=highest)
        power = jnp.dot(square, square, precision=highest)
        mixer = second_coef * square + third_coef * power
        current = first_coef * current + jnp.dot(mixer, current, precision=highest)
    return current

def advance(gradient, moment):
    current = momentum_decay * moment + (1.0 - momentum_decay) * gradient
    return (current, (1.0 - momentum_decay) * gradient + momentum_decay * current)

def reference(tokens, cotangent, routing, gating, inward, outward, scales, shifts, upward, downward, inward_moment, outward_moment, scales_moment, shifts_moment, upward_moment, downward_moment):
    blocks = TOKENS // TOK_DEV

    def sources_of(routes):
        return slot_sources(routes, EXPERTS, CAP)
    placed, source, filled = lax.map(sources_of, routing.reshape(blocks, TOK_DEV, TOP))
    gate_rows = gating.astype(jnp.float32).reshape(blocks, TOK_DEV, TOP, 1)
    fill_rows = filled.astype(jnp.float32)[..., None]

    def take_rows(block_rows, block_source):
        return block_rows[block_source // TOP]

    def pick_rows(block_out, block_place):
        return block_out[block_place]

    def layer(inputs, w_in, w_out, factor, offset, upper, lower):
        flat_rows = inputs.reshape(TOKENS, D)
        normed = low(normalize(flat_rows, factor[0], offset[0]))
        projected = []
        for member in range(3):
            made = both_ways(jnp.dot(normed, w_in[member], precision=highest))
            projected.append(made.reshape(GROUPS, SEQS, LEN, HEADS, HEAD_DIM))
        blended = lax.map(jax.checkpoint(attend), tuple(projected)).reshape(TOKENS, D)
        residual = flat_rows + low_back(jnp.dot(blended, w_out, precision=highest))
        second = low(normalize(residual, factor[1], offset[1])).reshape(blocks, TOK_DEV, D)
        gathered = jax.vmap(take_rows)(second, source) * fill_rows
        grouped = gathered.reshape(blocks, EXPERTS, CAP, D).transpose(1, 0, 2, 3).reshape(EXPERTS, blocks * CAP, D)
        expert_out = lax.map(jax.checkpoint(expert_pass), (grouped, upper, lower))
        expert_out = expert_out.reshape(EXPERTS, blocks, CAP, D).transpose(1, 0, 2, 3).reshape(blocks, EXPERTS * CAP, D)
        picked = jax.vmap(pick_rows)(expert_out, placed).reshape(blocks, TOK_DEV, TOP, D)
        mixture = lax.optimization_barrier(jnp.sum(picked * gate_rows, axis=2)).reshape(TOKENS, D)
        return (residual + mixture).reshape(GROUPS, ROWS, D)
    primals = (tokens.astype(jnp.float32), inward.astype(jnp.float32), outward.astype(jnp.float32), scales.astype(jnp.float32), shifts.astype(jnp.float32), upward.astype(jnp.float32), downward.astype(jnp.float32))
    output, pullback = jax.vjp(layer, *primals)
    gradients = pullback(cotangent.astype(jnp.float32))
    input_grad, inward_grad, outward_grad, scales_grad, shifts_grad, upward_grad, downward_grad = gradients
    inward_state, inward_push = advance(inward_grad, inward_moment)
    outward_state, outward_push = advance(outward_grad, outward_moment)
    scales_state, scales_push = advance(scales_grad, scales_moment)
    shifts_state, shifts_push = advance(shifts_grad, shifts_moment)
    upward_state, upward_push = advance(upward_grad, upward_moment)
    downward_state, downward_push = advance(downward_grad, downward_moment)
    inward_new = primals[1] - lax.map(orthogonal, inward_push)
    outward_new = primals[2] - orthogonal(outward_push)
    upward_new = primals[5] - 2.0 * lax.map(orthogonal, upward_push)
    downward_new = primals[6] - lax.map(orthogonal, downward_push)
    vector_rate = 0.6 / math.sqrt(TOKENS)
    scales_new = primals[3] - vector_rate * scales_push
    shifts_new = primals[4] - vector_rate * shifts_push
    return (output.astype(jnp.bfloat16), input_grad, inward_grad, outward_grad, scales_grad, shifts_grad, upward_grad, downward_grad, inward_state, outward_state, scales_state, shifts_state, upward_state, downward_state, inward_new, outward_new, scales_new, shifts_new, upward_new, downward_new)
```

```python
import functools
import math

import jax
import jax.numpy as jnp
import numpy as np
from jax import lax
from jax.experimental import pallas as pl
from jax.experimental.pallas import tpu as pltpu
from jax.sharding import PartitionSpec as P

HEAD_DIM = 64
LEN = 197


first_coef = 3.4445
second_coef = -4.775
third_coef = 2.0315
momentum_decay = 0.9
norm_epsilon = 1e-06
orth_epsilon = 1e-07
highest = lax.Precision.HIGHEST


def normalize(values, factor, offset):
    average = jnp.mean(values, axis=-1, keepdims=True)
    centred = values - average
    inverse = lax.rsqrt(jnp.mean(centred * centred, axis=-1, keepdims=True) + norm_epsilon)
    unit_rows = centred * inverse
    return (unit_rows * factor + offset, unit_rows, inverse)


def normalize_back(gradient, unit_rows, inverse, factor):
    inner = gradient * factor
    average = jnp.mean(inner, axis=-1, keepdims=True)
    along = jnp.mean(inner * unit_rows, axis=-1, keepdims=True)
    back = inverse * (inner - average - unit_rows * along)
    return (back, jnp.sum(gradient * unit_rows, axis=0), jnp.sum(gradient, axis=0))


def slot_sources(routes, experts, capacity):
    pairs = routes.shape[0] * routes.shape[1]
    chosen = routes.reshape(pairs)
    onehot = (chosen[:, None] == jnp.arange(experts, dtype=jnp.int32)[None, :]).astype(jnp.int32)
    earlier = jnp.cumsum(onehot, axis=0) - onehot
    placed = jnp.sum(earlier * onehot, axis=1) + chosen * capacity
    matches = placed[None, :] == jnp.arange(experts * capacity, dtype=jnp.int32)[:, None]
    source = jnp.sum(jnp.where(matches, jnp.arange(pairs, dtype=jnp.int32)[None, :], 0), axis=1)
    filled = jnp.any(matches, axis=1)
    return (placed, source, filled)


def orthogonal(matrix):
    summed = jnp.sqrt(jnp.sum(matrix * matrix))
    current = matrix / (summed + orth_epsilon)
    for repeat in range(5):
        square = lax.dot_general(
            current,
            current,
            (((1,), (1,)), ((), ())),
            precision=highest,
            preferred_element_type=jnp.float32,
        )
        power = jnp.dot(square, square, precision=highest, preferred_element_type=jnp.float32)
        mixer = second_coef * square + third_coef * power
        current = first_coef * current + jnp.dot(
            mixer, current, precision=highest, preferred_element_type=jnp.float32
        )
    return current


def advance(gradient, moment):
    current = momentum_decay * moment + (1.0 - momentum_decay) * gradient
    return (current, (1.0 - momentum_decay) * gradient + momentum_decay * current)


def expert_weights(upward, downward):
    return (
        lax.all_gather(upward, ("shard", "ctx"), axis=1, tiled=True),
        lax.all_gather(downward, ("shard", "ctx"), axis=1, tiled=True),
    )


def on_device(
    tokens,
    cotangent,
    routing,
    gating,
    inward,
    outward,
    scales,
    shifts,
    upward,
    downward,
    inward_moment,
    outward_moment,
    scales_moment,
    shifts_moment,
    upward_moment,
    downward_moment,
):
    rows_here = tokens.shape[1]
    features = tokens.shape[2]
    experts = upward.shape[0]
    top_count = routing.shape[2]
    capacity = 2 * top_count * rows_here // experts
    attn_scale = HEAD_DIM ** (-0.5)
    inputs = tokens[0].astype(jnp.float32)
    routes = routing[0]
    gate_pairs = gating[0].reshape(-1)
    zero_low = jnp.zeros((), jnp.bfloat16)
    full_in, full_out, all_scales, all_shifts = (
        lax.all_gather(inward, ("shard", "ctx", "tp"), axis=1, tiled=True),
        lax.all_gather(outward, ("shard", "ctx", "tp"), axis=0, tiled=True),
        lax.all_gather(scales, ("shard", "ctx", "tp"), axis=1, tiled=True),
        lax.all_gather(shifts, ("shard", "ctx", "tp"), axis=1, tiled=True),
    )
    factor = all_scales.astype(jnp.float32)
    offset = all_shifts.astype(jnp.float32)
    normed, unit_one, inverse_one = normalize(inputs, factor[0], offset[0])
    normed_low = normed.astype(jnp.bfloat16)
    projected = jnp.einsum(
        "td,kde->kte", normed_low, full_in, preferred_element_type=jnp.float32
    ).astype(jnp.bfloat16)
    head_rows = lax.all_to_all(projected, "ctx", split_axis=2, concat_axis=1, tiled=True)
    group_rows = head_rows.shape[1]
    head_width = head_rows.shape[2]
    seqs_here = group_rows // LEN
    shaped = head_rows.reshape(3, seqs_here, LEN, head_width // HEAD_DIM, HEAD_DIM)
    query_rows, key_rows, value_rows = (shaped[0], shaped[1], shaped[2])
    scores = (
        jnp.einsum("sqhd,skhd->shqk", query_rows, key_rows, preferred_element_type=jnp.float32)
        * attn_scale
    )
    top_score = jnp.max(scores, axis=-1, keepdims=True)
    logsum = top_score + jnp.log(jnp.sum(jnp.exp(scores - top_score), axis=-1, keepdims=True))
    soft_low = jnp.exp(scores - logsum).astype(jnp.bfloat16)
    blended = jnp.einsum(
        "shqk,skhd->sqhd", soft_low, value_rows, preferred_element_type=jnp.float32
    ).astype(jnp.bfloat16)
    blended_tokens = lax.all_to_all(
        blended.reshape(group_rows, head_width), "ctx", split_axis=0, concat_axis=1, tiled=True
    )
    residual = inputs + jnp.dot(blended_tokens, full_out, preferred_element_type=jnp.float32)
    second, unit_two, inverse_two = normalize(residual, factor[1], offset[1])
    second_low = second.astype(jnp.bfloat16)
    upstream = cotangent[0].astype(jnp.float32)
    placed, source, filled = slot_sources(routes, experts, capacity)
    slot_rows = jnp.where(filled[:, None], second_low[source // top_count], zero_low)
    slot_rows = slot_rows.reshape(experts, capacity, features)
    group_slots = lax.all_gather(slot_rows, "tp", axis=1, tiled=True)
    upper_full, lower_full = expert_weights(upward, downward)
    before = jnp.einsum("ecd,edf->ecf", group_slots, upper_full, preferred_element_type=jnp.float32)
    hidden = jax.nn.gelu(before).astype(jnp.bfloat16)
    partial_out = jnp.einsum("ecf,edf->ecd", hidden, lower_full, preferred_element_type=jnp.float32)
    own_out = lax.psum_scatter(
        partial_out.astype(jnp.bfloat16), "tp", scatter_dimension=1, tiled=True
    ).astype(jnp.float32)
    picked = own_out.reshape(experts * capacity, features)[placed].reshape(
        rows_here, top_count, features
    )
    mixture = jnp.sum(picked * gating[0][:, :, None], axis=1)
    result = (residual + mixture).astype(jnp.bfloat16)
    slot_grad = jnp.where(
        filled[:, None], upstream[source // top_count] * gate_pairs[source][:, None], 0.0
    )
    slot_grad = slot_grad.astype(jnp.bfloat16).reshape(experts, capacity, features)
    group_grad = lax.all_gather(slot_grad, "tp", axis=1, tiled=True)
    upper_full, lower_full = expert_weights(upward, downward)
    d_hidden = jnp.einsum(
        "ecd,edf->ecf", group_grad, lower_full, preferred_element_type=jnp.float32
    )
    unused, gelu_back = jax.vjp(jax.nn.gelu, before)
    d_before = gelu_back(d_hidden)[0].astype(jnp.bfloat16)
    lower_part = jnp.einsum("ecd,ecf->edf", group_grad, hidden, preferred_element_type=jnp.float32)
    upper_part = jnp.einsum(
        "ecd,ecf->edf", group_slots, d_before, preferred_element_type=jnp.float32
    )
    slot_input_part = jnp.einsum(
        "ecf,edf->ecd", d_before, upper_full, preferred_element_type=jnp.float32
    )
    slot_input = lax.psum_scatter(
        slot_input_part.astype(jnp.bfloat16), "tp", scatter_dimension=1, tiled=True
    ).astype(jnp.float32)
    d_second = jnp.sum(
        slot_input.reshape(experts * capacity, features)[placed].reshape(
            rows_here, top_count, features
        ),
        axis=1,
    )
    d_norm_two, scale_two, shift_two = normalize_back(d_second, unit_two, inverse_two, factor[1])
    d_residual = upstream + d_norm_two
    d_attended = d_residual.astype(jnp.bfloat16)
    outward_part = jnp.einsum(
        "td,te->de", blended_tokens, d_attended, preferred_element_type=jnp.float32
    )
    d_blended = jnp.einsum(
        "te,de->td", d_attended, full_out, preferred_element_type=jnp.float32
    ).astype(jnp.bfloat16)
    d_heads = lax.all_to_all(d_blended, "ctx", split_axis=1, concat_axis=0, tiled=True)
    d_heads = d_heads.reshape(seqs_here, LEN, head_width // HEAD_DIM, HEAD_DIM)
    soft_full = jnp.exp(
        jnp.einsum("sqhd,skhd->shqk", query_rows, key_rows, preferred_element_type=jnp.float32)
        * attn_scale
        - logsum
    )
    d_soft = jnp.einsum("sqhd,skhd->shqk", d_heads, value_rows, preferred_element_type=jnp.float32)
    value_grad = jnp.einsum(
        "shqk,sqhd->skhd", soft_low, d_heads, preferred_element_type=jnp.float32
    ).astype(jnp.bfloat16)
    row_inner = jnp.sum(soft_full * d_soft, axis=-1, keepdims=True)
    d_scores = (soft_full * (d_soft - row_inner)).astype(jnp.bfloat16)
    query_grad = (
        jnp.einsum("shqk,skhd->sqhd", d_scores, key_rows, preferred_element_type=jnp.float32)
        * attn_scale
    ).astype(jnp.bfloat16)
    key_grad = (
        jnp.einsum("shqk,sqhd->skhd", d_scores, query_rows, preferred_element_type=jnp.float32)
        * attn_scale
    ).astype(jnp.bfloat16)
    stacked_grad = jnp.stack([query_grad, key_grad, value_grad]).reshape(3, group_rows, head_width)
    token_grad = lax.all_to_all(stacked_grad, "ctx", split_axis=1, concat_axis=2, tiled=True)
    inward_part = jnp.einsum(
        "td,kte->kde", normed_low, token_grad, preferred_element_type=jnp.float32
    )
    d_normed = jnp.einsum("kte,kde->td", token_grad, full_in, preferred_element_type=jnp.float32)
    d_norm_one, scale_one, shift_one = normalize_back(d_normed, unit_one, inverse_one, factor[0])
    input_grad = d_residual + d_norm_one
    inward_grad, outward_grad, scales_grad, shifts_grad = (
        lax.psum_scatter(inward_part, ("shard", "ctx", "tp"), scatter_dimension=1, tiled=True),
        lax.psum_scatter(outward_part, ("shard", "ctx", "tp"), scatter_dimension=0, tiled=True),
        lax.psum_scatter(
            jnp.stack([scale_one, scale_two]),
            ("shard", "ctx", "tp"),
            scatter_dimension=1,
            tiled=True,
        ),
        lax.psum_scatter(
            jnp.stack([shift_one, shift_two]),
            ("shard", "ctx", "tp"),
            scatter_dimension=1,
            tiled=True,
        ),
    )
    upward_grad, downward_grad = (
        lax.psum_scatter(
            upper_part.astype(jnp.bfloat16), ("shard", "ctx"), scatter_dimension=1, tiled=True
        ).astype(jnp.float32),
        lax.psum_scatter(
            lower_part.astype(jnp.bfloat16), ("shard", "ctx"), scatter_dimension=1, tiled=True
        ).astype(jnp.float32),
    )
    inward_state, inward_push = advance(inward_grad, inward_moment)
    outward_state, outward_push = advance(outward_grad, outward_moment)
    scales_state, scales_push = advance(scales_grad, scales_moment)
    shifts_state, shifts_push = advance(shifts_grad, shifts_moment)
    upward_state, upward_push = advance(upward_grad, upward_moment)
    downward_state, downward_push = advance(downward_grad, downward_moment)
    devices = lax.axis_size(("shard", "ctx", "tp"))
    outer_count = lax.axis_size(("shard", "ctx"))
    inner_count = lax.axis_size("tp")
    rows_local = upward.shape[1]
    cols_local = upward.shape[2]
    slot_size = rows_local * cols_local
    attention_size = inward.shape[1] * features
    full_cols = inner_count * cols_local

    def flat_pad(portion):
        flatten = portion.reshape(portion.shape[0], -1)
        return jnp.pad(flatten, ((0, 0), (0, slot_size - flatten.shape[1])))

    matrices = jnp.concatenate(
        [
            flat_pad(inward_push),
            flat_pad(outward_push[None]),
            upward_push.reshape(experts, slot_size),
            downward_push.reshape(experts, slot_size),
        ]
    )
    matrix_count = matrices.shape[0]
    owner_table = np.arange(matrix_count) * devices // matrix_count
    outgoing = jnp.zeros((devices, slot_size), jnp.float32).at[owner_table].set(matrices)
    received = lax.all_to_all(
        outgoing.astype(jnp.bfloat16),
        ("shard", "ctx", "tp"),
        split_axis=0,
        concat_axis=0,
        tiled=True,
    ).astype(outgoing.dtype)
    myself = lax.axis_index(("shard", "ctx", "tp"))
    owned = (
        jnp.sum(
            jnp.where(
                jnp.asarray(owner_table, dtype=jnp.int32) == myself,
                jnp.arange(matrix_count, dtype=jnp.int32) + 1,
                0,
            )
        )
        - 1
    )
    attention_kind = jnp.logical_and(owned >= 0, owned < 4)
    expert_form = (
        received.reshape(outer_count, inner_count, rows_local, cols_local)
        .transpose(0, 2, 1, 3)
        .reshape(features, full_cols)
    )
    attention_form = jnp.pad(
        received[:, :attention_size].reshape(features, features),
        ((0, 0), (0, full_cols - features)),
    )
    orthogonal_form = orthogonal(jnp.where(attention_kind, attention_form, expert_form))
    back_expert = (
        orthogonal_form.reshape(outer_count, rows_local, inner_count, cols_local)
        .transpose(0, 2, 1, 3)
        .reshape(devices, slot_size)
    )
    back_attention = jnp.pad(
        orthogonal_form[:, :features].reshape(devices, attention_size),
        ((0, 0), (0, slot_size - attention_size)),
    )
    returned = lax.all_to_all(
        jnp.where(attention_kind, back_attention, back_expert).astype(jnp.bfloat16),
        ("shard", "ctx", "tp"),
        split_axis=0,
        concat_axis=0,
        tiled=True,
    ).astype(jnp.float32)
    mine_parts = returned[owner_table]
    inward_new = inward.astype(jnp.float32) - mine_parts[:3, :attention_size].reshape(inward.shape)
    outward_new = outward.astype(jnp.float32) - mine_parts[3, :attention_size].reshape(
        outward.shape
    )
    upward_new = upward.astype(jnp.float32) - 2.0 * mine_parts[4 : 4 + experts].reshape(
        upward.shape
    )
    downward_new = downward.astype(jnp.float32) - mine_parts[4 + experts :].reshape(downward.shape)
    total_tokens = lax.axis_size("shard") * lax.axis_size("ctx") * lax.axis_size("tp") * rows_here
    vector_rate = 0.6 / math.sqrt(total_tokens)
    scales_new = scales.astype(jnp.float32) - vector_rate * scales_push
    shifts_new = shifts.astype(jnp.float32) - vector_rate * shifts_push
    return (
        result[None],
        input_grad[None],
        inward_grad,
        outward_grad,
        scales_grad,
        shifts_grad,
        upward_grad,
        downward_grad,
        inward_state,
        outward_state,
        scales_state,
        shifts_state,
        upward_state,
        downward_state,
        inward_new,
        outward_new,
        scales_new,
        shifts_new,
        upward_new,
        downward_new,
    )


axes = ("shard", "ctx", "tp")
TILE = 256
SPAN = 208
VMEM_ASK = 60 * 1024 * 1024


def dot_nn(left, right):
    return lax.dot_general(
        left, right, (((1,), (0,)), ((), ())), preferred_element_type=jnp.float32
    )


def dot_nt(left, right):
    return lax.dot_general(
        left, right, (((1,), (1,)), ((), ())), preferred_element_type=jnp.float32
    )


def dot_tn(left, right):
    return lax.dot_general(
        left, right, (((0,), (0,)), ((), ())), preferred_element_type=jnp.float32
    )


def tile_pairs(count):
    return [(row, col) for row in range(count) for col in range(row, count)]


def wide_bands(size):
    return [pl.ds(start, TILE) for start in range(0, size, TILE)]


def wide_steps(count, gram, whole, low, whole_low, mixer):
    bands = wide_bands(gram.shape[0])

    def step(repeat, carry):
        wide_mix(gram, whole, low, whole_low, mixer)
        for band in bands:
            half = first_coef * gram[band, :] + dot_nn(mixer[band, :], low[...])
            gram[band, :] = first_coef * half + dot_nn(half.astype(jnp.bfloat16), mixer[...])
            whole[band, :] = first_coef * whole[band, :] + dot_nn(mixer[band, :], whole_low[...])
        return carry

    lax.fori_loop(0, count, step, 0)


def wide_mix(gram, whole, low, whole_low, mixer):
    low[...] = gram[...].astype(jnp.bfloat16)
    whole_low[...] = whole[...].astype(jnp.bfloat16)
    for band in wide_bands(gram.shape[0]):
        squared = dot_nn(low[band, :], low[...])
        mixer[band, :] = (second_coef * gram[band, :] + third_coef * squared).astype(jnp.bfloat16)


def wide_first_kernel(block0, block1, block3, part0, part1, part2, gram, whole, low, mixer, whole_low, block2):
    size = gram.shape[0]
    bands = wide_bands(size)
    rows = lax.broadcasted_iota(jnp.int32, (TILE, size), 0)
    cols = lax.broadcasted_iota(jnp.int32, (TILE, size), 1)
    for part, band in zip((part0, part1, part2), bands):
        block2[band, :] = part[...]
    trace = 0.0
    for place, band in enumerate(bands):
        part = dot_nt(block0[band, :], block0[...])
        for block in (block1, block2, block3):
            part = part + dot_nt(block[band, :], block[...])
        gram[band, :] = part
        trace = trace + jnp.sum(jnp.where(rows + place * TILE == cols, part, 0.0))
    factor = 1.0 / (jnp.sqrt(trace) + orth_epsilon)
    for place, band in enumerate(bands):
        gram[band, :] = gram[band, :] * (factor * factor)
        whole[band, :] = jnp.where(rows + place * TILE == cols, factor, 0.0)
    wide_steps(2, gram, whole, low, whole_low, mixer)


def wide_last_kernel(gram_in, whole_in, out, gram, whole, low, mixer, whole_low):
    bands = wide_bands(gram.shape[0])
    gram[...] = gram_in[...]
    whole[...] = whole_in[...]
    wide_steps(2, gram, whole, low, whole_low, mixer)
    wide_mix(gram, whole, low, whole_low, mixer)
    for row, band in enumerate(bands):
        last = first_coef * whole[band, :] + dot_nn(mixer[band, :], whole_low[...])
        for place, pair in enumerate(tile_pairs(len(bands))):
            if pair[0] == row:
                out[place] = last[:, pair[1] * TILE : (pair[1] + 1) * TILE].astype(out.dtype)


def wide_call(kernel, size, out_shape, kept, scratch, name, inputs):
    vmem = pl.BlockSpec(memory_space=pltpu.VMEM)
    square = (size, size)
    return pl.pallas_call(
        kernel,
        out_shape=out_shape,
        in_specs=[vmem] * len(inputs),
        out_specs=jax.tree.map(lambda shape: vmem, out_shape),
        scratch_shapes=[pltpu.VMEM(square, jnp.float32)] * kept
        + [pltpu.VMEM(square, jnp.bfloat16)] * scratch,
        compiler_params=pltpu.CompilerParams(vmem_limit_bytes=VMEM_ASK),
        cost_estimate=pl.CostEstimate(
            flops=20 * size**3, bytes_accessed=8 * size * size, transcendentals=0
        ),
        name=name,
    )(*inputs)


def wide_first(blocks):
    size = blocks[0].shape[0]
    shape = jax.ShapeDtypeStruct((size, size), jnp.float32)
    return wide_call(wide_first_kernel, size, [shape, shape], 0, 4, "wide_first", blocks)


def wide_last(gram, whole):
    size = gram.shape[0]
    pairs = len(tile_pairs(size // TILE))
    shape = jax.ShapeDtypeStruct((pairs, TILE, TILE), jnp.bfloat16)
    return wide_call(wide_last_kernel, size, shape, 2, 3, "wide_last", (gram, whole))


def store_rows(chip, value, outs, which):
    depth = outs[0].shape[2]
    for turn, out in enumerate(outs):
        other = jnp.bitwise_xor(chip, turn)
        for core in range(2):
            row = ((other // 2) * 2 + core) * 2 + other % 2
            out[which, core] = value[pl.ds(pl.multiple_of(row * depth, 16), depth), :].astype(
                out.dtype
            )


def apply_kernel(place, *refs):
    mixers, pushes, outs, (full, moved) = refs[:4], refs[4:6], refs[6:10], refs[10:]
    chip, core, tp = place[0], place[1], place[2]
    count = full.shape[0] // TILE
    for which in range(2):
        source = lax.rem(tp - 2 * core - which + 4, 4)
        for step in range(4):

            @pl.when(source == step)
            def _():
                for spot, (row, col) in enumerate(tile_pairs(count)):
                    tile = mixers[step][spot]
                    full[pl.ds(row * TILE, TILE), pl.ds(col * TILE, TILE)] = tile
                    if row != col:
                        full[pl.ds(col * TILE, TILE), pl.ds(row * TILE, TILE)] = tile.T

        for spot in range(2):

            @pl.when(lax.rem(tp + spot, 2) == which)
            def _():
                moved[...] = dot_nn(full[...], pushes[spot][...])

        store_rows(chip, moved, outs, which)


def apply_mixers(place, mixers, pushes, depth):
    size, width = pushes[0].shape
    vmem = pl.BlockSpec(memory_space=pltpu.VMEM)
    shape = jax.ShapeDtypeStruct((2, 2, depth, width), jnp.bfloat16)
    return pl.pallas_call(
        apply_kernel,
        in_specs=[pl.BlockSpec(memory_space=pltpu.SMEM)] + [vmem] * 6,
        out_specs=[vmem] * 4,
        out_shape=[shape] * 4,
        scratch_shapes=[
            pltpu.VMEM((size, size), jnp.bfloat16),
            pltpu.VMEM((size, width), jnp.float32),
        ],
        compiler_params=pltpu.CompilerParams(vmem_limit_bytes=VMEM_ASK),
        cost_estimate=pl.CostEstimate(
            flops=4 * size**3, bytes_accessed=10 * size * size, transcendentals=0
        ),
        name="apply_mixers",
    )(place, *mixers, *pushes)


def push_kernel(place, own, *refs):
    gots, moments, refs = refs[:2], refs[2:6], refs[6:]
    pushes, outs, (total,) = refs[:2], refs[2:6], refs[6:]
    chip, core, tp = place[0], place[1], place[2]
    keep = 1.0 - momentum_decay
    depth = outs[0].shape[2]
    for which in range(2):
        total[...] = (
            own[which].astype(jnp.float32)
            + gots[0][which].astype(jnp.float32)
            + gots[1][which].astype(jnp.float32)
        )
        store_rows(chip, total, outs, which)
        for turn, moment in enumerate(moments):
            other = jnp.bitwise_xor(chip, turn)
            for side in range(2):
                row = ((other // 2) * 2 + jnp.bitwise_xor(core, side)) * 2 + other % 2
                rows = pl.ds(pl.multiple_of(row * depth, 16), depth)
                pushed = (
                    (keep + momentum_decay * keep) * total[rows, :]
                    + momentum_decay * momentum_decay * moment[2 * which + side].astype(jnp.float32)
                ).astype(jnp.bfloat16)
                for spot in range(2):

                    @pl.when(lax.rem(tp + spot, 2) == which)
                    def _():
                        pushes[spot][rows, :] = pushed


def push_rows(place, own, gots, moments):
    size, width = own.shape[1:]
    depth = moments[0].shape[1]
    vmem = pl.BlockSpec(memory_space=pltpu.VMEM)
    rows = jax.ShapeDtypeStruct((2, 2, depth, width), jnp.bfloat16)
    return pl.pallas_call(
        push_kernel,
        in_specs=[pl.BlockSpec(memory_space=pltpu.SMEM)] + [vmem] * 7,
        out_specs=[vmem] * 6,
        out_shape=[jax.ShapeDtypeStruct((size, width), jnp.bfloat16)] * 2 + [rows] * 4,
        scratch_shapes=[pltpu.VMEM((size, width), jnp.float32)],
        compiler_params=pltpu.CompilerParams(vmem_limit_bytes=VMEM_ASK),
        cost_estimate=pl.CostEstimate(
            flops=20 * size * width, bytes_accessed=24 * size * width, transcendentals=0
        ),
        name="push_rows",
    )(place, own, *gots, *moments)


def square_kernel(matrix, out, current, low, square, square_low, mixer):
    size = current.shape[0]
    bands = [pl.ds(start, TILE) for start in range(0, size, TILE)]
    total = 0.0
    for band in bands:
        part = matrix[band, :].astype(jnp.float32)
        total = total + jnp.sum(part * part)
    factor = 1.0 / (jnp.sqrt(total) + orth_epsilon)
    for band in bands:
        current[band, :] = matrix[band, :].astype(jnp.float32) * factor

    def step(repeat, carry):
        low[...] = current[...].astype(jnp.bfloat16)
        for band in bands:
            part = dot_nt(low[band, :], low[...])
            square[band, :] = part
            square_low[band, :] = part.astype(jnp.bfloat16)
        for band in bands:
            mixed = second_coef * square[band, :] + third_coef * dot_nn(
                square_low[band, :], square_low[...]
            )
            mixer[band, :] = mixed.astype(jnp.bfloat16)
        for band in bands:
            current[band, :] = first_coef * current[band, :] + dot_nn(mixer[band, :], low[...])
        return carry

    lax.fori_loop(0, 5, step, 0)
    out[...] = current[...].astype(out.dtype)


def orthogonal_square(matrix):
    size = matrix.shape[0]
    return pl.pallas_call(
        square_kernel,
        out_shape=jax.ShapeDtypeStruct((size, size), jnp.bfloat16),
        in_specs=[pl.BlockSpec(memory_space=pltpu.VMEM)],
        out_specs=pl.BlockSpec(memory_space=pltpu.VMEM),
        scratch_shapes=[
            pltpu.VMEM((size, size), jnp.float32),
            pltpu.VMEM((size, size), jnp.bfloat16),
            pltpu.VMEM((size, size), jnp.float32),
            pltpu.VMEM((size, size), jnp.bfloat16),
            pltpu.VMEM((size, size), jnp.bfloat16),
        ],
        compiler_params=pltpu.CompilerParams(vmem_limit_bytes=VMEM_ASK),
        cost_estimate=pl.CostEstimate(
            flops=30 * size**3, bytes_accessed=4 * matrix.size, transcendentals=0
        ),
        name="square_orthogonal",
    )(matrix)


root = math.sqrt(2.0 / math.pi)


def gelu_pair(value):
    squared = value * value
    part = 0.5 * jnp.tanh(value * (root + (root * 0.044715) * squared)) + 0.5
    bend = value * (2.0 * root + (6.0 * root * 0.044715) * squared)
    return value * part, part + part * (1.0 - part) * bend


def one_hot(rank):
    return lax.broadcasted_iota(jnp.int32, (SPAN, rank.shape[1]), 0) == rank


def assemble(chip, core, pieces, whole):
    depth = pieces[0].shape[1]
    for place, piece in enumerate(pieces):
        other = jnp.bitwise_xor(chip, place // 2)
        row = ((other // 2) * 2 + jnp.bitwise_xor(core, place % 2)) * 2 + other % 2
        whole[pl.ds(pl.multiple_of(row * depth, 16), depth), :] = piece[0]


def gate_of(hot, gate):
    return jnp.sum(jnp.where(hot, gate, 0.0), axis=1, keepdims=True)


def experts_kernel(
    starts, rank, gate, *refs
):
    blocks = rank.shape[1]
    ups, downs, refs = refs[:8], refs[8:16], refs[16:]
    tokens_hbm, refs = refs[: 2 * blocks], refs[2 * blocks :]
    hidden_out, before_out, *refs = refs
    outs, refs = refs[:5], refs[5:]
    rows, cots, upper, lower, slots, grads, upper_sum, lower_sum, leaving, sems, out_sems = refs
    targets = [(outs[turn].at[0], outs[turn].at[1]) for turn in range(3)] + [(outs[3], outs[4])]
    expert = pl.program_id(0)
    base = expert * (blocks + 1)
    chip = starts[pl.num_programs(0) * (blocks + 1)]
    core = starts[pl.num_programs(0) * (blocks + 1) + 1]
    low = jnp.bfloat16

    @pl.when(expert == 0)
    def _():
        copies = []
        for block in range(blocks):
            for which, held in enumerate((rows, cots)):
                place = which * blocks + block
                copies.append(
                    pltpu.make_async_copy(tokens_hbm[place], held.at[block], sems.at[place])
                )
        for copy in copies:
            copy.start()

    assemble(chip, core, ups, upper)
    assemble(chip, core, downs, lower)

    for block in range(blocks):

        @pl.when(expert == 0)
        def _():
            for which, held in enumerate((rows, cots)):
                place = which * blocks + block
                pltpu.make_async_copy(tokens_hbm[place], held.at[block], sems.at[place]).wait()

        start = pl.multiple_of(starts[base + block], 16)
        hot = one_hot(rank[0, block : block + 1, :])
        spread = jnp.where(hot, 1.0, 0.0).astype(low)
        weight = gate_of(hot, gate[0, block : block + 1, :])
        slots[pl.ds(start, SPAN), :] = dot_nn(spread, rows[block]).astype(low)
        grads[pl.ds(start, SPAN), :] = (dot_nn(spread, cots[block]) * weight).astype(low)

    end = pl.multiple_of(starts[base + blocks], 16)
    slots[pl.ds(end, TILE), :] = jnp.zeros((TILE, slots.shape[1]), low)
    grads[pl.ds(end, TILE), :] = jnp.zeros((TILE, slots.shape[1]), low)
    upper_sum[...] = jnp.zeros_like(upper_sum)
    lower_sum[...] = jnp.zeros_like(lower_sum)

    def work(tile, carry):
        band = pl.ds(pl.multiple_of(tile * TILE, TILE), TILE)
        slot_rows, slot_grads = slots[band, :], grads[band, :]
        hidden, slope = gelu_pair(dot_nn(slot_rows, upper[...]))
        hidden = hidden.astype(low)
        d_before = (dot_nn(slot_grads, lower[...]) * slope).astype(low)
        hidden_out[0, band, :] = hidden
        before_out[0, band, :] = d_before
        upper_sum[...] += dot_tn(slot_rows, d_before)
        lower_sum[...] += dot_tn(slot_grads, hidden)
        return carry

    lax.fori_loop(0, (starts[base + blocks] + TILE - 1) // TILE, work, 0)

    for turn, target in enumerate(targets):

        @pl.when(expert == turn)
        def _():
            if turn > 0:
                for which in range(2):
                    pltpu.make_async_copy(
                        leaving.at[which], targets[turn - 1][which], out_sems.at[2 * turn - 2 + which]
                    ).wait()
            leaving[0] = upper_sum[...].astype(low)
            leaving[1] = lower_sum[...].astype(low)
            copies = [
                pltpu.make_async_copy(leaving.at[which], target[which], out_sems.at[2 * turn + which])
                for which in range(2)
            ]
            for copy in copies:
                copy.start()
            if turn == 3:
                for copy in copies:
                    copy.wait()


def tokens_kernel(
    gated, starts, rank, gate, acts, *refs
):
    pieces, (part_own, part_other, whole, moved, spread, found) = refs[:8], refs[8:]
    expert = pl.program_id(0)
    count, blocks = rank.shape[0], rank.shape[1]
    base = expert * (blocks + 1)
    chip, core = starts[count * (blocks + 1)], starts[count * (blocks + 1) + 1]
    low = jnp.bfloat16

    @pl.when(expert == 0)
    def _():
        moved[...] = jnp.zeros_like(moved)

    assemble(chip, core, pieces, whole)

    def work(tile, carry):
        band = pl.ds(pl.multiple_of(tile * TILE, TILE), TILE)
        moved[expert, band, :] = dot_nt(acts[0, band, :], whole[...]).astype(low)
        return carry

    lax.fori_loop(0, (starts[base + blocks] + TILE - 1) // TILE, work, 0)

    @pl.when(expert == count - 1)
    def _():
        for side, part in enumerate((part_own, part_other)):

            def collect(place, carry):
                block = side * (blocks // 2) + place
                for each in range(count):
                    start = pl.multiple_of(starts[each * (blocks + 1) + block], 16)
                    hot = one_hot(rank[each, pl.ds(block, 1), :])
                    rows = moved[each, pl.ds(start, SPAN), :]
                    if gated:
                        weight = gate_of(hot, gate[each, pl.ds(block, 1), :])
                        rows = (rows.astype(jnp.float32) * weight).astype(low)
                    band = pl.ds(each * SPAN, SPAN)
                    spread[band, :] = jnp.where(hot, 1.0, 0.0).astype(low)
                    found[band, :] = rows
                part[place] = dot_tn(spread[...], found[...]).astype(low)
                return carry

            lax.fori_loop(0, blocks // 2, collect, 0)


def pass_shapes(rank, pieces):
    count = pieces[0].shape[0]
    blocks, padded = rank.shape[1], rank.shape[2]
    tiles = -(-blocks * SPAN // TILE)

    def of_expert(expert, starts):
        return (expert, 0, 0)

    piece_specs = [
        pl.BlockSpec(
            (1,) + pieces[0].shape[1:],
            lambda expert, starts, turn=place // 2: (jnp.bitwise_xor(expert, turn), 0, 0),
        )
        for place in range(8)
    ]
    return count, blocks, padded, tiles, of_expert, piece_specs


def experts_pass(starts, rank, gate, rows, cots, ups, downs):
    count, blocks, padded, tiles, of_expert, piece_specs = pass_shapes(rank, ups)
    features = rows[0].shape[1]
    width = ups[0].shape[2]
    most = blocks * SPAN
    low = jnp.bfloat16
    vectors = pl.BlockSpec((1, blocks, padded), of_expert)
    acts = pl.BlockSpec((1, tiles * TILE, width), of_expert)
    acts_shape = jax.ShapeDtypeStruct((count, tiles * TILE, width), low)
    grad_shape = jax.ShapeDtypeStruct((features, width), low)
    pair_shape = jax.ShapeDtypeStruct((2, features, width), low)
    return pl.pallas_call(
        experts_kernel,
        grid_spec=pltpu.PrefetchScalarGridSpec(
            num_scalar_prefetch=1,
            grid=(count,),
            in_specs=[vectors, vectors]
            + piece_specs * 2
            + [pl.BlockSpec(memory_space=pl.ANY)] * (2 * blocks),
            out_specs=[acts, acts] + [pl.BlockSpec(memory_space=pl.ANY)] * 5,
            scratch_shapes=[
                pltpu.VMEM((blocks, padded, features), low),
                pltpu.VMEM((blocks, padded, features), low),
                pltpu.VMEM((features, width), low),
                pltpu.VMEM((features, width), low),
                pltpu.VMEM((most + TILE, features), low),
                pltpu.VMEM((most + TILE, features), low),
                pltpu.VMEM((features, width), jnp.float32),
                pltpu.VMEM((features, width), jnp.float32),
                pltpu.VMEM((2, features, width), low),
                pltpu.SemaphoreType.DMA((2 * blocks,)),
                pltpu.SemaphoreType.DMA((8,)),
            ],
        ),
        out_shape=[acts_shape, acts_shape] + [pair_shape] * 3 + [grad_shape] * 2,
        compiler_params=pltpu.CompilerParams(vmem_limit_bytes=VMEM_ASK),
        cost_estimate=pl.CostEstimate(
            flops=4 * count * most * features * width,
            bytes_accessed=60 * 1024 * 1024,
            transcendentals=count * most * width,
        ),
        name="experts_pass",
    )(starts, rank, gate, *ups, *downs, *rows, *cots)


def tokens_pass(starts, rank, gate, acts, pieces, gated):
    count, blocks, padded, tiles, of_expert, piece_specs = pass_shapes(rank, pieces)
    width = pieces[0].shape[2]
    features = 8 * pieces[0].shape[1]
    most = blocks * SPAN
    low = jnp.bfloat16
    vectors = pl.BlockSpec(rank.shape, lambda expert, starts: (0, 0, 0))
    parts = pl.BlockSpec((blocks // 2, padded, features), lambda expert, starts: (0, 0, 0))
    part_shape = jax.ShapeDtypeStruct((blocks // 2, padded, features), low)
    return pl.pallas_call(
        functools.partial(tokens_kernel, gated),
        grid_spec=pltpu.PrefetchScalarGridSpec(
            num_scalar_prefetch=1,
            grid=(count,),
            in_specs=[vectors, vectors, pl.BlockSpec((1, tiles * TILE, width), of_expert)]
            + piece_specs,
            out_specs=[parts, parts],
            scratch_shapes=[
                pltpu.VMEM((features, width), low),
                pltpu.VMEM((count, most + TILE, features), low),
                pltpu.VMEM((count * SPAN, padded), low),
                pltpu.VMEM((count * SPAN, features), low),
            ],
        ),
        out_shape=[part_shape, part_shape],
        compiler_params=pltpu.CompilerParams(vmem_limit_bytes=VMEM_ASK),
        cost_estimate=pl.CostEstimate(
            flops=2 * count * most * features * width,
            bytes_accessed=30 * 1024 * 1024,
            transcendentals=0,
        ),
        name="tokens_gated" if gated else "tokens_plain",
    )(starts, rank, gate, acts, *pieces)


IMAGE = 208


def row_norm(values, factor, offset):
    width = values.shape[1]
    average = jnp.sum(values, axis=1, keepdims=True) / width
    centred = values - average
    spread = jnp.sum(centred * centred, axis=1, keepdims=True) / width
    inverse = lax.rsqrt(spread + norm_epsilon)
    unit = centred * inverse
    return unit * factor + offset, unit, inverse


def row_norm_back(gradient, unit, inverse, factor):
    width = gradient.shape[1]
    inner = gradient * factor
    average = jnp.sum(inner, axis=1, keepdims=True) / width
    along = jnp.sum(inner * unit, axis=1, keepdims=True) / width
    return inverse * (inner - average - unit * along)


def head_soft(query, key, here, keys_used):
    own = jnp.where(here, query, jnp.zeros_like(query))
    scores = dot_nt(own, key) * (HEAD_DIM ** (-0.5))
    scores = jnp.where(keys_used, scores, -1e30)
    powers = jnp.exp(scores - jnp.max(scores, axis=1, keepdims=True))
    return powers / jnp.sum(powers, axis=1, keepdims=True)


def forward_kernel(
    place, tokens, norms, w0, w1, w2, w3, others_near, others_far,
    normed_out, qkv_out, blended_out, residual_out, second_out, weights,
):
    features = tokens.shape[2]
    low = jnp.bfloat16

    @pl.when(pl.program_id(0) == 0)
    def _():
        chip, core = place[0], place[1]
        depth = features // 8
        others = (others_near.at[0], others_near.at[1], others_far.at[0], others_far.at[1])
        for side, pieces in enumerate(((w0, w1, w2, w3), others)):
            for turn, piece in enumerate(pieces):
                other = jnp.bitwise_xor(chip, turn)
                row = ((other // 2) * 2 + jnp.bitwise_xor(core, side)) * 2 + other % 2
                rows = pl.ds(pl.multiple_of(row * depth, 16), depth)
                for which in range(4):
                    weights[which, rows, :] = piece[which]

    normed, unused, unused = row_norm(
        tokens[0].astype(jnp.float32), norms[0:1, :], norms[2:3, :]
    )
    normed_out[0] = normed.astype(low)
    for which in range(3):
        qkv_out[0, which] = dot_nn(normed_out[0], weights[which]).astype(low)
    keys_used = lax.broadcasted_iota(jnp.int32, (IMAGE, IMAGE), 1) < LEN
    first = lax.broadcasted_iota(jnp.int32, (IMAGE, 2 * HEAD_DIM), 1) < HEAD_DIM
    for start in range(0, features, 2 * HEAD_DIM):
        cols = pl.ds(start, 2 * HEAD_DIM)
        query, key, value = (qkv_out[0, which, :, cols] for which in range(3))
        mixed = []
        for here in (first, jnp.logical_not(first)):
            soft = head_soft(query, key, here, keys_used).astype(low)
            mixed.append(dot_nn(soft, value))
        blended_out[0, :, cols] = jnp.where(first, mixed[0], mixed[1]).astype(low)
    residual = tokens[0].astype(jnp.float32) + dot_nn(blended_out[0], weights[3])
    residual_out[0] = residual
    second, unused, unused = row_norm(residual, norms[1:2, :], norms[3:4, :])
    second_out[0] = second.astype(low)


def attention_forward(place, tokens, norms, pieces, others):
    images, rows, features = tokens.shape
    low = jnp.bfloat16
    image = pl.BlockSpec((1, rows, features), lambda i, place: (i, 0, 0))
    shape = jax.ShapeDtypeStruct((images, rows, features), low)
    return pl.pallas_call(
        forward_kernel,
        grid_spec=pltpu.PrefetchScalarGridSpec(
            num_scalar_prefetch=1,
            grid=(images,),
            in_specs=[image, pl.BlockSpec(norms.shape, lambda i, place: (0, 0))]
            + [pl.BlockSpec(pieces[0].shape, lambda i, place: (0, 0, 0))] * 4
            + [pl.BlockSpec(others[0].shape, lambda i, place: (0, 0, 0, 0))] * 2,
            out_specs=[
                image,
                pl.BlockSpec((1, 3, rows, features), lambda i, place: (i, 0, 0, 0)),
                image,
                image,
                image,
                pl.BlockSpec((4, features, features), lambda i, place: (0, 0, 0)),
            ],
        ),
        out_shape=[
            shape,
            jax.ShapeDtypeStruct((images, 3, rows, features), low),
            shape,
            jax.ShapeDtypeStruct((images, rows, features), jnp.float32),
            shape,
            jax.ShapeDtypeStruct((4, features, features), low),
        ],
        compiler_params=pltpu.CompilerParams(vmem_limit_bytes=VMEM_ASK),
        cost_estimate=pl.CostEstimate(
            flops=10 * images * rows * features * features,
            bytes_accessed=16 * 1024 * 1024,
            transcendentals=0,
        ),
        name="attention_forward",
    )(place, tokens, norms, *pieces, *others)


def backward_kernel(
    place, tokens, cots, residual, blended, normed, qkv, weights, norms,
    second0, second1, second2, second3,
    input_grad, mine, theirs, vectors,
    parts, d_heads, d_qkv, d_sum,
):
    image = pl.program_id(0)
    features = tokens.shape[2]
    low = jnp.bfloat16
    core = place[1]
    seconds = (second0, second1, second2, second3)
    last = image == pl.num_programs(0) - 1

    @pl.when(image == 0)
    def _():
        vectors[...] = jnp.zeros_like(vectors)

    d_second = seconds[0][0].astype(jnp.float32)
    for piece in seconds[1:]:
        d_second = d_second + piece[0].astype(jnp.float32)
    unused, unit, inverse = row_norm(residual[0], norms[1:2, :], norms[3:4, :])
    vectors[1:2, :] += jnp.sum(d_second * unit, axis=0, keepdims=True)
    vectors[3:4, :] += jnp.sum(d_second, axis=0, keepdims=True)
    d_sum[...] = cots[0].astype(jnp.float32) + row_norm_back(
        d_second, unit, inverse, norms[1:2, :]
    )
    d_attended = d_sum[...].astype(low)
    d_heads[...] = dot_nt(d_attended, weights[3]).astype(low)
    out_part = dot_tn(blended[0], d_attended)

    @pl.when(image == 0)
    def _():
        parts[3] = out_part

    @pl.when(image > 0)
    def _():
        parts[3] = parts[3] + out_part

    keys_used = lax.broadcasted_iota(jnp.int32, (IMAGE, IMAGE), 1) < LEN
    first = lax.broadcasted_iota(jnp.int32, (IMAGE, 2 * HEAD_DIM), 1) < HEAD_DIM
    scale = HEAD_DIM ** (-0.5)
    for start in range(0, features, 2 * HEAD_DIM):
        cols = pl.ds(start, 2 * HEAD_DIM)
        query, key, value = (qkv[0, which, :, cols] for which in range(3))
        upper = d_heads[:, cols]
        found = []
        for here in (first, jnp.logical_not(first)):
            soft = head_soft(query, key, here, keys_used)
            d_soft = dot_nt(jnp.where(here, upper, jnp.zeros_like(upper)), value)
            inner = jnp.sum(soft * d_soft, axis=1, keepdims=True)
            d_scores = (soft * (d_soft - inner)).astype(low)
            found.append(
                (
                    dot_nn(d_scores, key) * scale,
                    dot_tn(d_scores, query) * scale,
                    dot_tn(soft.astype(low), upper),
                )
            )
        for which in range(3):
            d_qkv[which, :, cols] = jnp.where(first, found[0][which], found[1][which]).astype(low)
    d_normed = dot_nt(d_qkv[0], weights[0])
    for which in range(1, 3):
        d_normed = d_normed + dot_nt(d_qkv[which], weights[which])
    for which in range(3):
        in_part = dot_tn(normed[0], d_qkv[which])

        @pl.when(image == 0)
        def _():
            parts[which] = in_part

        @pl.when(image > 0)
        def _():
            parts[which] = parts[which] + in_part

    unused, unit, inverse = row_norm(
        tokens[0].astype(jnp.float32), norms[0:1, :], norms[2:3, :]
    )
    vectors[0:1, :] += jnp.sum(d_normed * unit, axis=0, keepdims=True)
    vectors[2:3, :] += jnp.sum(d_normed, axis=0, keepdims=True)
    input_grad[0] = d_sum[...] + row_norm_back(d_normed, unit, inverse, norms[0:1, :])

    @pl.when(last)
    def _():
        slab = mine.shape[2]
        for which in range(4):
            for side in range(2):
                own = pl.ds(pl.multiple_of((2 * side + core) * slab, slab), slab)
                other = pl.ds(pl.multiple_of((2 * side + 1 - core) * slab, slab), slab)
                mine[which, side] = parts[which, own, :].astype(low)
                theirs[which, side] = parts[which, other, :].astype(low)


def attention_backward(place, tokens, cots, residual, blended, normed, qkv, seconds, weights, norms):
    images, rows, features = tokens.shape
    low = jnp.bfloat16
    image = pl.BlockSpec((1, rows, features), lambda i, place: (i, 0, 0))
    half_shape = jax.ShapeDtypeStruct((4, 2, features // 4, features), low)
    half = pl.BlockSpec(half_shape.shape, lambda i, place: (0, 0, 0, 0))
    return pl.pallas_call(
        backward_kernel,
        grid_spec=pltpu.PrefetchScalarGridSpec(
            num_scalar_prefetch=1,
            grid=(images,),
            in_specs=[
                image,
                image,
                image,
                image,
                image,
                pl.BlockSpec((1, 3, rows, features), lambda i, place: (i, 0, 0, 0)),
                pl.BlockSpec(weights.shape, lambda i, place: (0, 0, 0)),
                pl.BlockSpec(norms.shape, lambda i, place: (0, 0)),
            ]
            + [image] * 4,
            out_specs=[
                image,
                half,
                half,
                pl.BlockSpec((8, features), lambda i, place: (0, 0)),
            ],
            scratch_shapes=[
                pltpu.VMEM((4, features, features), jnp.float32),
                pltpu.VMEM((rows, features), low),
                pltpu.VMEM((3, rows, features), low),
                pltpu.VMEM((rows, features), jnp.float32),
            ],
        ),
        out_shape=[
            jax.ShapeDtypeStruct((images, rows, features), jnp.float32),
            half_shape,
            half_shape,
            jax.ShapeDtypeStruct((8, features), jnp.float32),
        ],
        compiler_params=pltpu.CompilerParams(vmem_limit_bytes=VMEM_ASK),
        cost_estimate=pl.CostEstimate(
            flops=40 * images * rows * features * features,
            bytes_accessed=24 * 1024 * 1024,
            transcendentals=0,
        ),
        name="attention_backward",
    )(place, tokens, cots, residual, blended, normed, qkv, weights, norms, *seconds)


def route_to(place):
    shards, ctxs, tps = (lax.axis_size(name) for name in axes)
    pairs = []
    for shard in range(shards):
        for ctx in range(ctxs):
            for tp in range(tps):
                other_shard, other_ctx, other_tp = place(shard, ctx, tp)
                pairs.append(
                    (
                        (shard * ctxs + ctx) * tps + tp,
                        (other_shard * ctxs + other_ctx) * tps + other_tp % tps,
                    )
                )
    return pairs


def swap_core(value):
    return lax.ppermute(value, axes, route_to(lambda s, c, t: (s ^ 1, c, t)))


def swap_chip(value, turn):
    return lax.ppermute(
        value, axes, route_to(lambda s, c, t: (s ^ (turn & 2), c ^ (turn & 1), t))
    )


def swap_tp(value, turn):
    return lax.ppermute(value, axes, route_to(lambda s, c, t: (s, c, t ^ turn)))


def pass_on(value):
    return lax.ppermute(value, axes, route_to(lambda s, c, t: (s, c, t + 1)))


def worker_route(source, target):
    shards, ctxs, tps = (lax.axis_size(name) for name in axes)
    pairs = []
    for shard in range(shards):
        for ctx in range(ctxs):
            for worker in range(tps):
                if worker // 2 == shard % 2:
                    base = (shard * ctxs + ctx) * tps
                    pairs.append((base + source(worker) % tps, base + target(worker) % tps))
    return pairs


def to_worker(value, turn):
    return lax.ppermute(value, axes, worker_route(lambda w: w + turn, lambda w: w))


def from_worker(value, turn):
    step = 1 if turn > 0 else -1
    return lax.ppermute(
        value, axes, worker_route(lambda w: w + turn - step, lambda w: w + turn)
    )


def pick(value, index, axis=0):
    return lax.dynamic_index_in_dim(value, index, axis, keepdims=False)


def relative(value, chip):
    return [pick(value, jnp.bitwise_xor(chip, turn)) for turn in range(4)]


def pass_by(value, steps):
    return lax.ppermute(value, axes, route_to(lambda s, c, t: (s, c, t + steps)))


def direct_gather(value):
    return [value] + [pass_by(value, steps) for steps in range(1, lax.axis_size("tp"))]


class Live:
    def __init__(self, values=None):
        vars(self).update(values or {})

    @property
    def drop(self):
        return Drop(vars(self))


class Drop:
    def __init__(self, values):
        self._values = values

    def __getattr__(self, name):
        return self._values.pop(name)


def hold(live):
    return Live(lax.optimization_barrier(vars(live)))


def by_tp(held, tp):
    count = len(held)
    stacked = jnp.stack(held)
    return jnp.stack([pick(stacked, (tp - place) % count) for place in range(count)])


def place_chips(pieces, chip):
    stacked = jnp.stack(pieces)
    return jnp.stack([pick(stacked, jnp.bitwise_xor(chip, place)) for place in range(4)])


def place_cores(own, other, core):
    return jnp.where(core == 0, jnp.stack([own, other]), jnp.stack([other, own]))


def low_dot(spec, left, right):
    return jnp.einsum(
        spec,
        left.astype(jnp.bfloat16),
        right.astype(jnp.bfloat16),
        preferred_element_type=jnp.float32,
    )


def plane_device(
    tokens,
    cotangent,
    routing,
    gating,
    inward,
    outward,
    scales,
    shifts,
    upward,
    downward,
    inward_moment,
    outward_moment,
    scales_moment,
    shifts_moment,
    upward_moment,
    downward_moment,
):
    rows_here = tokens.shape[1]
    features = tokens.shape[2]
    seqs = rows_here // LEN
    experts = upward.shape[0]
    half_experts = experts // 2
    shard = lax.axis_index("shard")
    core = shard % 2
    ctx = lax.axis_index("ctx")
    tp = lax.axis_index("tp")
    tps = lax.axis_size("tp")
    devices = lax.axis_size(axes)
    chip = (shard // 2) * 2 + ctx
    low = jnp.bfloat16
    rows_attn = inward.shape[1]
    rows_local = upward.shape[1]
    cols_local = upward.shape[2]

    v = Live()
    place = jnp.stack([chip, core, tp]).astype(jnp.int32)
    y_here, x_here = shard // 2, ctx
    padded = seqs * IMAGE
    half = tps // 2
    own_tokens, own_cot = (
        jnp.pad(value[0].reshape(seqs, LEN, features), ((0, 0), (0, IMAGE - LEN), (0, 0)))
        for value in (tokens, cotangent)
    )

    def halves(value):
        value = value.astype(low).reshape(2, half_experts, rows_local, cols_local)
        return pick(value, core), pick(value, 1 - core)

    def own_order(value):
        return jnp.stack([pick(value, jnp.bitwise_xor(chip, r)) for r in range(4)])

    up_kept, up_sent = halves(upward)
    down_kept, down_sent = halves(downward)
    v.up, v.down = [own_order(up_kept)], [own_order(down_kept)]
    v.up_x, v.down_y = [swap_chip(v.up[0], 1)], [swap_chip(v.down[0], 2)]
    v.column = direct_gather(jnp.concatenate([inward, outward[None]]))
    v.sent = jnp.stack([up_sent, down_sent])
    v.cots = [own_cot.reshape(padded, features)]

    packed = jnp.concatenate([routing[0].astype(jnp.float32).T, gating[0].T])
    packed = jnp.pad(
        packed.reshape(4, seqs, LEN), ((0, 0), (0, 0), (0, IMAGE - LEN)), constant_values=-1.0
    )
    norm_rows = jnp.concatenate([scales, shifts]).astype(jnp.float32)
    packed = jnp.concatenate(
        [packed.reshape(4, padded), jnp.pad(norm_rows, ((0, 0), (0, padded - rows_attn)))]
    )
    v.packs = direct_gather(packed)
    v = hold(v)

    column = by_tp(v.drop.column, tp).transpose(1, 0, 2, 3)
    column = column.reshape(4, tps * rows_attn, features)
    v.pieces = [column, swap_chip(column, 1), swap_chip(column, 2)]
    v.cots.append(pass_on(v.cots[-1]))
    v.got = swap_core(v.drop.sent)
    packs = jnp.stack(v.packs)
    v.packs = [packs, swap_core(packs)]
    v = hold(v)

    column, from_x, from_y = v.pieces
    v.far = [swap_chip(from_x[:2], 2), swap_chip(from_y[2:], 1)]
    v.others = [swap_core(jnp.stack(v.pieces[:2]))]
    got = v.drop.got
    v.up.append(own_order(got[0]))
    v.down.append(own_order(got[1]))
    own_packs, other_packs = v.drop.packs
    norms = [by_tp(list(each[:, 4:, :rows_attn]), tp) for each in (own_packs, other_packs)]
    norms = place_cores(*norms, core)
    v.norms = [norms, swap_chip(norms, 1)]
    packs = jnp.concatenate([own_packs, other_packs])
    mine = core * half_experts + jnp.bitwise_xor(chip, jnp.arange(4, dtype=jnp.int32))
    hits = packs[None, :, :2] == mine.astype(jnp.float32)[:, None, None, None]
    chosen = jnp.any(hits, axis=2)
    gate_tok = jnp.sum(jnp.where(hits, packs[None, :, 2:4], 0.0), axis=2)
    places = jnp.arange(padded)
    earlier = (places[:, None] < places[None, :]).astype(low)
    rank = jnp.einsum(
        "rbt,tu->rbu", chosen.astype(low), earlier, preferred_element_type=jnp.float32
    )
    rank = jnp.where(chosen, rank, -1.0).astype(jnp.int32)
    counts = jnp.sum(chosen.astype(jnp.int32), axis=2)
    counts = (counts + 15) // 16 * 16
    starts = jnp.cumsum(jnp.pad(counts, ((0, 0), (1, 0))), axis=1).astype(jnp.int32).reshape(-1)
    v.routes = (jnp.concatenate([starts, place[:2]]), rank, gate_tok)
    v = hold(v)
    far = jnp.concatenate(v.drop.far)
    v.pieces = v.pieces + [far]
    v.others.append(swap_core(jnp.stack(v.pieces[2:])))
    v.cots.append(pass_on(v.cots[-1]))
    v.up_x.append(swap_chip(v.up[1], 1))
    v.down_y.append(swap_chip(v.down[1], 2))
    norms = place_cores(*v.norms, ctx)
    v.norms = [norms, swap_chip(norms, 2)]
    v = hold(v)
    norms = place_cores(*v.drop.norms, y_here)
    norms = norms.transpose(4, 0, 2, 1, 3, 5).reshape(4, features)

    normed, qkv, blended, residual, second, full_weights = attention_forward(
        place, own_tokens, norms, v.drop.pieces, v.drop.others
    )
    v.seconds = [second.reshape(padded, features)]
    v.up_xy, v.down_xy = [swap_chip(v.up_x[0], 2)], [swap_chip(v.down_y[0], 1)]
    v.cots.append(pass_on(v.cots[-1]))
    v.cots_other = [swap_core(each) for each in v.cots[:2]]
    v = hold(v)

    v.seconds.append(pass_on(v.seconds[-1]))
    v.up_xy.append(swap_chip(v.up_x[1], 2))
    v.down_xy.append(swap_chip(v.down_y[1], 1))
    v.cots_other += [swap_core(each) for each in v.cots[2:]]
    v = hold(v)
    v.seconds.append(pass_on(v.seconds[-1]))
    v.down_x, v.up_y = [swap_chip(v.down[0], 1)], [swap_chip(v.up[0], 2)]
    v.seconds_other = [swap_core(v.seconds[0])]
    moments = halves(upward_moment) + halves(downward_moment)
    v.moments = moments[0], moments[2], swap_core(jnp.stack([moments[1], moments[3]]))
    v = hold(v)
    v.seconds.append(pass_on(v.seconds[-1]))
    v.down_x.append(swap_chip(v.down[1], 1))
    v.up_y.append(swap_chip(v.up[1], 2))
    v.seconds_other += [swap_core(each) for each in v.seconds[1:3]]
    moments = v.drop.moments
    moments = jnp.stack([moments[0], moments[2][0], moments[1], moments[2][1]])
    v.moments = [pick(moments, jnp.bitwise_xor(chip, turn), 1) for turn in range(4)]
    v = hold(v)
    v.seconds_other.append(swap_core(v.seconds[3]))
    v = hold(v)

    ups = v.drop.up + v.drop.up_x + v.drop.up_y + v.drop.up_xy
    downs = v.drop.down + v.drop.down_x + v.drop.down_y + v.drop.down_xy
    v.moments = [v.moments[0]] + [swap_chip(v.moments[turn], turn) for turn in range(1, 4)]
    hidden, before, v.own, v.near_x, v.near_y, v.far_x, v.far_y = experts_pass(
        *v.routes,
        v.drop.seconds + v.drop.seconds_other,
        v.drop.cots + v.drop.cots_other,
        ups, downs,
    )
    v.hidden, v.before = hidden, before
    v.ups, v.downs = ups, downs
    v = hold(v)

    v.part = tokens_pass(*v.routes, v.drop.before, v.drop.ups, False)
    v.far_x, v.far_y = swap_chip(v.far_x, 1), swap_chip(v.far_y, 2)
    v = hold(v)

    def join(own, other):
        return (own.astype(jnp.float32) + other.astype(jnp.float32)).astype(low)

    v.along_x = v.near_x.at[1].set(join(v.near_x[1], v.drop.far_y))
    v.along_y = v.near_y.at[0].set(join(v.near_y[0], v.drop.far_x))
    v.near_x = v.near_y = None
    v.part = [v.part[0], swap_core(v.part[1])]
    v = hold(v)
    kept = join(*v.drop.part)
    v.along_x, v.along_y = swap_chip(v.along_x, 1), swap_chip(v.along_y, 2)
    v.seconds = [kept[0]] + [pass_by(kept[turn], -turn) for turn in range(1, tps)]
    v.mixed = tokens_pass(*v.drop.routes, v.drop.hidden, v.drop.downs, True)
    v = hold(v)

    *pushes, rows0, rows1, rows2, rows3 = push_rows(
        place, v.drop.own, (v.drop.along_x, v.drop.along_y), v.drop.moments
    )
    v.push, v.rows = pushes, [rows0, rows1, rows2, rows3]
    v = hold(v)

    def rows_out(rows):
        return [rows[0]] + [swap_chip(rows[turn], turn) for turn in range(1, 4)]

    def rows_between(got):
        got = place_chips(got, chip)
        return pick(got, core, 2), swap_core(pick(got, 1 - core, 2))

    def rows_in(kept, got):
        joined = place_cores(kept, got, core).transpose(2, 0, 1, 3, 4)
        joined = joined.reshape(2, experts, rows_local, cols_local)
        return joined.astype(jnp.float32)

    v.joined = [v.push[0]] + [to_worker(v.push[1], turn) for turn in (1, 3)]
    v.block = v.push[0]
    v.rows = rows_out(v.rows)
    v.input_grad, v.own, v.gone, v.vectors = attention_backward(
        place, own_tokens, own_cot, residual, blended, normed, qkv,
        [each.reshape(seqs, IMAGE, features) for each in v.drop.seconds],
        full_weights, norms,
    )
    v = hold(v)

    def added(value, got):
        return value.astype(jnp.float32) + got.astype(jnp.float32)

    third = features // 3
    v.gone = swap_core(v.gone)
    v.blocks = [to_worker(v.block[:third], 2)]
    v.rows = rows_between(v.rows)
    v = hold(v)
    sums = added(v.drop.own, v.drop.gone).reshape(4, 2, 2, tps, rows_attn, features)
    first, last = sums[:, :, :, :half], sums[:, :, :, half:]
    v.first = [pick(first, x_here, 2), swap_chip(pick(first, 1 - x_here, 2).astype(low), 1)]
    v.last = [pick(last, y_here, 1), swap_chip(pick(last, 1 - y_here, 1).astype(low), 2)]
    v.blocks.append(to_worker(v.block[third : 2 * third], 2))
    v = hold(v)
    first, last = added(*v.first), added(*v.last)
    v.first = [pick(first, y_here, 1), swap_chip(pick(first, 1 - y_here, 1).astype(low), 2)]
    v.last = [pick(last, x_here, 1), swap_chip(pick(last, 1 - x_here, 1).astype(low), 1)]
    v.blocks.append(to_worker(v.drop.block[2 * third :], 2))
    v.mixed = [v.mixed[0], swap_core(v.mixed[1])]
    v = hold(v)

    sums = jnp.concatenate([added(*v.drop.first), added(*v.drop.last)], axis=1)
    parts = [pick(sums, (tp - turn) % tps, 1) for turn in range(tps)]
    v.sums = [parts[0]] + [
        pass_by(parts[turn].astype(low), -turn) for turn in range(1, tps)
    ]
    mixed = added(*v.mixed)
    v.mixed = [mixed, pass_on(mixed[1].astype(low))]
    v.mixers = wide_first(v.drop.joined + v.drop.blocks)
    vectors = v.vectors[:4]
    v.vectors = [vectors, swap_core(vectors)]
    v = hold(v)
    sums = sum(part.astype(jnp.float32) for part in v.drop.sums)
    inward_grad, outward_grad = sums[:3], sums[3]
    inward_state, inward_push = advance(inward_grad, inward_moment)
    outward_state, outward_push = advance(outward_grad, outward_moment)
    v.column = direct_gather(jnp.concatenate([inward_push, outward_push[None]]).astype(low))
    v.mixers = [wide_last(*v.mixers)]
    mixed, got = v.mixed
    v.mixed = [mixed, pass_on(added(mixed[2], got).astype(low))]
    vectors = sum(v.vectors)
    v.vectors = [vectors, swap_chip(vectors, 1)]
    v = hold(v)
    column = by_tp(v.drop.column, tp).transpose(1, 0, 2, 3)
    gone = relative(column, chip)
    v.pushes = [gone[0]] + [swap_chip(gone[turn], turn) for turn in range(1, 4)]
    v.mixers.append(from_worker(v.mixers[0], 1))
    v.mixers.append(from_worker(v.mixers[0], -1))
    v = hold(v)
    pushes = place_chips(v.pushes, chip)
    v.pushes = [pushes, swap_core(pushes)]
    v.mixers.insert(2, from_worker(v.mixers[1], 2))
    vectors = sum(v.vectors)
    v.vectors = [vectors, swap_chip(vectors, 2)]
    v.input_grad = v.input_grad[:, :LEN].reshape(rows_here, features)
    upward_grad, downward_grad = rows_in(*v.drop.rows)
    v.states = [
        (upward_grad, advance(upward_grad, upward_moment)[0]),
        (downward_grad, advance(downward_grad, downward_moment)[0]),
    ]
    v = hold(v)
    pushes = place_cores(*v.drop.pushes, core)
    pushes = pushes.reshape(2, 2, 2, tps, rows_attn, features).transpose(1, 0, 2, 3, 4, 5)
    v.pushes = pushes.reshape(features, features)
    vectors = sum(v.vectors)
    v.vectors = [vectors, swap_tp(vectors, 1)]
    v.new = apply_mixers(place, v.drop.mixers, v.drop.push, rows_local)
    v = hold(v)

    v.new = rows_out(v.new)
    mixed, got = v.mixed
    v.mixed = [mixed, pass_on(added(mixed[3], got).astype(low))]
    vectors = sum(v.vectors)
    v.vectors = [vectors, swap_tp(vectors, 2)]
    v.moved = orthogonal_square(v.drop.pushes)
    v = hold(v)
    moved = v.drop.moved.reshape(2, 2, 2, tps, rows_attn, features)
    moved = pick(pick(moved, core, 1), tp, 2).reshape(4, rows_attn, features)
    gone = relative(moved, chip)
    v.moved = [gone[0]] + [swap_chip(gone[turn], turn) for turn in range(1, 4)]
    v.new = rows_between(v.new)
    mixed, got = v.drop.mixed
    result = (residual.reshape(padded, features) + added(mixed[0], got)).astype(low)
    v.result = result.reshape(seqs, IMAGE, features)[:, :LEN].reshape(rows_here, features)
    vectors = lax.dynamic_slice(
        sum(v.drop.vectors), (0, lax.axis_index(axes) * rows_attn), (4, rows_attn)
    )
    v = hold(v)
    result, input_grad = v.result, v.input_grad
    scales_grad, shifts_grad = vectors[:2], vectors[2:]
    scales_state, scales_push = advance(scales_grad, scales_moment)
    shifts_state, shifts_push = advance(shifts_grad, shifts_moment)
    up_new, down_new = rows_in(*v.new)
    upward_new = upward.astype(jnp.float32) - 2.0 * up_new
    downward_new = downward.astype(jnp.float32) - down_new
    (upward_grad, upward_state), (downward_grad, downward_state) = v.states
    got = place_chips(v.moved, chip).astype(jnp.float32)
    inward_new = inward.astype(jnp.float32) - got[:3]
    outward_new = outward.astype(jnp.float32) - got[3]
    vector_rate = 0.6 / math.sqrt(devices * rows_here)
    scales_new = scales.astype(jnp.float32) - vector_rate * scales_push
    shifts_new = shifts.astype(jnp.float32) - vector_rate * shifts_push
    return (
        result[None],
        input_grad[None],
        inward_grad,
        outward_grad,
        scales_grad,
        shifts_grad,
        upward_grad,
        downward_grad,
        inward_state,
        outward_state,
        scales_state,
        shifts_state,
        upward_state,
        downward_state,
        inward_new,
        outward_new,
        scales_new,
        shifts_new,
        upward_new,
        downward_new,
    )


def solution(mesh):
    in_specs = (
        P(("shard", "tp"), "ctx", None),
        P(("shard", "tp"), "ctx", None),
        P(("shard", "tp"), "ctx", None),
        P(("shard", "tp"), "ctx", None),
        P(None, ("shard", "ctx", "tp"), None),
        P(("shard", "ctx", "tp"), None),
        P(None, ("shard", "ctx", "tp")),
        P(None, ("shard", "ctx", "tp")),
        P(None, ("shard", "ctx"), "tp"),
        P(None, ("shard", "ctx"), "tp"),
        P(None, ("shard", "ctx", "tp"), None),
        P(("shard", "ctx", "tp"), None),
        P(None, ("shard", "ctx", "tp")),
        P(None, ("shard", "ctx", "tp")),
        P(None, ("shard", "ctx"), "tp"),
        P(None, ("shard", "ctx"), "tp"),
    )
    out_specs = (
        P(("shard", "tp"), "ctx", None),
        P(("shard", "tp"), "ctx", None),
        P(None, ("shard", "ctx", "tp"), None),
        P(("shard", "ctx", "tp"), None),
        P(None, ("shard", "ctx", "tp")),
        P(None, ("shard", "ctx", "tp")),
        P(None, ("shard", "ctx"), "tp"),
        P(None, ("shard", "ctx"), "tp"),
        P(None, ("shard", "ctx", "tp"), None),
        P(("shard", "ctx", "tp"), None),
        P(None, ("shard", "ctx", "tp")),
        P(None, ("shard", "ctx", "tp")),
        P(None, ("shard", "ctx"), "tp"),
        P(None, ("shard", "ctx"), "tp"),
        P(None, ("shard", "ctx", "tp"), None),
        P(("shard", "ctx", "tp"), None),
        P(None, ("shard", "ctx", "tp")),
        P(None, ("shard", "ctx", "tp")),
        P(None, ("shard", "ctx"), "tp"),
        P(None, ("shard", "ctx"), "tp"),
    )
    body = plane_device if mesh.shape["shard"] == 4 and mesh.shape["ctx"] == 2 and mesh.shape["tp"] == 4 else on_device
    return jax.shard_map(
        body, mesh=mesh, in_specs=in_specs, out_specs=out_specs, check_vma=False
    )
```

```python
import functools
import math

import jax
import jax.numpy as jnp
import numpy as np
from jax import lax
from jax.experimental import pallas as pl
from jax.experimental.pallas import tpu as pltpu
from jax.sharding import PartitionSpec as P

HEAD_DIM = 64
LEN = 197


first_coef = 3.4445
second_coef = -4.775
third_coef = 2.0315
momentum_decay = 0.9
norm_epsilon = 1e-06
orth_epsilon = 1e-07
highest = lax.Precision.HIGHEST


def normalize(values, factor, offset):
    average = jnp.mean(values, axis=-1, keepdims=True)
    centred = values - average
    inverse = lax.rsqrt(jnp.mean(centred * centred, axis=-1, keepdims=True) + norm_epsilon)
    unit_rows = centred * inverse
    return (unit_rows * factor + offset, unit_rows, inverse)


def normalize_back(gradient, unit_rows, inverse, factor):
    inner = gradient * factor
    average = jnp.mean(inner, axis=-1, keepdims=True)
    along = jnp.mean(inner * unit_rows, axis=-1, keepdims=True)
    back = inverse * (inner - average - unit_rows * along)
    return (back, jnp.sum(gradient * unit_rows, axis=0), jnp.sum(gradient, axis=0))


def slot_sources(routes, experts, capacity):
    pairs = routes.shape[0] * routes.shape[1]
    chosen = routes.reshape(pairs)
    onehot = (chosen[:, None] == jnp.arange(experts, dtype=jnp.int32)[None, :]).astype(jnp.int32)
    earlier = jnp.cumsum(onehot, axis=0) - onehot
    placed = jnp.sum(earlier * onehot, axis=1) + chosen * capacity
    matches = placed[None, :] == jnp.arange(experts * capacity, dtype=jnp.int32)[:, None]
    source = jnp.sum(jnp.where(matches, jnp.arange(pairs, dtype=jnp.int32)[None, :], 0), axis=1)
    filled = jnp.any(matches, axis=1)
    return (placed, source, filled)


def orthogonal(matrix):
    summed = jnp.sqrt(jnp.sum(matrix * matrix))
    current = matrix / (summed + orth_epsilon)
    for repeat in range(5):
        square = lax.dot_general(
            current,
            current,
            (((1,), (1,)), ((), ())),
            precision=highest,
            preferred_element_type=jnp.float32,
        )
        power = jnp.dot(square, square, precision=highest, preferred_element_type=jnp.float32)
        mixer = second_coef * square + third_coef * power
        current = first_coef * current + jnp.dot(
            mixer, current, precision=highest, preferred_element_type=jnp.float32
        )
    return current


def advance(gradient, moment):
    current = momentum_decay * moment + (1.0 - momentum_decay) * gradient
    return (current, (1.0 - momentum_decay) * gradient + momentum_decay * current)


def expert_weights(upward, downward):
    return (
        lax.all_gather(upward, ("shard", "ctx"), axis=1, tiled=True),
        lax.all_gather(downward, ("shard", "ctx"), axis=1, tiled=True),
    )


def on_device(
    tokens,
    cotangent,
    routing,
    gating,
    inward,
    outward,
    scales,
    shifts,
    upward,
    downward,
    inward_moment,
    outward_moment,
    scales_moment,
    shifts_moment,
    upward_moment,
    downward_moment,
):
    rows_here = tokens.shape[1]
    features = tokens.shape[2]
    experts = upward.shape[0]
    top_count = routing.shape[2]
    capacity = 2 * top_count * rows_here // experts
    attn_scale = HEAD_DIM ** (-0.5)
    inputs = tokens[0].astype(jnp.float32)
    routes = routing[0]
    gate_pairs = gating[0].reshape(-1)
    zero_low = jnp.zeros((), jnp.bfloat16)
    full_in, full_out, all_scales, all_shifts = (
        lax.all_gather(inward, ("shard", "ctx", "tp"), axis=1, tiled=True),
        lax.all_gather(outward, ("shard", "ctx", "tp"), axis=0, tiled=True),
        lax.all_gather(scales, ("shard", "ctx", "tp"), axis=1, tiled=True),
        lax.all_gather(shifts, ("shard", "ctx", "tp"), axis=1, tiled=True),
    )
    factor = all_scales.astype(jnp.float32)
    offset = all_shifts.astype(jnp.float32)
    normed, unit_one, inverse_one = normalize(inputs, factor[0], offset[0])
    normed_low = normed.astype(jnp.bfloat16)
    projected = jnp.einsum(
        "td,kde->kte", normed_low, full_in, preferred_element_type=jnp.float32
    ).astype(jnp.bfloat16)
    head_rows = lax.all_to_all(projected, "ctx", split_axis=2, concat_axis=1, tiled=True)
    group_rows = head_rows.shape[1]
    head_width = head_rows.shape[2]
    seqs_here = group_rows // LEN
    shaped = head_rows.reshape(3, seqs_here, LEN, head_width // HEAD_DIM, HEAD_DIM)
    query_rows, key_rows, value_rows = (shaped[0], shaped[1], shaped[2])
    scores = (
        jnp.einsum("sqhd,skhd->shqk", query_rows, key_rows, preferred_element_type=jnp.float32)
        * attn_scale
    )
    top_score = jnp.max(scores, axis=-1, keepdims=True)
    logsum = top_score + jnp.log(jnp.sum(jnp.exp(scores - top_score), axis=-1, keepdims=True))
    soft_low = jnp.exp(scores - logsum).astype(jnp.bfloat16)
    blended = jnp.einsum(
        "shqk,skhd->sqhd", soft_low, value_rows, preferred_element_type=jnp.float32
    ).astype(jnp.bfloat16)
    blended_tokens = lax.all_to_all(
        blended.reshape(group_rows, head_width), "ctx", split_axis=0, concat_axis=1, tiled=True
    )
    residual = inputs + jnp.dot(blended_tokens, full_out, preferred_element_type=jnp.float32)
    second, unit_two, inverse_two = normalize(residual, factor[1], offset[1])
    second_low = second.astype(jnp.bfloat16)
    upstream = cotangent[0].astype(jnp.float32)
    placed, source, filled = slot_sources(routes, experts, capacity)
    slot_rows = jnp.where(filled[:, None], second_low[source // top_count], zero_low)
    slot_rows = slot_rows.reshape(experts, capacity, features)
    group_slots = lax.all_gather(slot_rows, "tp", axis=1, tiled=True)
    upper_full, lower_full = expert_weights(upward, downward)
    before = jnp.einsum("ecd,edf->ecf", group_slots, upper_full, preferred_element_type=jnp.float32)
    hidden = jax.nn.gelu(before).astype(jnp.bfloat16)
    partial_out = jnp.einsum("ecf,edf->ecd", hidden, lower_full, preferred_element_type=jnp.float32)
    own_out = lax.psum_scatter(
        partial_out.astype(jnp.bfloat16), "tp", scatter_dimension=1, tiled=True
    ).astype(jnp.float32)
    picked = own_out.reshape(experts * capacity, features)[placed].reshape(
        rows_here, top_count, features
    )
    mixture = jnp.sum(picked * gating[0][:, :, None], axis=1)
    result = (residual + mixture).astype(jnp.bfloat16)
    slot_grad = jnp.where(
        filled[:, None], upstream[source // top_count] * gate_pairs[source][:, None], 0.0
    )
    slot_grad = slot_grad.astype(jnp.bfloat16).reshape(experts, capacity, features)
    group_grad = lax.all_gather(slot_grad, "tp", axis=1, tiled=True)
    upper_full, lower_full = expert_weights(upward, downward)
    d_hidden = jnp.einsum(
        "ecd,edf->ecf", group_grad, lower_full, preferred_element_type=jnp.float32
    )
    unused, gelu_back = jax.vjp(jax.nn.gelu, before)
    d_before = gelu_back(d_hidden)[0].astype(jnp.bfloat16)
    lower_part = jnp.einsum("ecd,ecf->edf", group_grad, hidden, preferred_element_type=jnp.float32)
    upper_part = jnp.einsum(
        "ecd,ecf->edf", group_slots, d_before, preferred_element_type=jnp.float32
    )
    slot_input_part = jnp.einsum(
        "ecf,edf->ecd", d_before, upper_full, preferred_element_type=jnp.float32
    )
    slot_input = lax.psum_scatter(
        slot_input_part.astype(jnp.bfloat16), "tp", scatter_dimension=1, tiled=True
    ).astype(jnp.float32)
    d_second = jnp.sum(
        slot_input.reshape(experts * capacity, features)[placed].reshape(
            rows_here, top_count, features
        ),
        axis=1,
    )
    d_norm_two, scale_two, shift_two = normalize_back(d_second, unit_two, inverse_two, factor[1])
    d_residual = upstream + d_norm_two
    d_attended = d_residual.astype(jnp.bfloat16)
    outward_part = jnp.einsum(
        "td,te->de", blended_tokens, d_attended, preferred_element_type=jnp.float32
    )
    d_blended = jnp.einsum(
        "te,de->td", d_attended, full_out, preferred_element_type=jnp.float32
    ).astype(jnp.bfloat16)
    d_heads = lax.all_to_all(d_blended, "ctx", split_axis=1, concat_axis=0, tiled=True)
    d_heads = d_heads.reshape(seqs_here, LEN, head_width // HEAD_DIM, HEAD_DIM)
    soft_full = jnp.exp(
        jnp.einsum("sqhd,skhd->shqk", query_rows, key_rows, preferred_element_type=jnp.float32)
        * attn_scale
        - logsum
    )
    d_soft = jnp.einsum("sqhd,skhd->shqk", d_heads, value_rows, preferred_element_type=jnp.float32)
    value_grad = jnp.einsum(
        "shqk,sqhd->skhd", soft_low, d_heads, preferred_element_type=jnp.float32
    ).astype(jnp.bfloat16)
    row_inner = jnp.sum(soft_full * d_soft, axis=-1, keepdims=True)
    d_scores = (soft_full * (d_soft - row_inner)).astype(jnp.bfloat16)
    query_grad = (
        jnp.einsum("shqk,skhd->sqhd", d_scores, key_rows, preferred_element_type=jnp.float32)
        * attn_scale
    ).astype(jnp.bfloat16)
    key_grad = (
        jnp.einsum("shqk,sqhd->skhd", d_scores, query_rows, preferred_element_type=jnp.float32)
        * attn_scale
    ).astype(jnp.bfloat16)
    stacked_grad = jnp.stack([query_grad, key_grad, value_grad]).reshape(3, group_rows, head_width)
    token_grad = lax.all_to_all(stacked_grad, "ctx", split_axis=1, concat_axis=2, tiled=True)
    inward_part = jnp.einsum(
        "td,kte->kde", normed_low, token_grad, preferred_element_type=jnp.float32
    )
    d_normed = jnp.einsum("kte,kde->td", token_grad, full_in, preferred_element_type=jnp.float32)
    d_norm_one, scale_one, shift_one = normalize_back(d_normed, unit_one, inverse_one, factor[0])
    input_grad = d_residual + d_norm_one
    inward_grad, outward_grad, scales_grad, shifts_grad = (
        lax.psum_scatter(inward_part, ("shard", "ctx", "tp"), scatter_dimension=1, tiled=True),
        lax.psum_scatter(outward_part, ("shard", "ctx", "tp"), scatter_dimension=0, tiled=True),
        lax.psum_scatter(
            jnp.stack([scale_one, scale_two]),
            ("shard", "ctx", "tp"),
            scatter_dimension=1,
            tiled=True,
        ),
        lax.psum_scatter(
            jnp.stack([shift_one, shift_two]),
            ("shard", "ctx", "tp"),
            scatter_dimension=1,
            tiled=True,
        ),
    )
    upward_grad, downward_grad = (
        lax.psum_scatter(
            upper_part.astype(jnp.bfloat16), ("shard", "ctx"), scatter_dimension=1, tiled=True
        ).astype(jnp.float32),
        lax.psum_scatter(
            lower_part.astype(jnp.bfloat16), ("shard", "ctx"), scatter_dimension=1, tiled=True
        ).astype(jnp.float32),
    )
    inward_state, inward_push = advance(inward_grad, inward_moment)
    outward_state, outward_push = advance(outward_grad, outward_moment)
    scales_state, scales_push = advance(scales_grad, scales_moment)
    shifts_state, shifts_push = advance(shifts_grad, shifts_moment)
    upward_state, upward_push = advance(upward_grad, upward_moment)
    downward_state, downward_push = advance(downward_grad, downward_moment)
    devices = lax.axis_size(("shard", "ctx", "tp"))
    outer_count = lax.axis_size(("shard", "ctx"))
    inner_count = lax.axis_size("tp")
    rows_local = upward.shape[1]
    cols_local = upward.shape[2]
    slot_size = rows_local * cols_local
    attention_size = inward.shape[1] * features
    full_cols = inner_count * cols_local

    def flat_pad(portion):
        flatten = portion.reshape(portion.shape[0], -1)
        return jnp.pad(flatten, ((0, 0), (0, slot_size - flatten.shape[1])))

    matrices = jnp.concatenate(
        [
            flat_pad(inward_push),
            flat_pad(outward_push[None]),
            upward_push.reshape(experts, slot_size),
            downward_push.reshape(experts, slot_size),
        ]
    )
    matrix_count = matrices.shape[0]
    owner_table = np.arange(matrix_count) * devices // matrix_count
    outgoing = jnp.zeros((devices, slot_size), jnp.float32).at[owner_table].set(matrices)
    received = lax.all_to_all(
        outgoing.astype(jnp.bfloat16),
        ("shard", "ctx", "tp"),
        split_axis=0,
        concat_axis=0,
        tiled=True,
    ).astype(outgoing.dtype)
    myself = lax.axis_index(("shard", "ctx", "tp"))
    owned = (
        jnp.sum(
            jnp.where(
                jnp.asarray(owner_table, dtype=jnp.int32) == myself,
                jnp.arange(matrix_count, dtype=jnp.int32) + 1,
                0,
            )
        )
        - 1
    )
    attention_kind = jnp.logical_and(owned >= 0, owned < 4)
    expert_form = (
        received.reshape(outer_count, inner_count, rows_local, cols_local)
        .transpose(0, 2, 1, 3)
        .reshape(features, full_cols)
    )
    attention_form = jnp.pad(
        received[:, :attention_size].reshape(features, features),
        ((0, 0), (0, full_cols - features)),
    )
    orthogonal_form = orthogonal(jnp.where(attention_kind, attention_form, expert_form))
    back_expert = (
        orthogonal_form.reshape(outer_count, rows_local, inner_count, cols_local)
        .transpose(0, 2, 1, 3)
        .reshape(devices, slot_size)
    )
    back_attention = jnp.pad(
        orthogonal_form[:, :features].reshape(devices, attention_size),
        ((0, 0), (0, slot_size - attention_size)),
    )
    returned = lax.all_to_all(
        jnp.where(attention_kind, back_attention, back_expert).astype(jnp.bfloat16),
        ("shard", "ctx", "tp"),
        split_axis=0,
        concat_axis=0,
        tiled=True,
    ).astype(jnp.float32)
    mine_parts = returned[owner_table]
    inward_new = inward.astype(jnp.float32) - mine_parts[:3, :attention_size].reshape(inward.shape)
    outward_new = outward.astype(jnp.float32) - mine_parts[3, :attention_size].reshape(
        outward.shape
    )
    upward_new = upward.astype(jnp.float32) - 2.0 * mine_parts[4 : 4 + experts].reshape(
        upward.shape
    )
    downward_new = downward.astype(jnp.float32) - mine_parts[4 + experts :].reshape(downward.shape)
    total_tokens = lax.axis_size("shard") * lax.axis_size("ctx") * lax.axis_size("tp") * rows_here
    vector_rate = 0.6 / math.sqrt(total_tokens)
    scales_new = scales.astype(jnp.float32) - vector_rate * scales_push
    shifts_new = shifts.astype(jnp.float32) - vector_rate * shifts_push
    return (
        result[None],
        input_grad[None],
        inward_grad,
        outward_grad,
        scales_grad,
        shifts_grad,
        upward_grad,
        downward_grad,
        inward_state,
        outward_state,
        scales_state,
        shifts_state,
        upward_state,
        downward_state,
        inward_new,
        outward_new,
        scales_new,
        shifts_new,
        upward_new,
        downward_new,
    )


axes = ("shard", "ctx", "tp")
TILE = 256
SPAN = 208
VMEM_ASK = 60 * 1024 * 1024


def dot_nn(left, right):
    return lax.dot_general(
        left, right, (((1,), (0,)), ((), ())), preferred_element_type=jnp.float32
    )


def dot_nt(left, right):
    return lax.dot_general(
        left, right, (((1,), (1,)), ((), ())), preferred_element_type=jnp.float32
    )


def dot_tn(left, right):
    return lax.dot_general(
        left, right, (((0,), (0,)), ((), ())), preferred_element_type=jnp.float32
    )


def tile_pairs(count):
    return [(row, col) for row in range(count) for col in range(row, count)]


def wide_bands(size):
    return [pl.ds(start, TILE) for start in range(0, size, TILE)]


def wide_steps(count, gram, whole, low, whole_low, mixer):
    bands = wide_bands(gram.shape[0])

    def step(repeat, carry):
        wide_mix(gram, whole, low, whole_low, mixer)
        for band in bands:
            half = first_coef * gram[band, :] + dot_nn(mixer[band, :], low[...])
            gram[band, :] = first_coef * half + dot_nn(half.astype(jnp.bfloat16), mixer[...])
            whole[band, :] = first_coef * whole[band, :] + dot_nn(mixer[band, :], whole_low[...])
        return carry

    lax.fori_loop(0, count, step, 0)


def wide_mix(gram, whole, low, whole_low, mixer):
    low[...] = gram[...].astype(jnp.bfloat16)
    whole_low[...] = whole[...].astype(jnp.bfloat16)
    for band in wide_bands(gram.shape[0]):
        squared = dot_nn(low[band, :], low[...])
        mixer[band, :] = (second_coef * gram[band, :] + third_coef * squared).astype(jnp.bfloat16)


def wide_first_kernel(block0, block1, block3, part0, part1, part2, gram, whole, low, mixer, whole_low, block2):
    size = gram.shape[0]
    bands = wide_bands(size)
    rows = lax.broadcasted_iota(jnp.int32, (TILE, size), 0)
    cols = lax.broadcasted_iota(jnp.int32, (TILE, size), 1)
    for part, band in zip((part0, part1, part2), bands):
        block2[band, :] = part[...]
    trace = 0.0
    for place, band in enumerate(bands):
        part = dot_nt(block0[band, :], block0[...])
        for block in (block1, block2, block3):
            part = part + dot_nt(block[band, :], block[...])
        gram[band, :] = part
        trace = trace + jnp.sum(jnp.where(rows + place * TILE == cols, part, 0.0))
    factor = 1.0 / (jnp.sqrt(trace) + orth_epsilon)
    for place, band in enumerate(bands):
        gram[band, :] = gram[band, :] * (factor * factor)
        whole[band, :] = jnp.where(rows + place * TILE == cols, factor, 0.0)
    wide_steps(2, gram, whole, low, whole_low, mixer)


def wide_last_kernel(gram_in, whole_in, out, gram, whole, low, mixer, whole_low):
    bands = wide_bands(gram.shape[0])
    gram[...] = gram_in[...]
    whole[...] = whole_in[...]
    wide_steps(2, gram, whole, low, whole_low, mixer)
    wide_mix(gram, whole, low, whole_low, mixer)
    for row, band in enumerate(bands):
        last = first_coef * whole[band, :] + dot_nn(mixer[band, :], whole_low[...])
        for place, pair in enumerate(tile_pairs(len(bands))):
            if pair[0] == row:
                out[place] = last[:, pair[1] * TILE : (pair[1] + 1) * TILE].astype(out.dtype)


def wide_call(kernel, size, out_shape, kept, scratch, name, inputs):
    vmem = pl.BlockSpec(memory_space=pltpu.VMEM)
    square = (size, size)
    return pl.pallas_call(
        kernel,
        out_shape=out_shape,
        in_specs=[vmem] * len(inputs),
        out_specs=jax.tree.map(lambda shape: vmem, out_shape),
        scratch_shapes=[pltpu.VMEM(square, jnp.float32)] * kept
        + [pltpu.VMEM(square, jnp.bfloat16)] * scratch,
        compiler_params=pltpu.CompilerParams(vmem_limit_bytes=VMEM_ASK),
        cost_estimate=pl.CostEstimate(
            flops=20 * size**3, bytes_accessed=8 * size * size, transcendentals=0
        ),
        name=name,
    )(*inputs)


def wide_first(blocks):
    size = blocks[0].shape[0]
    shape = jax.ShapeDtypeStruct((size, size), jnp.float32)
    return wide_call(wide_first_kernel, size, [shape, shape], 0, 4, "wide_first", blocks)


def wide_last(gram, whole):
    size = gram.shape[0]
    pairs = len(tile_pairs(size // TILE))
    shape = jax.ShapeDtypeStruct((pairs, TILE, TILE), jnp.bfloat16)
    return wide_call(wide_last_kernel, size, shape, 2, 3, "wide_last", (gram, whole))


def store_rows(chip, value, outs, which):
    depth = outs[0].shape[2]
    for turn, out in enumerate(outs):
        other = jnp.bitwise_xor(chip, turn)
        for core in range(2):
            row = ((other // 2) * 2 + core) * 2 + other % 2
            out[which, core] = value[pl.ds(pl.multiple_of(row * depth, 16), depth), :].astype(
                out.dtype
            )


def apply_kernel(place, *refs):
    mixers, pushes, outs, (full, moved) = refs[:4], refs[4:6], refs[6:10], refs[10:]
    chip, core, tp = place[0], place[1], place[2]
    count = full.shape[0] // TILE
    for which in range(2):
        source = lax.rem(tp - 2 * core - which + 4, 4)
        for step in range(4):

            @pl.when(source == step)
            def _():
                for spot, (row, col) in enumerate(tile_pairs(count)):
                    tile = mixers[step][spot]
                    full[pl.ds(row * TILE, TILE), pl.ds(col * TILE, TILE)] = tile
                    if row != col:
                        full[pl.ds(col * TILE, TILE), pl.ds(row * TILE, TILE)] = tile.T

        for spot in range(2):

            @pl.when(lax.rem(tp + spot, 2) == which)
            def _():
                moved[...] = dot_nn(full[...], pushes[spot][...])

        store_rows(chip, moved, outs, which)


def apply_mixers(place, mixers, pushes, depth):
    size, width = pushes[0].shape
    vmem = pl.BlockSpec(memory_space=pltpu.VMEM)
    shape = jax.ShapeDtypeStruct((2, 2, depth, width), jnp.bfloat16)
    return pl.pallas_call(
        apply_kernel,
        in_specs=[pl.BlockSpec(memory_space=pltpu.SMEM)] + [vmem] * 6,
        out_specs=[vmem] * 4,
        out_shape=[shape] * 4,
        scratch_shapes=[
            pltpu.VMEM((size, size), jnp.bfloat16),
            pltpu.VMEM((size, width), jnp.float32),
        ],
        compiler_params=pltpu.CompilerParams(vmem_limit_bytes=VMEM_ASK),
        cost_estimate=pl.CostEstimate(
            flops=4 * size**3, bytes_accessed=10 * size * size, transcendentals=0
        ),
        name="apply_mixers",
    )(place, *mixers, *pushes)


def push_kernel(place, own, *refs):
    gots, moments, refs = refs[:2], refs[2:6], refs[6:]
    pushes, bands, outs, (total,) = refs[:2], refs[2:5], refs[5:9], refs[9:]
    chip, core, tp = place[0], place[1], place[2]
    keep = 1.0 - momentum_decay
    depth = outs[0].shape[2]
    for which in range(2):
        total[...] = (
            own[which].astype(jnp.float32)
            + gots[0][which].astype(jnp.float32)
            + gots[1][which].astype(jnp.float32)
        )
        store_rows(chip, total, outs, which)
        for turn, moment in enumerate(moments):
            other = jnp.bitwise_xor(chip, turn)
            for side in range(2):
                row = ((other // 2) * 2 + jnp.bitwise_xor(core, side)) * 2 + other % 2
                rows = pl.ds(pl.multiple_of(row * depth, 16), depth)
                pushed = (
                    (keep + momentum_decay * keep) * total[rows, :]
                    + momentum_decay * momentum_decay * moment[2 * which + side].astype(jnp.float32)
                ).astype(jnp.bfloat16)
                for spot in range(2):

                    @pl.when(lax.rem(tp + spot, 2) == which)
                    def _():
                        pushes[spot][rows, :] = pushed

    for place, band in enumerate(bands):
        band[...] = pushes[0][pl.ds(place * TILE, TILE), :]


def push_rows(place, own, gots, moments):
    size, width = own.shape[1:]
    depth = moments[0].shape[1]
    vmem = pl.BlockSpec(memory_space=pltpu.VMEM)
    rows = jax.ShapeDtypeStruct((2, 2, depth, width), jnp.bfloat16)
    return pl.pallas_call(
        push_kernel,
        in_specs=[pl.BlockSpec(memory_space=pltpu.SMEM)] + [vmem] * 7,
        out_specs=[vmem] * 9,
        out_shape=[jax.ShapeDtypeStruct((size, width), jnp.bfloat16)] * 2
        + [jax.ShapeDtypeStruct((TILE, width), jnp.bfloat16)] * 3
        + [rows] * 4,
        scratch_shapes=[pltpu.VMEM((size, width), jnp.float32)],
        compiler_params=pltpu.CompilerParams(vmem_limit_bytes=VMEM_ASK),
        cost_estimate=pl.CostEstimate(
            flops=20 * size * width, bytes_accessed=24 * size * width, transcendentals=0
        ),
        name="push_rows",
    )(place, own, *gots, *moments)


def square_kernel(matrix, out, current, low, square, square_low, mixer):
    size = current.shape[0]
    bands = [pl.ds(start, TILE) for start in range(0, size, TILE)]
    total = 0.0
    for band in bands:
        part = matrix[band, :].astype(jnp.float32)
        total = total + jnp.sum(part * part)
    factor = 1.0 / (jnp.sqrt(total) + orth_epsilon)
    for band in bands:
        current[band, :] = matrix[band, :].astype(jnp.float32) * factor

    def step(repeat, carry):
        low[...] = current[...].astype(jnp.bfloat16)
        for band in bands:
            part = dot_nt(low[band, :], low[...])
            square[band, :] = part
            square_low[band, :] = part.astype(jnp.bfloat16)
        for band in bands:
            mixed = second_coef * square[band, :] + third_coef * dot_nn(
                square_low[band, :], square_low[...]
            )
            mixer[band, :] = mixed.astype(jnp.bfloat16)
        for band in bands:
            current[band, :] = first_coef * current[band, :] + dot_nn(mixer[band, :], low[...])
        return carry

    lax.fori_loop(0, 5, step, 0)
    out[...] = current[...].astype(out.dtype)


def orthogonal_square(matrix):
    size = matrix.shape[0]
    return pl.pallas_call(
        square_kernel,
        out_shape=jax.ShapeDtypeStruct((size, size), jnp.bfloat16),
        in_specs=[pl.BlockSpec(memory_space=pltpu.VMEM)],
        out_specs=pl.BlockSpec(memory_space=pltpu.VMEM),
        scratch_shapes=[
            pltpu.VMEM((size, size), jnp.float32),
            pltpu.VMEM((size, size), jnp.bfloat16),
            pltpu.VMEM((size, size), jnp.float32),
            pltpu.VMEM((size, size), jnp.bfloat16),
            pltpu.VMEM((size, size), jnp.bfloat16),
        ],
        compiler_params=pltpu.CompilerParams(vmem_limit_bytes=VMEM_ASK),
        cost_estimate=pl.CostEstimate(
            flops=30 * size**3, bytes_accessed=4 * matrix.size, transcendentals=0
        ),
        name="square_orthogonal",
    )(matrix)


root = math.sqrt(2.0 / math.pi)


def gelu_pair(value):
    squared = value * value
    part = 0.5 * jnp.tanh(value * (root + (root * 0.044715) * squared)) + 0.5
    bend = value * (2.0 * root + (6.0 * root * 0.044715) * squared)
    return value * part, part + part * (1.0 - part) * bend


def one_hot(rank):
    return lax.broadcasted_iota(jnp.int32, (SPAN, rank.shape[1]), 0) == rank


def assemble(chip, core, pieces, whole):
    depth = pieces[0].shape[1]
    for place, piece in enumerate(pieces):
        other = jnp.bitwise_xor(chip, place // 2)
        row = ((other // 2) * 2 + jnp.bitwise_xor(core, place % 2)) * 2 + other % 2
        whole[pl.ds(pl.multiple_of(row * depth, 16), depth), :] = piece[0]


def gate_of(hot, gate):
    return jnp.sum(jnp.where(hot, gate, 0.0), axis=1, keepdims=True)


def experts_kernel(
    starts, rank, gate, *refs
):
    blocks = rank.shape[1]
    ups, downs, refs = refs[:8], refs[8:16], refs[16:]
    tokens_hbm, refs = refs[: 2 * blocks], refs[2 * blocks :]
    hidden_out, before_out, *refs = refs
    outs, refs = refs[:5], refs[5:]
    rows, cots, upper, lower, slots, grads, upper_sum, lower_sum, leaving, sems, out_sems = refs
    targets = [(outs[turn].at[0], outs[turn].at[1]) for turn in range(3)] + [(outs[3], outs[4])]
    expert = pl.program_id(0)
    base = expert * (blocks + 1)
    chip = starts[pl.num_programs(0) * (blocks + 1)]
    core = starts[pl.num_programs(0) * (blocks + 1) + 1]
    low = jnp.bfloat16

    @pl.when(expert == 0)
    def _():
        copies = []
        for block in range(blocks):
            for which, held in enumerate((rows, cots)):
                place = which * blocks + block
                copies.append(
                    pltpu.make_async_copy(tokens_hbm[place], held.at[block], sems.at[place])
                )
        for copy in copies:
            copy.start()

    assemble(chip, core, ups, upper)
    assemble(chip, core, downs, lower)

    for block in range(blocks):

        @pl.when(expert == 0)
        def _():
            for which, held in enumerate((rows, cots)):
                place = which * blocks + block
                pltpu.make_async_copy(tokens_hbm[place], held.at[block], sems.at[place]).wait()

        start = pl.multiple_of(starts[base + block], 16)
        hot = one_hot(rank[0, block : block + 1, :])
        spread = jnp.where(hot, 1.0, 0.0).astype(low)
        weight = gate_of(hot, gate[0, block : block + 1, :])
        slots[pl.ds(start, SPAN), :] = dot_nn(spread, rows[block]).astype(low)
        grads[pl.ds(start, SPAN), :] = (dot_nn(spread, cots[block]) * weight).astype(low)

    end = pl.multiple_of(starts[base + blocks], 16)
    slots[pl.ds(end, TILE), :] = jnp.zeros((TILE, slots.shape[1]), low)
    grads[pl.ds(end, TILE), :] = jnp.zeros((TILE, slots.shape[1]), low)
    upper_sum[...] = jnp.zeros_like(upper_sum)
    lower_sum[...] = jnp.zeros_like(lower_sum)

    def work(tile, carry):
        band = pl.ds(pl.multiple_of(tile * TILE, TILE), TILE)
        slot_rows, slot_grads = slots[band, :], grads[band, :]
        hidden, slope = gelu_pair(dot_nn(slot_rows, upper[...]))
        hidden = hidden.astype(low)
        d_before = (dot_nn(slot_grads, lower[...]) * slope).astype(low)
        hidden_out[0, band, :] = hidden
        before_out[0, band, :] = d_before
        upper_sum[...] += dot_tn(slot_rows, d_before)
        lower_sum[...] += dot_tn(slot_grads, hidden)
        return carry

    lax.fori_loop(0, (starts[base + blocks] + TILE - 1) // TILE, work, 0)

    for turn, target in enumerate(targets):

        @pl.when(expert == turn)
        def _():
            if turn > 0:
                for which in range(2):
                    pltpu.make_async_copy(
                        leaving.at[which], targets[turn - 1][which], out_sems.at[2 * turn - 2 + which]
                    ).wait()
            leaving[0] = upper_sum[...].astype(low)
            leaving[1] = lower_sum[...].astype(low)
            copies = [
                pltpu.make_async_copy(leaving.at[which], target[which], out_sems.at[2 * turn + which])
                for which in range(2)
            ]
            for copy in copies:
                copy.start()
            if turn == 3:
                for copy in copies:
                    copy.wait()


def tokens_kernel(
    gated, starts, rank, gate, acts, *refs
):
    pieces, (part_own, part_other, whole, moved, spread, found) = refs[:8], refs[8:]
    expert = pl.program_id(0)
    count, blocks = rank.shape[0], rank.shape[1]
    base = expert * (blocks + 1)
    chip, core = starts[count * (blocks + 1)], starts[count * (blocks + 1) + 1]
    low = jnp.bfloat16

    @pl.when(expert == 0)
    def _():
        moved[...] = jnp.zeros_like(moved)

    assemble(chip, core, pieces, whole)

    def work(tile, carry):
        band = pl.ds(pl.multiple_of(tile * TILE, TILE), TILE)
        moved[expert, band, :] = dot_nt(acts[0, band, :], whole[...]).astype(low)
        return carry

    lax.fori_loop(0, (starts[base + blocks] + TILE - 1) // TILE, work, 0)

    @pl.when(expert == count - 1)
    def _():
        for side, part in enumerate((part_own, part_other)):
            for place in range(blocks // 2):
                block = side * (blocks // 2) + place
                ways, rows_of = spread.at[place % 2], found.at[place % 2]
                for each in range(count):
                    start = pl.multiple_of(starts[each * (blocks + 1) + block], 16)
                    hot = one_hot(rank[each, block : block + 1, :])
                    rows = moved[each, pl.ds(start, SPAN), :]
                    if gated:
                        weight = gate_of(hot, gate[each, block : block + 1, :])
                        rows = (rows.astype(jnp.float32) * weight).astype(low)
                    band = pl.ds(each * SPAN, SPAN)
                    ways[band, :] = jnp.where(hot, 1.0, 0.0).astype(low)
                    rows_of[band, :] = rows
                part[place] = dot_tn(ways[...], rows_of[...]).astype(low)


def pass_shapes(rank, pieces):
    count = pieces[0].shape[0]
    blocks, padded = rank.shape[1], rank.shape[2]
    tiles = -(-blocks * SPAN // TILE)

    def of_expert(expert, starts):
        return (expert, 0, 0)

    piece_specs = [
        pl.BlockSpec(
            (1,) + pieces[0].shape[1:],
            lambda expert, starts, turn=place // 2: (jnp.bitwise_xor(expert, turn), 0, 0),
        )
        for place in range(8)
    ]
    return count, blocks, padded, tiles, of_expert, piece_specs


def experts_pass(starts, rank, gate, rows, cots, ups, downs):
    count, blocks, padded, tiles, of_expert, piece_specs = pass_shapes(rank, ups)
    features = rows[0].shape[1]
    width = ups[0].shape[2]
    most = blocks * SPAN
    low = jnp.bfloat16
    vectors = pl.BlockSpec((1, blocks, padded), of_expert)
    acts = pl.BlockSpec((1, tiles * TILE, width), of_expert)
    acts_shape = jax.ShapeDtypeStruct((count, tiles * TILE, width), low)
    grad_shape = jax.ShapeDtypeStruct((features, width), low)
    pair_shape = jax.ShapeDtypeStruct((2, features, width), low)
    return pl.pallas_call(
        experts_kernel,
        grid_spec=pltpu.PrefetchScalarGridSpec(
            num_scalar_prefetch=1,
            grid=(count,),
            in_specs=[vectors, vectors]
            + piece_specs * 2
            + [pl.BlockSpec(memory_space=pl.ANY)] * (2 * blocks),
            out_specs=[acts, acts] + [pl.BlockSpec(memory_space=pl.ANY)] * 5,
            scratch_shapes=[
                pltpu.VMEM((blocks, padded, features), low),
                pltpu.VMEM((blocks, padded, features), low),
                pltpu.VMEM((features, width), low),
                pltpu.VMEM((features, width), low),
                pltpu.VMEM((most + TILE, features), low),
                pltpu.VMEM((most + TILE, features), low),
                pltpu.VMEM((features, width), jnp.float32),
                pltpu.VMEM((features, width), jnp.float32),
                pltpu.VMEM((2, features, width), low),
                pltpu.SemaphoreType.DMA((2 * blocks,)),
                pltpu.SemaphoreType.DMA((8,)),
            ],
        ),
        out_shape=[acts_shape, acts_shape] + [pair_shape] * 3 + [grad_shape] * 2,
        compiler_params=pltpu.CompilerParams(vmem_limit_bytes=VMEM_ASK),
        cost_estimate=pl.CostEstimate(
            flops=4 * count * most * features * width,
            bytes_accessed=60 * 1024 * 1024,
            transcendentals=count * most * width,
        ),
        name="experts_pass",
    )(starts, rank, gate, *ups, *downs, *rows, *cots)


def tokens_pass(starts, rank, gate, acts, pieces, gated):
    count, blocks, padded, tiles, of_expert, piece_specs = pass_shapes(rank, pieces)
    width = pieces[0].shape[2]
    features = 8 * pieces[0].shape[1]
    most = blocks * SPAN
    low = jnp.bfloat16
    vectors = pl.BlockSpec(rank.shape, lambda expert, starts: (0, 0, 0))
    parts = pl.BlockSpec((blocks // 2, padded, features), lambda expert, starts: (0, 0, 0))
    part_shape = jax.ShapeDtypeStruct((blocks // 2, padded, features), low)
    return pl.pallas_call(
        functools.partial(tokens_kernel, gated),
        grid_spec=pltpu.PrefetchScalarGridSpec(
            num_scalar_prefetch=1,
            grid=(count,),
            in_specs=[vectors, vectors, pl.BlockSpec((1,) + acts.shape[1:], of_expert)]
            + piece_specs,
            out_specs=[parts, parts],
            scratch_shapes=[
                pltpu.VMEM((features, width), low),
                pltpu.VMEM((count, most + TILE, features), low),
                pltpu.VMEM((2, count * SPAN, padded), low),
                pltpu.VMEM((2, count * SPAN, features), low),
            ],
        ),
        out_shape=[part_shape, part_shape],
        compiler_params=pltpu.CompilerParams(vmem_limit_bytes=VMEM_ASK),
        cost_estimate=pl.CostEstimate(
            flops=2 * count * most * features * width,
            bytes_accessed=30 * 1024 * 1024,
            transcendentals=0,
        ),
        name="tokens_gated" if gated else "tokens_plain",
    )(starts, rank, gate, acts, *pieces)


IMAGE = 208


def row_norm(values, factor, offset):
    width = values.shape[1]
    average = jnp.sum(values, axis=1, keepdims=True) / width
    centred = values - average
    spread = jnp.sum(centred * centred, axis=1, keepdims=True) / width
    inverse = lax.rsqrt(spread + norm_epsilon)
    unit = centred * inverse
    return unit * factor + offset, unit, inverse


def row_norm_back(gradient, unit, inverse, factor):
    width = gradient.shape[1]
    inner = gradient * factor
    average = jnp.sum(inner, axis=1, keepdims=True) / width
    along = jnp.sum(inner * unit, axis=1, keepdims=True) / width
    return inverse * (inner - average - unit * along)


def head_soft(query, key, here, keys_used):
    own = jnp.where(here, query, jnp.zeros_like(query))
    scores = dot_nt(own, key) * (HEAD_DIM ** (-0.5))
    scores = jnp.where(keys_used, scores, -1e30)
    powers = jnp.exp(scores - jnp.max(scores, axis=1, keepdims=True))
    return powers / jnp.sum(powers, axis=1, keepdims=True)


def forward_kernel(
    place, tokens, norms, w0, w1, w2, w3, others_near, others_far,
    normed_out, qkv_out, blended_out, residual_out, second_out, weights,
):
    features = tokens.shape[1]
    low = jnp.bfloat16

    chip, core = place[0], place[1]
    depth = features // 8
    others = (others_near.at[0], others_near.at[1], others_far.at[0], others_far.at[1])
    for side, pieces in enumerate(((w0, w1, w2, w3), others)):
        for turn, piece in enumerate(pieces):
            other = jnp.bitwise_xor(chip, turn)
            row = ((other // 2) * 2 + jnp.bitwise_xor(core, side)) * 2 + other % 2
            rows = pl.ds(pl.multiple_of(row * depth, 16), depth)
            for which in range(4):
                weights[which, rows, :] = piece[which]

    normed, unused, unused = row_norm(
        tokens[...].astype(jnp.float32), norms[0:1, :], norms[2:3, :]
    )
    normed_out[...] = normed.astype(low)
    for which in range(3):
        qkv_out[which] = dot_nn(normed_out[...], weights[which]).astype(low)
    keys_used = lax.broadcasted_iota(jnp.int32, (IMAGE, IMAGE), 1) < LEN
    first = lax.broadcasted_iota(jnp.int32, (IMAGE, 2 * HEAD_DIM), 1) < HEAD_DIM

    def attend(image, carry):
        rows = pl.ds(pl.multiple_of(image * IMAGE, 16), IMAGE)
        for start in range(0, features, 2 * HEAD_DIM):
            cols = pl.ds(start, 2 * HEAD_DIM)
            query, key, value = (qkv_out[which, rows, cols] for which in range(3))
            mixed = []
            for here in (first, jnp.logical_not(first)):
                soft = head_soft(query, key, here, keys_used).astype(low)
                mixed.append(dot_nn(soft, value))
            blended_out[rows, cols] = jnp.where(first, mixed[0], mixed[1]).astype(low)
        return carry

    lax.fori_loop(0, tokens.shape[0] // IMAGE, attend, 0)
    residual = tokens[...].astype(jnp.float32) + dot_nn(blended_out[...], weights[3])
    residual_out[...] = residual
    second, unused, unused = row_norm(residual, norms[1:2, :], norms[3:4, :])
    second_out[...] = second.astype(low)


def attention_forward(place, tokens, norms, pieces, others):
    rows, features = tokens.shape
    low = jnp.bfloat16
    vmem = pl.BlockSpec(memory_space=pltpu.VMEM)
    shape = jax.ShapeDtypeStruct((rows, features), low)
    return pl.pallas_call(
        forward_kernel,
        in_specs=[pl.BlockSpec(memory_space=pltpu.SMEM)] + [vmem] * 8,
        out_specs=[vmem] * 6,
        out_shape=[
            shape,
            jax.ShapeDtypeStruct((3, rows, features), low),
            shape,
            jax.ShapeDtypeStruct((rows, features), jnp.float32),
            shape,
            jax.ShapeDtypeStruct((4, features, features), low),
        ],
        compiler_params=pltpu.CompilerParams(vmem_limit_bytes=VMEM_ASK),
        cost_estimate=pl.CostEstimate(
            flops=10 * rows * features * features,
            bytes_accessed=16 * 1024 * 1024,
            transcendentals=0,
        ),
        name="attention_forward",
    )(place, tokens, norms, *pieces, *others)


def backward_kernel(
    place, tokens, cots, residual, blended, normed, qkv, weights, norms,
    second0, second1, second2, second3,
    input_grad, mine, theirs, vectors,
    part, d_heads, d_qkv, d_sum,
):
    rows_all, features = tokens.shape
    low = jnp.bfloat16
    core = place[1]

    def store_part(which, value):
        part[...] = value
        slab = mine.shape[2]
        for side in range(2):
            own = pl.ds(pl.multiple_of((2 * side + core) * slab, slab), slab)
            other = pl.ds(pl.multiple_of((2 * side + 1 - core) * slab, slab), slab)
            mine[which, side] = part[own, :].astype(low)
            theirs[which, side] = part[other, :].astype(low)

    d_second = second0[...].astype(jnp.float32)
    for piece in (second1, second2, second3):
        d_second = d_second + piece[...].astype(jnp.float32)
    unused, unit, inverse = row_norm(residual[...], norms[1:2, :], norms[3:4, :])
    vectors[...] = jnp.zeros_like(vectors)
    vectors[1:2, :] = jnp.sum(d_second * unit, axis=0, keepdims=True)
    vectors[3:4, :] = jnp.sum(d_second, axis=0, keepdims=True)
    d_sum[...] = cots[...].astype(jnp.float32) + row_norm_back(
        d_second, unit, inverse, norms[1:2, :]
    )
    d_attended = d_sum[...].astype(low)
    d_heads[...] = dot_nt(d_attended, weights[3]).astype(low)
    store_part(3, dot_tn(blended[...], d_attended))

    keys_used = lax.broadcasted_iota(jnp.int32, (IMAGE, IMAGE), 1) < LEN
    first = lax.broadcasted_iota(jnp.int32, (IMAGE, 2 * HEAD_DIM), 1) < HEAD_DIM
    scale = HEAD_DIM ** (-0.5)

    def attend(image, carry):
        rows = pl.ds(pl.multiple_of(image * IMAGE, 16), IMAGE)
        for start in range(0, features, 2 * HEAD_DIM):
            cols = pl.ds(start, 2 * HEAD_DIM)
            query, key, value = (qkv[which, rows, cols] for which in range(3))
            upper = d_heads[rows, cols]
            found = []
            for here in (first, jnp.logical_not(first)):
                soft = head_soft(query, key, here, keys_used)
                d_soft = dot_nt(jnp.where(here, upper, jnp.zeros_like(upper)), value)
                inner = jnp.sum(soft * d_soft, axis=1, keepdims=True)
                d_scores = (soft * (d_soft - inner)).astype(low)
                found.append(
                    (
                        dot_nn(d_scores, key) * scale,
                        dot_tn(d_scores, query) * scale,
                        dot_tn(soft.astype(low), upper),
                    )
                )
            for which in range(3):
                d_qkv[which, rows, cols] = jnp.where(
                    first, found[0][which], found[1][which]
                ).astype(low)
        return carry

    lax.fori_loop(0, rows_all // IMAGE, attend, 0)
    d_normed = dot_nt(d_qkv[0], weights[0])
    for which in range(1, 3):
        d_normed = d_normed + dot_nt(d_qkv[which], weights[which])
    for which in range(3):
        store_part(which, dot_tn(normed[...], d_qkv[which]))
    unused, unit, inverse = row_norm(
        tokens[...].astype(jnp.float32), norms[0:1, :], norms[2:3, :]
    )
    vectors[0:1, :] = jnp.sum(d_normed * unit, axis=0, keepdims=True)
    vectors[2:3, :] = jnp.sum(d_normed, axis=0, keepdims=True)
    input_grad[...] = d_sum[...] + row_norm_back(d_normed, unit, inverse, norms[0:1, :])


def attention_backward(place, tokens, cots, residual, blended, normed, qkv, seconds, weights, norms):
    rows, features = tokens.shape
    low = jnp.bfloat16
    vmem = pl.BlockSpec(memory_space=pltpu.VMEM)
    half_shape = jax.ShapeDtypeStruct((4, 2, features // 4, features), low)
    return pl.pallas_call(
        backward_kernel,
        in_specs=[pl.BlockSpec(memory_space=pltpu.SMEM)] + [vmem] * 12,
        out_specs=[vmem] * 4,
        scratch_shapes=[
            pltpu.VMEM((features, features), jnp.float32),
            pltpu.VMEM((rows, features), low),
            pltpu.VMEM((3, rows, features), low),
            pltpu.VMEM((rows, features), jnp.float32),
        ],
        out_shape=[
            jax.ShapeDtypeStruct((rows, features), jnp.float32),
            half_shape,
            half_shape,
            jax.ShapeDtypeStruct((8, features), jnp.float32),
        ],
        compiler_params=pltpu.CompilerParams(vmem_limit_bytes=VMEM_ASK),
        cost_estimate=pl.CostEstimate(
            flops=40 * rows * features * features,
            bytes_accessed=24 * 1024 * 1024,
            transcendentals=0,
        ),
        name="attention_backward",
    )(place, tokens, cots, residual, blended, normed, qkv, weights, norms, *seconds)


def route_to(place):
    shards, ctxs, tps = (lax.axis_size(name) for name in axes)
    pairs = []
    for shard in range(shards):
        for ctx in range(ctxs):
            for tp in range(tps):
                other_shard, other_ctx, other_tp = place(shard, ctx, tp)
                pairs.append(
                    (
                        (shard * ctxs + ctx) * tps + tp,
                        (other_shard * ctxs + other_ctx) * tps + other_tp % tps,
                    )
                )
    return pairs


def swap_core(value):
    return lax.ppermute(value, axes, route_to(lambda s, c, t: (s ^ 1, c, t)))


def swap_chip(value, turn):
    return lax.ppermute(
        value, axes, route_to(lambda s, c, t: (s ^ (turn & 2), c ^ (turn & 1), t))
    )


def swap_tp(value, turn):
    return lax.ppermute(value, axes, route_to(lambda s, c, t: (s, c, t ^ turn)))


def pass_on(value):
    return lax.ppermute(value, axes, route_to(lambda s, c, t: (s, c, t + 1)))


def worker_route(source, target):
    shards, ctxs, tps = (lax.axis_size(name) for name in axes)
    pairs = []
    for shard in range(shards):
        for ctx in range(ctxs):
            for worker in range(tps):
                if worker // 2 == shard % 2:
                    base = (shard * ctxs + ctx) * tps
                    pairs.append((base + source(worker) % tps, base + target(worker) % tps))
    return pairs


def to_worker(value, turn):
    return lax.ppermute(value, axes, worker_route(lambda w: w + turn, lambda w: w))


def from_worker(value, turn):
    step = 1 if turn > 0 else -1
    return lax.ppermute(
        value, axes, worker_route(lambda w: w + turn - step, lambda w: w + turn)
    )


def pick(value, index, axis=0):
    return lax.dynamic_index_in_dim(value, index, axis, keepdims=False)


def relative(value, chip):
    return [pick(value, jnp.bitwise_xor(chip, turn)) for turn in range(4)]


def pass_by(value, steps):
    return lax.ppermute(value, axes, route_to(lambda s, c, t: (s, c, t + steps)))


def direct_gather(value):
    return [value] + [pass_by(value, steps) for steps in range(1, lax.axis_size("tp"))]


class Live:
    def __init__(self, values=None):
        vars(self).update(values or {})

    @property
    def drop(self):
        return Drop(vars(self))


class Drop:
    def __init__(self, values):
        self._values = values

    def __getattr__(self, name):
        return self._values.pop(name)


def hold(live):
    return Live(lax.optimization_barrier(vars(live)))


def by_tp(held, tp):
    count = len(held)
    stacked = jnp.stack(held)
    return jnp.stack([pick(stacked, (tp - place) % count) for place in range(count)])


def place_chips(pieces, chip):
    stacked = jnp.stack(pieces)
    return jnp.stack([pick(stacked, jnp.bitwise_xor(chip, place)) for place in range(4)])


def place_cores(own, other, core):
    return jnp.where(core == 0, jnp.stack([own, other]), jnp.stack([other, own]))


def low_dot(spec, left, right):
    return jnp.einsum(
        spec,
        left.astype(jnp.bfloat16),
        right.astype(jnp.bfloat16),
        preferred_element_type=jnp.float32,
    )


def plane_device(
    tokens,
    cotangent,
    routing,
    gating,
    inward,
    outward,
    scales,
    shifts,
    upward,
    downward,
    inward_moment,
    outward_moment,
    scales_moment,
    shifts_moment,
    upward_moment,
    downward_moment,
):
    rows_here = tokens.shape[1]
    features = tokens.shape[2]
    seqs = rows_here // LEN
    experts = upward.shape[0]
    half_experts = experts // 2
    shard = lax.axis_index("shard")
    core = shard % 2
    ctx = lax.axis_index("ctx")
    tp = lax.axis_index("tp")
    tps = lax.axis_size("tp")
    devices = lax.axis_size(axes)
    chip = (shard // 2) * 2 + ctx
    low = jnp.bfloat16
    rows_attn = inward.shape[1]
    rows_local = upward.shape[1]
    cols_local = upward.shape[2]

    v = Live()
    device = jnp.stack([chip, core, tp]).astype(jnp.int32)
    y_here, x_here = shard // 2, ctx
    padded = seqs * IMAGE
    half = tps // 2
    own_tokens, own_cot = (
        jnp.pad(
            value[0].reshape(seqs, LEN, features), ((0, 0), (0, IMAGE - LEN), (0, 0))
        ).reshape(padded, features)
        for value in (tokens, cotangent)
    )

    def halves(value):
        value = value.astype(low).reshape(2, half_experts, rows_local, cols_local)
        return pick(value, core), pick(value, 1 - core)

    def own_order(value):
        return jnp.stack([pick(value, jnp.bitwise_xor(chip, r)) for r in range(4)])

    up_kept, up_sent = halves(upward)
    down_kept, down_sent = halves(downward)
    v.up, v.down = [own_order(up_kept)], [own_order(down_kept)]
    v.up_x, v.down_y = [swap_chip(v.up[0], 1)], [swap_chip(v.down[0], 2)]
    v.column = direct_gather(jnp.concatenate([inward, outward[None]]))
    v.sent = jnp.stack([up_sent, down_sent])
    v.cots = [own_cot]

    packed = jnp.concatenate([routing[0].astype(jnp.float32).T, gating[0].T])
    packed = jnp.pad(
        packed.reshape(4, seqs, LEN), ((0, 0), (0, 0), (0, IMAGE - LEN)), constant_values=-1.0
    )
    norm_rows = jnp.concatenate([scales, shifts]).astype(jnp.float32)
    packed = jnp.concatenate(
        [packed.reshape(4, padded), jnp.pad(norm_rows, ((0, 0), (0, padded - rows_attn)))]
    )
    v.packs = direct_gather(packed)
    v = hold(v)

    column = by_tp(v.drop.column, tp).transpose(1, 0, 2, 3)
    column = column.reshape(4, tps * rows_attn, features)
    v.pieces = [column, swap_chip(column, 1), swap_chip(column, 2)]
    v.cots.append(pass_on(v.cots[-1]))
    v.got = swap_core(v.drop.sent)
    packs = jnp.stack(v.packs)
    v.packs = [packs, swap_core(packs)]
    v = hold(v)

    column, from_x, from_y = v.pieces
    v.far = [swap_chip(from_x[:2], 2), swap_chip(from_y[2:], 1)]
    v.others = [swap_core(jnp.stack(v.pieces[:2]))]
    got = v.drop.got
    v.up.append(own_order(got[0]))
    v.down.append(own_order(got[1]))
    own_packs, other_packs = v.drop.packs
    norms = [by_tp(list(each[:, 4:, :rows_attn]), tp) for each in (own_packs, other_packs)]
    norms = place_cores(*norms, core)
    v.norms = [norms, swap_chip(norms, 1)]
    packs = jnp.concatenate([own_packs, other_packs])
    mine = core * half_experts + jnp.bitwise_xor(chip, jnp.arange(4, dtype=jnp.int32))
    hits = packs[None, :, :2] == mine.astype(jnp.float32)[:, None, None, None]
    chosen = jnp.any(hits, axis=2)
    gate_tok = jnp.sum(jnp.where(hits, packs[None, :, 2:4], 0.0), axis=2)
    places = jnp.arange(padded)
    earlier = (places[:, None] < places[None, :]).astype(low)
    rank = jnp.einsum(
        "rbt,tu->rbu", chosen.astype(low), earlier, preferred_element_type=jnp.float32
    )
    rank = jnp.where(chosen, rank, -1.0).astype(jnp.int32)
    counts = jnp.sum(chosen.astype(jnp.int32), axis=2)
    counts = (counts + 15) // 16 * 16
    starts = jnp.cumsum(jnp.pad(counts, ((0, 0), (1, 0))), axis=1).astype(jnp.int32).reshape(-1)
    v.routes = (jnp.concatenate([starts, device[:2]]), rank, gate_tok)
    v = hold(v)
    far = jnp.concatenate(v.drop.far)
    v.pieces = v.pieces + [far]
    v.others.append(swap_core(jnp.stack(v.pieces[2:])))
    v.cots.append(pass_on(v.cots[-1]))
    v.up_x.append(swap_chip(v.up[1], 1))
    v.down_y.append(swap_chip(v.down[1], 2))
    norms = place_cores(*v.norms, ctx)
    v.norms = [norms, swap_chip(norms, 2)]
    v = hold(v)
    norms = place_cores(*v.drop.norms, y_here)
    norms = norms.transpose(4, 0, 2, 1, 3, 5).reshape(4, features)

    normed, qkv, blended, residual, second, full_weights = attention_forward(
        device, own_tokens, norms, v.drop.pieces, v.drop.others
    )
    v.seconds = [second]
    v.up_xy, v.down_xy = [swap_chip(v.up_x[0], 2)], [swap_chip(v.down_y[0], 1)]
    v.cots.append(pass_on(v.cots[-1]))
    v.cots_other = [swap_core(each) for each in v.cots[:2]]
    v = hold(v)

    v.seconds.append(pass_on(v.seconds[-1]))
    v.up_xy.append(swap_chip(v.up_x[1], 2))
    v.down_xy.append(swap_chip(v.down_y[1], 1))
    v.cots_other += [swap_core(each) for each in v.cots[2:]]
    v = hold(v)
    v.seconds.append(pass_on(v.seconds[-1]))
    v.down_x, v.up_y = [swap_chip(v.down[0], 1)], [swap_chip(v.up[0], 2)]
    v.seconds_other = [swap_core(v.seconds[0])]
    moments = halves(upward_moment) + halves(downward_moment)
    v.moments = moments[0], moments[2], swap_core(jnp.stack([moments[1], moments[3]]))
    v = hold(v)
    v.seconds.append(pass_on(v.seconds[-1]))
    v.down_x.append(swap_chip(v.down[1], 1))
    v.up_y.append(swap_chip(v.up[1], 2))
    v.seconds_other += [swap_core(each) for each in v.seconds[1:3]]
    moments = v.drop.moments
    moments = jnp.stack([moments[0], moments[2][0], moments[1], moments[2][1]])
    v.moments = [pick(moments, jnp.bitwise_xor(chip, turn), 1) for turn in range(4)]
    v = hold(v)
    v.seconds_other.append(swap_core(v.seconds[3]))
    v = hold(v)

    ups = v.drop.up + v.drop.up_x + v.drop.up_y + v.drop.up_xy
    downs = v.drop.down + v.drop.down_x + v.drop.down_y + v.drop.down_xy
    v.moments = [v.moments[0]] + [swap_chip(v.moments[turn], turn) for turn in range(1, 4)]
    hidden, before, v.own, v.near_x, v.near_y, v.far_x, v.far_y = experts_pass(
        *v.routes,
        v.drop.seconds + v.drop.seconds_other,
        v.drop.cots + v.drop.cots_other,
        ups, downs,
    )
    v.hidden, v.before = hidden, before
    v.ups, v.downs = ups, downs
    v = hold(v)

    v.part = tokens_pass(*v.routes, v.drop.before, v.drop.ups, False)
    v.far_x, v.far_y = swap_chip(v.far_x, 1), swap_chip(v.far_y, 2)
    v = hold(v)

    def join(own, other):
        return (own.astype(jnp.float32) + other.astype(jnp.float32)).astype(low)

    v.along_x = v.near_x.at[1].set(join(v.near_x[1], v.drop.far_y))
    v.along_y = v.near_y.at[0].set(join(v.near_y[0], v.drop.far_x))
    v.near_x = v.near_y = None
    v.part = [v.part[0], swap_core(v.part[1])]
    v = hold(v)
    kept = join(*v.drop.part)
    v.along_x, v.along_y = swap_chip(v.along_x, 1), swap_chip(v.along_y, 2)
    v.seconds = [kept[0]] + [pass_by(kept[turn], -turn) for turn in range(1, tps)]
    v.mixed = tokens_pass(*v.drop.routes, v.drop.hidden, v.drop.downs, True)
    v = hold(v)

    push, push_next, band0, band1, band2, *rows = push_rows(
        device, v.drop.own, (v.drop.along_x, v.drop.along_y), v.drop.moments
    )
    v.push, v.blocks, v.rows = [push, push_next], [band0, band1, band2], rows
    v.mixed = [v.mixed[0], swap_core(v.mixed[1])]
    v = hold(v)

    def rows_out(rows):
        return [rows[0]] + [swap_chip(rows[turn], turn) for turn in range(1, 4)]

    def rows_between(got):
        got = place_chips(got, chip)
        return pick(got, core, 2), swap_core(pick(got, 1 - core, 2))

    def rows_in(kept, got):
        joined = place_cores(kept, got, core).transpose(2, 0, 1, 3, 4)
        joined = joined.reshape(2, experts, rows_local, cols_local)
        return joined.astype(jnp.float32)

    v.joined = [v.push[0]] + [to_worker(v.push[1], turn) for turn in (1, 3)]
    v.rows = rows_out(v.rows)
    v.input_grad, v.own, v.gone, v.vectors = attention_backward(
        device, own_tokens, own_cot, residual, blended, normed, qkv,
        v.drop.seconds,
        full_weights, norms,
    )
    v = hold(v)

    def added(value, got):
        return value.astype(jnp.float32) + got.astype(jnp.float32)

    shape = (4, 2, 2, tps, rows_attn, features)
    v.gone = swap_core(v.gone)
    v.blocks[:2] = [to_worker(block, 2) for block in v.blocks[:2]]
    vectors = v.vectors[:4]
    v.vectors = [vectors, swap_core(vectors)]
    v.input_grad = v.input_grad.reshape(seqs, IMAGE, features)[:, :LEN].reshape(rows_here, features)
    mixed = added(*v.mixed)
    v.mixed = [mixed[0]] + [mixed[turn].astype(low) for turn in range(1, tps)]
    v = hold(v)
    own, gone = v.drop.own.reshape(shape), v.drop.gone.reshape(shape)

    def first_part(x):
        return added(pick(own, x, 2)[:, :, :half], pick(gone, x, 2)[:, :, :half])

    def last_part(y):
        return added(pick(own, y, 1)[:, :, half:], pick(gone, y, 1)[:, :, half:])

    v.first = [first_part(x_here), swap_chip(first_part(1 - x_here).astype(low), 1)]
    v.last = [last_part(y_here), swap_chip(last_part(1 - y_here).astype(low), 2)]
    v.mixed.append(pass_on(v.mixed[1]))
    vectors = sum(v.vectors)
    v.vectors = [vectors, swap_chip(vectors, 1)]
    v = hold(v)
    first, last = added(*v.first), added(*v.last)
    v.first = [pick(first, y_here, 1), swap_chip(pick(first, 1 - y_here, 1).astype(low), 2)]
    v.last = [pick(last, x_here, 1), swap_chip(pick(last, 1 - x_here, 1).astype(low), 1)]
    v.blocks[2] = to_worker(v.blocks[2], 2)
    vectors = sum(v.vectors)
    v.vectors = [vectors, swap_chip(vectors, 2)]
    v = hold(v)

    sums = jnp.concatenate([added(*v.drop.first), added(*v.drop.last)], axis=1)
    vectors = jnp.pad(sum(v.drop.vectors)[:, None], ((0, 0), (0, 7), (0, 0)))
    parts = [
        jnp.concatenate([pick(sums, (tp - turn) % tps, 1), vectors], axis=1).astype(low)
        for turn in range(tps)
    ]
    v.sums = [parts[0]] + [pass_by(parts[turn], -turn) for turn in range(1, tps)]
    v.mixers = wide_first(v.drop.joined + v.drop.blocks)
    v = hold(v)
    sums = sum(part.astype(jnp.float32) for part in v.drop.sums)
    v.vectors = lax.dynamic_slice(
        sums[:, rows_attn], (0, lax.axis_index(axes) * rows_attn), (4, rows_attn)
    )
    sums = sums[:, :rows_attn]
    inward_grad, outward_grad = sums[:3], sums[3]
    inward_state, inward_push = advance(inward_grad, inward_moment)
    outward_state, outward_push = advance(outward_grad, outward_moment)
    v.column = direct_gather(jnp.concatenate([inward_push, outward_push[None]]).astype(low))
    v.mixers = [wide_last(*v.mixers)]
    v = hold(v)
    column = by_tp(v.drop.column, tp).transpose(1, 0, 2, 3)
    gone = relative(column, chip)
    v.pushes = [gone[0]] + [swap_chip(gone[turn], turn) for turn in range(1, 4)]
    v.mixers.append(from_worker(v.mixers[0], 1))
    v.mixers.append(from_worker(v.mixers[0], -1))
    v = hold(v)
    pushes = place_chips(v.pushes, chip)
    v.pushes = [pushes, swap_core(pushes)]
    v.mixers.insert(2, from_worker(v.mixers[1], 2))
    v.rows = rows_between(v.rows)
    v = hold(v)
    pushes = place_cores(*v.drop.pushes, core)
    pushes = pushes.reshape(2, 2, 2, tps, rows_attn, features).transpose(1, 0, 2, 3, 4, 5)
    v.pushes = pushes.reshape(features, features)
    v.new = apply_mixers(device, v.drop.mixers, v.drop.push, rows_local)
    v = hold(v)

    v.new = rows_out(v.new)
    v.mixed[4] = pass_on(added(v.mixed[2], v.mixed[4]).astype(low))
    v.moved = orthogonal_square(v.drop.pushes)
    v = hold(v)
    moved = v.drop.moved.reshape(2, 2, 2, tps, rows_attn, features)
    moved = pick(pick(moved, core, 1), tp, 2).reshape(4, rows_attn, features)
    gone = relative(moved, chip)
    v.moved = [gone[0]] + [swap_chip(gone[turn], turn) for turn in range(1, 4)]
    v.new = rows_between(v.new)
    upward_grad, downward_grad = rows_in(*v.drop.rows)
    v.states = [
        (upward_grad, advance(upward_grad, upward_moment)[0]),
        (downward_grad, advance(downward_grad, downward_moment)[0]),
    ]
    v.mixed[4] = pass_on(added(v.mixed[3], v.mixed[4]).astype(low))
    v = hold(v)
    mixed = v.drop.mixed
    result = (residual + added(mixed[0], mixed[4])).astype(low)
    result = result.reshape(seqs, IMAGE, features)[:, :LEN].reshape(rows_here, features)
    input_grad = v.input_grad
    scales_grad, shifts_grad = v.vectors[:2], v.vectors[2:]
    scales_state, scales_push = advance(scales_grad, scales_moment)
    shifts_state, shifts_push = advance(shifts_grad, shifts_moment)
    up_new, down_new = rows_in(*v.new)
    upward_new = upward.astype(jnp.float32) - 2.0 * up_new
    downward_new = downward.astype(jnp.float32) - down_new
    (upward_grad, upward_state), (downward_grad, downward_state) = v.states
    got = place_chips(v.moved, chip).astype(jnp.float32)
    inward_new = inward.astype(jnp.float32) - got[:3]
    outward_new = outward.astype(jnp.float32) - got[3]
    vector_rate = 0.6 / math.sqrt(devices * rows_here)
    scales_new = scales.astype(jnp.float32) - vector_rate * scales_push
    shifts_new = shifts.astype(jnp.float32) - vector_rate * shifts_push
    return (
        result[None],
        input_grad[None],
        inward_grad,
        outward_grad,
        scales_grad,
        shifts_grad,
        upward_grad,
        downward_grad,
        inward_state,
        outward_state,
        scales_state,
        shifts_state,
        upward_state,
        downward_state,
        inward_new,
        outward_new,
        scales_new,
        shifts_new,
        upward_new,
        downward_new,
    )


def solution(mesh):
    in_specs = (
        P(("shard", "tp"), "ctx", None),
        P(("shard", "tp"), "ctx", None),
        P(("shard", "tp"), "ctx", None),
        P(("shard", "tp"), "ctx", None),
        P(None, ("shard", "ctx", "tp"), None),
        P(("shard", "ctx", "tp"), None),
        P(None, ("shard", "ctx", "tp")),
        P(None, ("shard", "ctx", "tp")),
        P(None, ("shard", "ctx"), "tp"),
        P(None, ("shard", "ctx"), "tp"),
        P(None, ("shard", "ctx", "tp"), None),
        P(("shard", "ctx", "tp"), None),
        P(None, ("shard", "ctx", "tp")),
        P(None, ("shard", "ctx", "tp")),
        P(None, ("shard", "ctx"), "tp"),
        P(None, ("shard", "ctx"), "tp"),
    )
    out_specs = (
        P(("shard", "tp"), "ctx", None),
        P(("shard", "tp"), "ctx", None),
        P(None, ("shard", "ctx", "tp"), None),
        P(("shard", "ctx", "tp"), None),
        P(None, ("shard", "ctx", "tp")),
        P(None, ("shard", "ctx", "tp")),
        P(None, ("shard", "ctx"), "tp"),
        P(None, ("shard", "ctx"), "tp"),
        P(None, ("shard", "ctx", "tp"), None),
        P(("shard", "ctx", "tp"), None),
        P(None, ("shard", "ctx", "tp")),
        P(None, ("shard", "ctx", "tp")),
        P(None, ("shard", "ctx"), "tp"),
        P(None, ("shard", "ctx"), "tp"),
        P(None, ("shard", "ctx", "tp"), None),
        P(("shard", "ctx", "tp"), None),
        P(None, ("shard", "ctx", "tp")),
        P(None, ("shard", "ctx", "tp")),
        P(None, ("shard", "ctx"), "tp"),
        P(None, ("shard", "ctx"), "tp"),
    )
    body = plane_device if mesh.shape["shard"] == 4 and mesh.shape["ctx"] == 2 and mesh.shape["tp"] == 4 else on_device
    return jax.shard_map(
        body, mesh=mesh, in_specs=in_specs, out_specs=out_specs, check_vma=False
    )
```

```python
import functools
import math

import jax
import jax.numpy as jnp
import numpy as np
from jax import lax
from jax.experimental import pallas as pl
from jax.experimental.pallas import tpu as pltpu
from jax.sharding import PartitionSpec as P

HEAD_DIM = 64
LEN = 197


first_coef = 3.4445
second_coef = -4.775
third_coef = 2.0315
momentum_decay = 0.9
norm_epsilon = 1e-06
orth_epsilon = 1e-07
highest = lax.Precision.HIGHEST


def normalize(values, factor, offset):
    average = jnp.mean(values, axis=-1, keepdims=True)
    centred = values - average
    inverse = lax.rsqrt(jnp.mean(centred * centred, axis=-1, keepdims=True) + norm_epsilon)
    unit_rows = centred * inverse
    return (unit_rows * factor + offset, unit_rows, inverse)


def normalize_back(gradient, unit_rows, inverse, factor):
    inner = gradient * factor
    average = jnp.mean(inner, axis=-1, keepdims=True)
    along = jnp.mean(inner * unit_rows, axis=-1, keepdims=True)
    back = inverse * (inner - average - unit_rows * along)
    return (back, jnp.sum(gradient * unit_rows, axis=0), jnp.sum(gradient, axis=0))


def slot_sources(routes, experts, capacity):
    pairs = routes.shape[0] * routes.shape[1]
    chosen = routes.reshape(pairs)
    onehot = (chosen[:, None] == jnp.arange(experts, dtype=jnp.int32)[None, :]).astype(jnp.int32)
    earlier = jnp.cumsum(onehot, axis=0) - onehot
    placed = jnp.sum(earlier * onehot, axis=1) + chosen * capacity
    matches = placed[None, :] == jnp.arange(experts * capacity, dtype=jnp.int32)[:, None]
    source = jnp.sum(jnp.where(matches, jnp.arange(pairs, dtype=jnp.int32)[None, :], 0), axis=1)
    filled = jnp.any(matches, axis=1)
    return (placed, source, filled)


def orthogonal(matrix):
    summed = jnp.sqrt(jnp.sum(matrix * matrix))
    current = matrix / (summed + orth_epsilon)
    for repeat in range(5):
        square = lax.dot_general(
            current,
            current,
            (((1,), (1,)), ((), ())),
            precision=highest,
            preferred_element_type=jnp.float32,
        )
        power = jnp.dot(square, square, precision=highest, preferred_element_type=jnp.float32)
        mixer = second_coef * square + third_coef * power
        current = first_coef * current + jnp.dot(
            mixer, current, precision=highest, preferred_element_type=jnp.float32
        )
    return current


def advance(gradient, moment):
    current = momentum_decay * moment + (1.0 - momentum_decay) * gradient
    return (current, (1.0 - momentum_decay) * gradient + momentum_decay * current)


def expert_weights(upward, downward):
    return (
        lax.all_gather(upward, ("shard", "ctx"), axis=1, tiled=True),
        lax.all_gather(downward, ("shard", "ctx"), axis=1, tiled=True),
    )


def on_device(
    tokens,
    cotangent,
    routing,
    gating,
    inward,
    outward,
    scales,
    shifts,
    upward,
    downward,
    inward_moment,
    outward_moment,
    scales_moment,
    shifts_moment,
    upward_moment,
    downward_moment,
):
    rows_here = tokens.shape[1]
    features = tokens.shape[2]
    experts = upward.shape[0]
    top_count = routing.shape[2]
    capacity = 2 * top_count * rows_here // experts
    attn_scale = HEAD_DIM ** (-0.5)
    inputs = tokens[0].astype(jnp.float32)
    routes = routing[0]
    gate_pairs = gating[0].reshape(-1)
    zero_low = jnp.zeros((), jnp.bfloat16)
    full_in, full_out, all_scales, all_shifts = (
        lax.all_gather(inward, ("shard", "ctx", "tp"), axis=1, tiled=True),
        lax.all_gather(outward, ("shard", "ctx", "tp"), axis=0, tiled=True),
        lax.all_gather(scales, ("shard", "ctx", "tp"), axis=1, tiled=True),
        lax.all_gather(shifts, ("shard", "ctx", "tp"), axis=1, tiled=True),
    )
    factor = all_scales.astype(jnp.float32)
    offset = all_shifts.astype(jnp.float32)
    normed, unit_one, inverse_one = normalize(inputs, factor[0], offset[0])
    normed_low = normed.astype(jnp.bfloat16)
    projected = jnp.einsum(
        "td,kde->kte", normed_low, full_in, preferred_element_type=jnp.float32
    ).astype(jnp.bfloat16)
    head_rows = lax.all_to_all(projected, "ctx", split_axis=2, concat_axis=1, tiled=True)
    group_rows = head_rows.shape[1]
    head_width = head_rows.shape[2]
    seqs_here = group_rows // LEN
    shaped = head_rows.reshape(3, seqs_here, LEN, head_width // HEAD_DIM, HEAD_DIM)
    query_rows, key_rows, value_rows = (shaped[0], shaped[1], shaped[2])
    scores = (
        jnp.einsum("sqhd,skhd->shqk", query_rows, key_rows, preferred_element_type=jnp.float32)
        * attn_scale
    )
    top_score = jnp.max(scores, axis=-1, keepdims=True)
    logsum = top_score + jnp.log(jnp.sum(jnp.exp(scores - top_score), axis=-1, keepdims=True))
    soft_low = jnp.exp(scores - logsum).astype(jnp.bfloat16)
    blended = jnp.einsum(
        "shqk,skhd->sqhd", soft_low, value_rows, preferred_element_type=jnp.float32
    ).astype(jnp.bfloat16)
    blended_tokens = lax.all_to_all(
        blended.reshape(group_rows, head_width), "ctx", split_axis=0, concat_axis=1, tiled=True
    )
    residual = inputs + jnp.dot(blended_tokens, full_out, preferred_element_type=jnp.float32)
    second, unit_two, inverse_two = normalize(residual, factor[1], offset[1])
    second_low = second.astype(jnp.bfloat16)
    upstream = cotangent[0].astype(jnp.float32)
    placed, source, filled = slot_sources(routes, experts, capacity)
    slot_rows = jnp.where(filled[:, None], second_low[source // top_count], zero_low)
    slot_rows = slot_rows.reshape(experts, capacity, features)
    group_slots = lax.all_gather(slot_rows, "tp", axis=1, tiled=True)
    upper_full, lower_full = expert_weights(upward, downward)
    before = jnp.einsum("ecd,edf->ecf", group_slots, upper_full, preferred_element_type=jnp.float32)
    hidden = jax.nn.gelu(before).astype(jnp.bfloat16)
    partial_out = jnp.einsum("ecf,edf->ecd", hidden, lower_full, preferred_element_type=jnp.float32)
    own_out = lax.psum_scatter(
        partial_out.astype(jnp.bfloat16), "tp", scatter_dimension=1, tiled=True
    ).astype(jnp.float32)
    picked = own_out.reshape(experts * capacity, features)[placed].reshape(
        rows_here, top_count, features
    )
    mixture = jnp.sum(picked * gating[0][:, :, None], axis=1)
    result = (residual + mixture).astype(jnp.bfloat16)
    slot_grad = jnp.where(
        filled[:, None], upstream[source // top_count] * gate_pairs[source][:, None], 0.0
    )
    slot_grad = slot_grad.astype(jnp.bfloat16).reshape(experts, capacity, features)
    group_grad = lax.all_gather(slot_grad, "tp", axis=1, tiled=True)
    upper_full, lower_full = expert_weights(upward, downward)
    d_hidden = jnp.einsum(
        "ecd,edf->ecf", group_grad, lower_full, preferred_element_type=jnp.float32
    )
    unused, gelu_back = jax.vjp(jax.nn.gelu, before)
    d_before = gelu_back(d_hidden)[0].astype(jnp.bfloat16)
    lower_part = jnp.einsum("ecd,ecf->edf", group_grad, hidden, preferred_element_type=jnp.float32)
    upper_part = jnp.einsum(
        "ecd,ecf->edf", group_slots, d_before, preferred_element_type=jnp.float32
    )
    slot_input_part = jnp.einsum(
        "ecf,edf->ecd", d_before, upper_full, preferred_element_type=jnp.float32
    )
    slot_input = lax.psum_scatter(
        slot_input_part.astype(jnp.bfloat16), "tp", scatter_dimension=1, tiled=True
    ).astype(jnp.float32)
    d_second = jnp.sum(
        slot_input.reshape(experts * capacity, features)[placed].reshape(
            rows_here, top_count, features
        ),
        axis=1,
    )
    d_norm_two, scale_two, shift_two = normalize_back(d_second, unit_two, inverse_two, factor[1])
    d_residual = upstream + d_norm_two
    d_attended = d_residual.astype(jnp.bfloat16)
    outward_part = jnp.einsum(
        "td,te->de", blended_tokens, d_attended, preferred_element_type=jnp.float32
    )
    d_blended = jnp.einsum(
        "te,de->td", d_attended, full_out, preferred_element_type=jnp.float32
    ).astype(jnp.bfloat16)
    d_heads = lax.all_to_all(d_blended, "ctx", split_axis=1, concat_axis=0, tiled=True)
    d_heads = d_heads.reshape(seqs_here, LEN, head_width // HEAD_DIM, HEAD_DIM)
    soft_full = jnp.exp(
        jnp.einsum("sqhd,skhd->shqk", query_rows, key_rows, preferred_element_type=jnp.float32)
        * attn_scale
        - logsum
    )
    d_soft = jnp.einsum("sqhd,skhd->shqk", d_heads, value_rows, preferred_element_type=jnp.float32)
    value_grad = jnp.einsum(
        "shqk,sqhd->skhd", soft_low, d_heads, preferred_element_type=jnp.float32
    ).astype(jnp.bfloat16)
    row_inner = jnp.sum(soft_full * d_soft, axis=-1, keepdims=True)
    d_scores = (soft_full * (d_soft - row_inner)).astype(jnp.bfloat16)
    query_grad = (
        jnp.einsum("shqk,skhd->sqhd", d_scores, key_rows, preferred_element_type=jnp.float32)
        * attn_scale
    ).astype(jnp.bfloat16)
    key_grad = (
        jnp.einsum("shqk,sqhd->skhd", d_scores, query_rows, preferred_element_type=jnp.float32)
        * attn_scale
    ).astype(jnp.bfloat16)
    stacked_grad = jnp.stack([query_grad, key_grad, value_grad]).reshape(3, group_rows, head_width)
    token_grad = lax.all_to_all(stacked_grad, "ctx", split_axis=1, concat_axis=2, tiled=True)
    inward_part = jnp.einsum(
        "td,kte->kde", normed_low, token_grad, preferred_element_type=jnp.float32
    )
    d_normed = jnp.einsum("kte,kde->td", token_grad, full_in, preferred_element_type=jnp.float32)
    d_norm_one, scale_one, shift_one = normalize_back(d_normed, unit_one, inverse_one, factor[0])
    input_grad = d_residual + d_norm_one
    inward_grad, outward_grad, scales_grad, shifts_grad = (
        lax.psum_scatter(inward_part, ("shard", "ctx", "tp"), scatter_dimension=1, tiled=True),
        lax.psum_scatter(outward_part, ("shard", "ctx", "tp"), scatter_dimension=0, tiled=True),
        lax.psum_scatter(
            jnp.stack([scale_one, scale_two]),
            ("shard", "ctx", "tp"),
            scatter_dimension=1,
            tiled=True,
        ),
        lax.psum_scatter(
            jnp.stack([shift_one, shift_two]),
            ("shard", "ctx", "tp"),
            scatter_dimension=1,
            tiled=True,
        ),
    )
    upward_grad, downward_grad = (
        lax.psum_scatter(
            upper_part.astype(jnp.bfloat16), ("shard", "ctx"), scatter_dimension=1, tiled=True
        ).astype(jnp.float32),
        lax.psum_scatter(
            lower_part.astype(jnp.bfloat16), ("shard", "ctx"), scatter_dimension=1, tiled=True
        ).astype(jnp.float32),
    )
    inward_state, inward_push = advance(inward_grad, inward_moment)
    outward_state, outward_push = advance(outward_grad, outward_moment)
    scales_state, scales_push = advance(scales_grad, scales_moment)
    shifts_state, shifts_push = advance(shifts_grad, shifts_moment)
    upward_state, upward_push = advance(upward_grad, upward_moment)
    downward_state, downward_push = advance(downward_grad, downward_moment)
    devices = lax.axis_size(("shard", "ctx", "tp"))
    outer_count = lax.axis_size(("shard", "ctx"))
    inner_count = lax.axis_size("tp")
    rows_local = upward.shape[1]
    cols_local = upward.shape[2]
    slot_size = rows_local * cols_local
    attention_size = inward.shape[1] * features
    full_cols = inner_count * cols_local

    def flat_pad(portion):
        flatten = portion.reshape(portion.shape[0], -1)
        return jnp.pad(flatten, ((0, 0), (0, slot_size - flatten.shape[1])))

    matrices = jnp.concatenate(
        [
            flat_pad(inward_push),
            flat_pad(outward_push[None]),
            upward_push.reshape(experts, slot_size),
            downward_push.reshape(experts, slot_size),
        ]
    )
    matrix_count = matrices.shape[0]
    owner_table = np.arange(matrix_count) * devices // matrix_count
    outgoing = jnp.zeros((devices, slot_size), jnp.float32).at[owner_table].set(matrices)
    received = lax.all_to_all(
        outgoing.astype(jnp.bfloat16),
        ("shard", "ctx", "tp"),
        split_axis=0,
        concat_axis=0,
        tiled=True,
    ).astype(outgoing.dtype)
    myself = lax.axis_index(("shard", "ctx", "tp"))
    owned = (
        jnp.sum(
            jnp.where(
                jnp.asarray(owner_table, dtype=jnp.int32) == myself,
                jnp.arange(matrix_count, dtype=jnp.int32) + 1,
                0,
            )
        )
        - 1
    )
    attention_kind = jnp.logical_and(owned >= 0, owned < 4)
    expert_form = (
        received.reshape(outer_count, inner_count, rows_local, cols_local)
        .transpose(0, 2, 1, 3)
        .reshape(features, full_cols)
    )
    attention_form = jnp.pad(
        received[:, :attention_size].reshape(features, features),
        ((0, 0), (0, full_cols - features)),
    )
    orthogonal_form = orthogonal(jnp.where(attention_kind, attention_form, expert_form))
    back_expert = (
        orthogonal_form.reshape(outer_count, rows_local, inner_count, cols_local)
        .transpose(0, 2, 1, 3)
        .reshape(devices, slot_size)
    )
    back_attention = jnp.pad(
        orthogonal_form[:, :features].reshape(devices, attention_size),
        ((0, 0), (0, slot_size - attention_size)),
    )
    returned = lax.all_to_all(
        jnp.where(attention_kind, back_attention, back_expert).astype(jnp.bfloat16),
        ("shard", "ctx", "tp"),
        split_axis=0,
        concat_axis=0,
        tiled=True,
    ).astype(jnp.float32)
    mine_parts = returned[owner_table]
    inward_new = inward.astype(jnp.float32) - mine_parts[:3, :attention_size].reshape(inward.shape)
    outward_new = outward.astype(jnp.float32) - mine_parts[3, :attention_size].reshape(
        outward.shape
    )
    upward_new = upward.astype(jnp.float32) - 2.0 * mine_parts[4 : 4 + experts].reshape(
        upward.shape
    )
    downward_new = downward.astype(jnp.float32) - mine_parts[4 + experts :].reshape(downward.shape)
    total_tokens = lax.axis_size("shard") * lax.axis_size("ctx") * lax.axis_size("tp") * rows_here
    vector_rate = 0.6 / math.sqrt(total_tokens)
    scales_new = scales.astype(jnp.float32) - vector_rate * scales_push
    shifts_new = shifts.astype(jnp.float32) - vector_rate * shifts_push
    return (
        result[None],
        input_grad[None],
        inward_grad,
        outward_grad,
        scales_grad,
        shifts_grad,
        upward_grad,
        downward_grad,
        inward_state,
        outward_state,
        scales_state,
        shifts_state,
        upward_state,
        downward_state,
        inward_new,
        outward_new,
        scales_new,
        shifts_new,
        upward_new,
        downward_new,
    )


axes = ("shard", "ctx", "tp")
TILE = 256
SPAN = 208
VMEM_ASK = 60 * 1024 * 1024


def dot_nn(left, right):
    return lax.dot_general(
        left, right, (((1,), (0,)), ((), ())), preferred_element_type=jnp.float32
    )


def dot_nt(left, right):
    return lax.dot_general(
        left, right, (((1,), (1,)), ((), ())), preferred_element_type=jnp.float32
    )


def dot_tn(left, right):
    return lax.dot_general(
        left, right, (((0,), (0,)), ((), ())), preferred_element_type=jnp.float32
    )


def tile_pairs(count):
    return [(row, col) for row in range(count) for col in range(row, count)]


def wide_bands(size):
    return [pl.ds(start, TILE) for start in range(0, size, TILE)]


def wide_steps(count, gram, whole, low, whole_low, mixer):
    bands = wide_bands(gram.shape[0])

    def step(repeat, carry):
        wide_mix(gram, whole, low, whole_low, mixer)
        for band in bands:
            half = first_coef * gram[band, :] + dot_nn(mixer[band, :], low[...])
            gram[band, :] = first_coef * half + dot_nn(half.astype(jnp.bfloat16), mixer[...])
            whole[band, :] = first_coef * whole[band, :] + dot_nn(mixer[band, :], whole_low[...])
        return carry

    lax.fori_loop(0, count, step, 0)


def wide_mix(gram, whole, low, whole_low, mixer):
    low[...] = gram[...].astype(jnp.bfloat16)
    whole_low[...] = whole[...].astype(jnp.bfloat16)
    for band in wide_bands(gram.shape[0]):
        squared = dot_nn(low[band, :], low[...])
        mixer[band, :] = (second_coef * gram[band, :] + third_coef * squared).astype(jnp.bfloat16)


def wide_first_kernel(block0, block1, block3, part0, part1, part2, gram, whole, low, mixer, whole_low, block2):
    size = gram.shape[0]
    bands = wide_bands(size)
    rows = lax.broadcasted_iota(jnp.int32, (TILE, size), 0)
    cols = lax.broadcasted_iota(jnp.int32, (TILE, size), 1)
    for part, band in zip((part0, part1, part2), bands):
        block2[band, :] = part[...]
    trace = 0.0
    for place, band in enumerate(bands):
        part = dot_nt(block0[band, :], block0[...])
        for block in (block1, block2, block3):
            part = part + dot_nt(block[band, :], block[...])
        gram[band, :] = part
        trace = trace + jnp.sum(jnp.where(rows + place * TILE == cols, part, 0.0))
    factor = 1.0 / (jnp.sqrt(trace) + orth_epsilon)
    for place, band in enumerate(bands):
        gram[band, :] = gram[band, :] * (factor * factor)
        whole[band, :] = jnp.where(rows + place * TILE == cols, factor, 0.0)
    wide_steps(2, gram, whole, low, whole_low, mixer)


def wide_last_kernel(gram_in, whole_in, out, gram, whole, low, mixer, whole_low):
    bands = wide_bands(gram.shape[0])
    gram[...] = gram_in[...]
    whole[...] = whole_in[...]
    wide_steps(2, gram, whole, low, whole_low, mixer)
    wide_mix(gram, whole, low, whole_low, mixer)
    for row, band in enumerate(bands):
        last = first_coef * whole[band, :] + dot_nn(mixer[band, :], whole_low[...])
        for place, pair in enumerate(tile_pairs(len(bands))):
            if pair[0] == row:
                out[place] = last[:, pair[1] * TILE : (pair[1] + 1) * TILE].astype(out.dtype)


def wide_call(kernel, size, out_shape, kept, scratch, name, inputs):
    vmem = pl.BlockSpec(memory_space=pltpu.VMEM)
    square = (size, size)
    return pl.pallas_call(
        kernel,
        out_shape=out_shape,
        in_specs=[vmem] * len(inputs),
        out_specs=jax.tree.map(lambda shape: vmem, out_shape),
        scratch_shapes=[pltpu.VMEM(square, jnp.float32)] * kept
        + [pltpu.VMEM(square, jnp.bfloat16)] * scratch,
        compiler_params=pltpu.CompilerParams(vmem_limit_bytes=VMEM_ASK),
        cost_estimate=pl.CostEstimate(
            flops=20 * size**3, bytes_accessed=8 * size * size, transcendentals=0
        ),
        name=name,
    )(*inputs)


def wide_first(blocks):
    size = blocks[0].shape[0]
    shape = jax.ShapeDtypeStruct((size, size), jnp.float32)
    return wide_call(wide_first_kernel, size, [shape, shape], 0, 4, "wide_first", blocks)


def wide_last(gram, whole):
    size = gram.shape[0]
    pairs = len(tile_pairs(size // TILE))
    shape = jax.ShapeDtypeStruct((pairs, TILE, TILE), jnp.bfloat16)
    return wide_call(wide_last_kernel, size, shape, 2, 3, "wide_last", (gram, whole))


def store_rows(chip, value, outs, which):
    depth = outs[0].shape[2]
    for turn, out in enumerate(outs):
        other = jnp.bitwise_xor(chip, turn)
        for core in range(2):
            row = ((other // 2) * 2 + core) * 2 + other % 2
            out[which, core] = value[pl.ds(pl.multiple_of(row * depth, 16), depth), :].astype(
                out.dtype
            )


def apply_kernel(place, *refs):
    mixers, pushes, outs, (full, moved) = refs[:4], refs[4:6], refs[6:10], refs[10:]
    chip, core, tp = place[0], place[1], place[2]
    count = full.shape[0] // TILE
    for which in range(2):
        source = lax.rem(tp - 2 * core - which + 4, 4)
        for step in range(4):

            @pl.when(source == step)
            def _():
                for spot, (row, col) in enumerate(tile_pairs(count)):
                    tile = mixers[step][spot]
                    full[pl.ds(row * TILE, TILE), pl.ds(col * TILE, TILE)] = tile
                    if row != col:
                        full[pl.ds(col * TILE, TILE), pl.ds(row * TILE, TILE)] = tile.T

        for spot in range(2):

            @pl.when(lax.rem(tp + spot, 2) == which)
            def _():
                moved[...] = dot_nn(full[...], pushes[spot][...])

        store_rows(chip, moved, outs, which)


def apply_mixers(place, mixers, pushes, depth):
    size, width = pushes[0].shape
    vmem = pl.BlockSpec(memory_space=pltpu.VMEM)
    shape = jax.ShapeDtypeStruct((2, 2, depth, width), jnp.bfloat16)
    return pl.pallas_call(
        apply_kernel,
        in_specs=[pl.BlockSpec(memory_space=pltpu.SMEM)] + [vmem] * 6,
        out_specs=[vmem] * 4,
        out_shape=[shape] * 4,
        scratch_shapes=[
            pltpu.VMEM((size, size), jnp.bfloat16),
            pltpu.VMEM((size, width), jnp.float32),
        ],
        compiler_params=pltpu.CompilerParams(vmem_limit_bytes=VMEM_ASK),
        cost_estimate=pl.CostEstimate(
            flops=4 * size**3, bytes_accessed=10 * size * size, transcendentals=0
        ),
        name="apply_mixers",
    )(place, *mixers, *pushes)


def push_kernel(place, own, *refs):
    gots, moments, refs = refs[:2], refs[2:6], refs[6:]
    pushes, bands, outs, (total,) = refs[:2], refs[2:5], refs[5:9], refs[9:]
    chip, core, tp = place[0], place[1], place[2]
    keep = 1.0 - momentum_decay
    depth = outs[0].shape[2]
    for which in range(2):
        total[...] = (
            own[which].astype(jnp.float32)
            + gots[0][which].astype(jnp.float32)
            + gots[1][which].astype(jnp.float32)
        )
        store_rows(chip, total, outs, which)
        for turn, moment in enumerate(moments):
            other = jnp.bitwise_xor(chip, turn)
            for side in range(2):
                row = ((other // 2) * 2 + jnp.bitwise_xor(core, side)) * 2 + other % 2
                rows = pl.ds(pl.multiple_of(row * depth, 16), depth)
                pushed = (
                    (keep + momentum_decay * keep) * total[rows, :]
                    + momentum_decay * momentum_decay * moment[2 * which + side].astype(jnp.float32)
                ).astype(jnp.bfloat16)
                for spot in range(2):

                    @pl.when(lax.rem(tp + spot, 2) == which)
                    def _():
                        pushes[spot][rows, :] = pushed

    for place, band in enumerate(bands):
        band[...] = pushes[0][pl.ds(place * TILE, TILE), :]


def push_rows(place, own, gots, moments):
    size, width = own.shape[1:]
    depth = moments[0].shape[1]
    vmem = pl.BlockSpec(memory_space=pltpu.VMEM)
    rows = jax.ShapeDtypeStruct((2, 2, depth, width), jnp.bfloat16)
    return pl.pallas_call(
        push_kernel,
        in_specs=[pl.BlockSpec(memory_space=pltpu.SMEM)] + [vmem] * 7,
        out_specs=[vmem] * 9,
        out_shape=[jax.ShapeDtypeStruct((size, width), jnp.bfloat16)] * 2
        + [jax.ShapeDtypeStruct((TILE, width), jnp.bfloat16)] * 3
        + [rows] * 4,
        scratch_shapes=[pltpu.VMEM((size, width), jnp.float32)],
        compiler_params=pltpu.CompilerParams(vmem_limit_bytes=VMEM_ASK),
        cost_estimate=pl.CostEstimate(
            flops=20 * size * width, bytes_accessed=24 * size * width, transcendentals=0
        ),
        name="push_rows",
    )(place, own, *gots, *moments)


def square_kernel(matrix, out, current, low, square, square_low, mixer):
    size = current.shape[0]
    bands = [pl.ds(start, TILE) for start in range(0, size, TILE)]
    total = 0.0
    for band in bands:
        part = matrix[band, :].astype(jnp.float32)
        total = total + jnp.sum(part * part)
    factor = 1.0 / (jnp.sqrt(total) + orth_epsilon)
    for band in bands:
        current[band, :] = matrix[band, :].astype(jnp.float32) * factor

    def step(repeat, carry):
        low[...] = current[...].astype(jnp.bfloat16)
        for band in bands:
            part = dot_nt(low[band, :], low[...])
            square[band, :] = part
            square_low[band, :] = part.astype(jnp.bfloat16)
        for band in bands:
            mixed = second_coef * square[band, :] + third_coef * dot_nn(
                square_low[band, :], square_low[...]
            )
            mixer[band, :] = mixed.astype(jnp.bfloat16)
        for band in bands:
            current[band, :] = first_coef * current[band, :] + dot_nn(mixer[band, :], low[...])
        return carry

    lax.fori_loop(0, 5, step, 0)
    out[...] = current[...].astype(out.dtype)


def orthogonal_square(matrix):
    size = matrix.shape[0]
    return pl.pallas_call(
        square_kernel,
        out_shape=jax.ShapeDtypeStruct((size, size), jnp.bfloat16),
        in_specs=[pl.BlockSpec(memory_space=pltpu.VMEM)],
        out_specs=pl.BlockSpec(memory_space=pltpu.VMEM),
        scratch_shapes=[
            pltpu.VMEM((size, size), jnp.float32),
            pltpu.VMEM((size, size), jnp.bfloat16),
            pltpu.VMEM((size, size), jnp.float32),
            pltpu.VMEM((size, size), jnp.bfloat16),
            pltpu.VMEM((size, size), jnp.bfloat16),
        ],
        compiler_params=pltpu.CompilerParams(vmem_limit_bytes=VMEM_ASK),
        cost_estimate=pl.CostEstimate(
            flops=30 * size**3, bytes_accessed=4 * matrix.size, transcendentals=0
        ),
        name="square_orthogonal",
    )(matrix)


root = math.sqrt(2.0 / math.pi)


def gelu_pair(value):
    squared = value * value
    part = 0.5 * jnp.tanh(value * (root + (root * 0.044715) * squared)) + 0.5
    bend = value * (2.0 * root + (6.0 * root * 0.044715) * squared)
    return value * part, part + part * (1.0 - part) * bend


def one_hot(rank):
    return lax.broadcasted_iota(jnp.int32, (SPAN, rank.shape[1]), 0) == rank


def assemble(chip, core, pieces, whole):
    depth = pieces[0].shape[1]
    for place, piece in enumerate(pieces):
        other = jnp.bitwise_xor(chip, place // 2)
        row = ((other // 2) * 2 + jnp.bitwise_xor(core, place % 2)) * 2 + other % 2
        whole[pl.ds(pl.multiple_of(row * depth, 16), depth), :] = piece[0]


def each_band(count, work):
    wide = (count + 127) // 512

    def step(place, carry):
        work(pl.ds(pl.multiple_of(place * 512, 512), 512))
        return carry

    lax.fori_loop(0, wide, step, 0)
    rest = count - wide * 512
    start = wide * 512

    @pl.when(rest > 128)
    def _():
        work(pl.ds(pl.multiple_of(start, 512), 256))

    @pl.when(jnp.logical_or(rest > 256, jnp.logical_and(rest > 0, rest <= 128)))
    def _():
        work(pl.ds(pl.multiple_of(start + jnp.where(rest > 256, 256, 0), 128), 128))


def gate_of(hot, gate):
    return jnp.sum(jnp.where(hot, gate, 0.0), axis=1, keepdims=True)


def experts_kernel(
    starts, rank, gate, *refs
):
    blocks = rank.shape[1]
    ups, downs, refs = refs[:8], refs[8:16], refs[16:]
    tokens_hbm, refs = refs[: 2 * blocks], refs[2 * blocks :]
    hidden_out, before_out, *refs = refs
    outs, refs = refs[:5], refs[5:]
    rows, cots, upper, lower, slots, grads, upper_sum, lower_sum, leaving, sems, out_sems = refs
    targets = [(outs[turn].at[0], outs[turn].at[1]) for turn in range(3)] + [(outs[3], outs[4])]
    expert = pl.program_id(0)
    base = expert * (blocks + 1)
    chip = starts[pl.num_programs(0) * (blocks + 1)]
    core = starts[pl.num_programs(0) * (blocks + 1) + 1]
    low = jnp.bfloat16

    @pl.when(expert == 0)
    def _():
        copies = []
        for block in range(blocks):
            for which, held in enumerate((rows, cots)):
                place = which * blocks + block
                copies.append(
                    pltpu.make_async_copy(tokens_hbm[place], held.at[block], sems.at[place])
                )
        for copy in copies:
            copy.start()

    assemble(chip, core, ups, upper)
    assemble(chip, core, downs, lower)

    for block in range(blocks):

        @pl.when(expert == 0)
        def _():
            for which, held in enumerate((rows, cots)):
                place = which * blocks + block
                pltpu.make_async_copy(tokens_hbm[place], held.at[block], sems.at[place]).wait()

        start = pl.multiple_of(starts[base + block], 16)
        hot = one_hot(rank[0, block : block + 1, :])
        spread = jnp.where(hot, 1.0, 0.0).astype(low)
        weight = gate_of(hot, gate[0, block : block + 1, :])
        slots[pl.ds(start, SPAN), :] = dot_nn(spread, rows[block]).astype(low)
        grads[pl.ds(start, SPAN), :] = (dot_nn(spread, cots[block]) * weight).astype(low)

    end = pl.multiple_of(starts[base + blocks], 16)
    slots[pl.ds(end, TILE), :] = jnp.zeros((TILE, slots.shape[1]), low)
    grads[pl.ds(end, TILE), :] = jnp.zeros((TILE, slots.shape[1]), low)
    upper_sum[...] = jnp.zeros_like(upper_sum)
    lower_sum[...] = jnp.zeros_like(lower_sum)

    def work(band):
        slot_rows, slot_grads = slots[band, :], grads[band, :]
        hidden, slope = gelu_pair(dot_nn(slot_rows, upper[...]))
        hidden = hidden.astype(low)
        d_before = (dot_nn(slot_grads, lower[...]) * slope).astype(low)
        hidden_out[0, band, :] = hidden
        before_out[0, band, :] = d_before
        upper_sum[...] += dot_tn(slot_rows, d_before)
        lower_sum[...] += dot_tn(slot_grads, hidden)

    each_band(starts[base + blocks], work)

    for turn, target in enumerate(targets):

        @pl.when(expert == turn)
        def _():
            if turn > 0:
                for which in range(2):
                    pltpu.make_async_copy(
                        leaving.at[which], targets[turn - 1][which], out_sems.at[2 * turn - 2 + which]
                    ).wait()
            leaving[0] = upper_sum[...].astype(low)
            leaving[1] = lower_sum[...].astype(low)
            copies = [
                pltpu.make_async_copy(leaving.at[which], target[which], out_sems.at[2 * turn + which])
                for which in range(2)
            ]
            for copy in copies:
                copy.start()
            if turn == 3:
                for copy in copies:
                    copy.wait()


def tokens_kernel(
    gated, starts, rank, gate, acts, *refs
):
    pieces, (part_own, part_other, whole, moved, spread, found) = refs[:8], refs[8:]
    expert = pl.program_id(0)
    count, blocks = rank.shape[0], rank.shape[1]
    base = expert * (blocks + 1)
    chip, core = starts[count * (blocks + 1)], starts[count * (blocks + 1) + 1]
    low = jnp.bfloat16

    @pl.when(expert == 0)
    def _():
        moved[...] = jnp.zeros_like(moved)

    assemble(chip, core, pieces, whole)

    def work(band):
        moved[expert, band, :] = dot_nt(acts[0, band, :], whole[...]).astype(low)

    each_band(starts[base + blocks], work)

    @pl.when(expert == count - 1)
    def _():
        for side, part in enumerate((part_own, part_other)):
            for place in range(blocks // 2):
                block = side * (blocks // 2) + place
                ways, rows_of = spread.at[place % 2], found.at[place % 2]
                for each in range(count):
                    start = pl.multiple_of(starts[each * (blocks + 1) + block], 16)
                    hot = one_hot(rank[each, block : block + 1, :])
                    rows = moved[each, pl.ds(start, SPAN), :]
                    if gated:
                        weight = gate_of(hot, gate[each, block : block + 1, :])
                        rows = (rows.astype(jnp.float32) * weight).astype(low)
                    band = pl.ds(each * SPAN, SPAN)
                    ways[band, :] = jnp.where(hot, 1.0, 0.0).astype(low)
                    rows_of[band, :] = rows
                part[place] = dot_tn(ways[...], rows_of[...]).astype(low)


def pass_shapes(rank, pieces):
    count = pieces[0].shape[0]
    blocks, padded = rank.shape[1], rank.shape[2]
    tiles = -(-blocks * SPAN // TILE)

    def of_expert(expert, starts):
        return (expert, 0, 0)

    piece_specs = [
        pl.BlockSpec(
            (1,) + pieces[0].shape[1:],
            lambda expert, starts, turn=place // 2: (jnp.bitwise_xor(expert, turn), 0, 0),
        )
        for place in range(8)
    ]
    return count, blocks, padded, tiles, of_expert, piece_specs


def experts_pass(starts, rank, gate, rows, cots, ups, downs):
    count, blocks, padded, tiles, of_expert, piece_specs = pass_shapes(rank, ups)
    features = rows[0].shape[1]
    width = ups[0].shape[2]
    most = blocks * SPAN
    low = jnp.bfloat16
    vectors = pl.BlockSpec((1, blocks, padded), of_expert)
    acts = pl.BlockSpec((1, tiles * TILE, width), of_expert)
    acts_shape = jax.ShapeDtypeStruct((count, tiles * TILE, width), low)
    grad_shape = jax.ShapeDtypeStruct((features, width), low)
    pair_shape = jax.ShapeDtypeStruct((2, features, width), low)
    return pl.pallas_call(
        experts_kernel,
        grid_spec=pltpu.PrefetchScalarGridSpec(
            num_scalar_prefetch=1,
            grid=(count,),
            in_specs=[vectors, vectors]
            + piece_specs * 2
            + [pl.BlockSpec(memory_space=pl.ANY)] * (2 * blocks),
            out_specs=[acts, acts] + [pl.BlockSpec(memory_space=pl.ANY)] * 5,
            scratch_shapes=[
                pltpu.VMEM((blocks, padded, features), low),
                pltpu.VMEM((blocks, padded, features), low),
                pltpu.VMEM((features, width), low),
                pltpu.VMEM((features, width), low),
                pltpu.VMEM((most + TILE, features), low),
                pltpu.VMEM((most + TILE, features), low),
                pltpu.VMEM((features, width), jnp.float32),
                pltpu.VMEM((features, width), jnp.float32),
                pltpu.VMEM((2, features, width), low),
                pltpu.SemaphoreType.DMA((2 * blocks,)),
                pltpu.SemaphoreType.DMA((8,)),
            ],
        ),
        out_shape=[acts_shape, acts_shape] + [pair_shape] * 3 + [grad_shape] * 2,
        compiler_params=pltpu.CompilerParams(vmem_limit_bytes=VMEM_ASK),
        cost_estimate=pl.CostEstimate(
            flops=4 * count * most * features * width,
            bytes_accessed=60 * 1024 * 1024,
            transcendentals=count * most * width,
        ),
        name="experts_pass",
    )(starts, rank, gate, *ups, *downs, *rows, *cots)


def tokens_pass(starts, rank, gate, acts, pieces, gated):
    count, blocks, padded, tiles, of_expert, piece_specs = pass_shapes(rank, pieces)
    width = pieces[0].shape[2]
    features = 8 * pieces[0].shape[1]
    most = blocks * SPAN
    low = jnp.bfloat16
    vectors = pl.BlockSpec(rank.shape, lambda expert, starts: (0, 0, 0))
    parts = pl.BlockSpec((blocks // 2, padded, features), lambda expert, starts: (0, 0, 0))
    part_shape = jax.ShapeDtypeStruct((blocks // 2, padded, features), low)
    return pl.pallas_call(
        functools.partial(tokens_kernel, gated),
        grid_spec=pltpu.PrefetchScalarGridSpec(
            num_scalar_prefetch=1,
            grid=(count,),
            in_specs=[vectors, vectors, pl.BlockSpec((1,) + acts.shape[1:], of_expert)]
            + piece_specs,
            out_specs=[parts, parts],
            scratch_shapes=[
                pltpu.VMEM((features, width), low),
                pltpu.VMEM((count, most + TILE, features), low),
                pltpu.VMEM((2, count * SPAN, padded), low),
                pltpu.VMEM((2, count * SPAN, features), low),
            ],
        ),
        out_shape=[part_shape, part_shape],
        compiler_params=pltpu.CompilerParams(vmem_limit_bytes=VMEM_ASK),
        cost_estimate=pl.CostEstimate(
            flops=2 * count * most * features * width,
            bytes_accessed=30 * 1024 * 1024,
            transcendentals=0,
        ),
        name="tokens_gated" if gated else "tokens_plain",
    )(starts, rank, gate, acts, *pieces)


IMAGE = 208


def row_norm(values, factor, offset):
    width = values.shape[1]
    average = jnp.sum(values, axis=1, keepdims=True) / width
    centred = values - average
    spread = jnp.sum(centred * centred, axis=1, keepdims=True) / width
    inverse = lax.rsqrt(spread + norm_epsilon)
    unit = centred * inverse
    return unit * factor + offset, unit, inverse


def row_norm_back(gradient, unit, inverse, factor):
    width = gradient.shape[1]
    inner = gradient * factor
    average = jnp.sum(inner, axis=1, keepdims=True) / width
    along = jnp.sum(inner * unit, axis=1, keepdims=True) / width
    return inverse * (inner - average - unit * along)


def head_soft(query, key, here, keys_used):
    own = jnp.where(here, query, jnp.zeros_like(query))
    scores = dot_nt(own, key) * (HEAD_DIM ** (-0.5))
    scores = jnp.where(keys_used, scores, -1e30)
    powers = jnp.exp(scores - jnp.max(scores, axis=1, keepdims=True))
    return powers / jnp.sum(powers, axis=1, keepdims=True)


def forward_kernel(
    place, tokens, norms, w0, w1, w2, w3, others_near, others_far,
    normed_out, qkv_out, blended_out, residual_out, second_out, weights,
):
    features = tokens.shape[1]
    low = jnp.bfloat16

    chip, core = place[0], place[1]
    depth = features // 8
    others = (others_near.at[0], others_near.at[1], others_far.at[0], others_far.at[1])
    for side, pieces in enumerate(((w0, w1, w2, w3), others)):
        for turn, piece in enumerate(pieces):
            other = jnp.bitwise_xor(chip, turn)
            row = ((other // 2) * 2 + jnp.bitwise_xor(core, side)) * 2 + other % 2
            rows = pl.ds(pl.multiple_of(row * depth, 16), depth)
            for which in range(4):
                weights[which, rows, :] = piece[which]

    normed, unused, unused = row_norm(
        tokens[...].astype(jnp.float32), norms[0:1, :], norms[2:3, :]
    )
    normed_out[...] = normed.astype(low)
    for which in range(3):
        qkv_out[which] = dot_nn(normed_out[...], weights[which]).astype(low)
    keys_used = lax.broadcasted_iota(jnp.int32, (IMAGE, IMAGE), 1) < LEN
    first = lax.broadcasted_iota(jnp.int32, (IMAGE, 2 * HEAD_DIM), 1) < HEAD_DIM

    def attend(image, carry):
        rows = pl.ds(pl.multiple_of(image * IMAGE, 16), IMAGE)
        for start in range(0, features, 2 * HEAD_DIM):
            cols = pl.ds(start, 2 * HEAD_DIM)
            query, key, value = (qkv_out[which, rows, cols] for which in range(3))
            mixed = []
            for here in (first, jnp.logical_not(first)):
                soft = head_soft(query, key, here, keys_used).astype(low)
                mixed.append(dot_nn(soft, value))
            blended_out[rows, cols] = jnp.where(first, mixed[0], mixed[1]).astype(low)
        return carry

    lax.fori_loop(0, tokens.shape[0] // IMAGE, attend, 0)
    residual = tokens[...].astype(jnp.float32) + dot_nn(blended_out[...], weights[3])
    residual_out[...] = residual
    second, unused, unused = row_norm(residual, norms[1:2, :], norms[3:4, :])
    second_out[...] = second.astype(low)


def attention_forward(place, tokens, norms, pieces, others):
    rows, features = tokens.shape
    low = jnp.bfloat16
    vmem = pl.BlockSpec(memory_space=pltpu.VMEM)
    shape = jax.ShapeDtypeStruct((rows, features), low)
    return pl.pallas_call(
        forward_kernel,
        in_specs=[pl.BlockSpec(memory_space=pltpu.SMEM)] + [vmem] * 8,
        out_specs=[vmem] * 6,
        out_shape=[
            shape,
            jax.ShapeDtypeStruct((3, rows, features), low),
            shape,
            jax.ShapeDtypeStruct((rows, features), jnp.float32),
            shape,
            jax.ShapeDtypeStruct((4, features, features), low),
        ],
        compiler_params=pltpu.CompilerParams(vmem_limit_bytes=VMEM_ASK),
        cost_estimate=pl.CostEstimate(
            flops=10 * rows * features * features,
            bytes_accessed=16 * 1024 * 1024,
            transcendentals=0,
        ),
        name="attention_forward",
    )(place, tokens, norms, *pieces, *others)


def backward_kernel(
    place, tokens, cots, residual, blended, normed, qkv, weights, norms,
    second0, second1, second2, second3,
    input_grad, mine, theirs, vectors,
    part, d_heads, d_qkv, d_sum,
):
    rows_all, features = tokens.shape
    low = jnp.bfloat16
    core = place[1]

    def store_part(which, value):
        part[...] = value
        slab = mine.shape[2]
        for side in range(2):
            own = pl.ds(pl.multiple_of((2 * side + core) * slab, slab), slab)
            other = pl.ds(pl.multiple_of((2 * side + 1 - core) * slab, slab), slab)
            mine[which, side] = part[own, :].astype(low)
            theirs[which, side] = part[other, :].astype(low)

    d_second = second0[...].astype(jnp.float32)
    for piece in (second1, second2, second3):
        d_second = d_second + piece[...].astype(jnp.float32)
    unused, unit, inverse = row_norm(residual[...], norms[1:2, :], norms[3:4, :])
    vectors[...] = jnp.zeros_like(vectors)
    vectors[1:2, :] = jnp.sum(d_second * unit, axis=0, keepdims=True)
    vectors[3:4, :] = jnp.sum(d_second, axis=0, keepdims=True)
    d_sum[...] = cots[...].astype(jnp.float32) + row_norm_back(
        d_second, unit, inverse, norms[1:2, :]
    )
    d_attended = d_sum[...].astype(low)
    d_heads[...] = dot_nt(d_attended, weights[3]).astype(low)
    store_part(3, dot_tn(blended[...], d_attended))

    keys_used = lax.broadcasted_iota(jnp.int32, (IMAGE, IMAGE), 1) < LEN
    first = lax.broadcasted_iota(jnp.int32, (IMAGE, 2 * HEAD_DIM), 1) < HEAD_DIM
    scale = HEAD_DIM ** (-0.5)

    def attend(image, carry):
        rows = pl.ds(pl.multiple_of(image * IMAGE, 16), IMAGE)
        for start in range(0, features, 2 * HEAD_DIM):
            cols = pl.ds(start, 2 * HEAD_DIM)
            query, key, value = (qkv[which, rows, cols] for which in range(3))
            upper = d_heads[rows, cols]
            found = []
            for here in (first, jnp.logical_not(first)):
                soft = head_soft(query, key, here, keys_used)
                d_soft = dot_nt(jnp.where(here, upper, jnp.zeros_like(upper)), value)
                inner = jnp.sum(soft * d_soft, axis=1, keepdims=True)
                d_scores = (soft * (d_soft - inner)).astype(low)
                found.append(
                    (
                        dot_nn(d_scores, key) * scale,
                        dot_tn(d_scores, query) * scale,
                        dot_tn(soft.astype(low), upper),
                    )
                )
            for which in range(3):
                d_qkv[which, rows, cols] = jnp.where(
                    first, found[0][which], found[1][which]
                ).astype(low)
        return carry

    lax.fori_loop(0, rows_all // IMAGE, attend, 0)
    d_normed = dot_nt(d_qkv[0], weights[0])
    for which in range(1, 3):
        d_normed = d_normed + dot_nt(d_qkv[which], weights[which])
    for which in range(3):
        store_part(which, dot_tn(normed[...], d_qkv[which]))
    unused, unit, inverse = row_norm(
        tokens[...].astype(jnp.float32), norms[0:1, :], norms[2:3, :]
    )
    vectors[0:1, :] = jnp.sum(d_normed * unit, axis=0, keepdims=True)
    vectors[2:3, :] = jnp.sum(d_normed, axis=0, keepdims=True)
    input_grad[...] = d_sum[...] + row_norm_back(d_normed, unit, inverse, norms[0:1, :])


def attention_backward(place, tokens, cots, residual, blended, normed, qkv, seconds, weights, norms):
    rows, features = tokens.shape
    low = jnp.bfloat16
    vmem = pl.BlockSpec(memory_space=pltpu.VMEM)
    half_shape = jax.ShapeDtypeStruct((4, 2, features // 4, features), low)
    return pl.pallas_call(
        backward_kernel,
        in_specs=[pl.BlockSpec(memory_space=pltpu.SMEM)] + [vmem] * 12,
        out_specs=[vmem] * 4,
        scratch_shapes=[
            pltpu.VMEM((features, features), jnp.float32),
            pltpu.VMEM((rows, features), low),
            pltpu.VMEM((3, rows, features), low),
            pltpu.VMEM((rows, features), jnp.float32),
        ],
        out_shape=[
            jax.ShapeDtypeStruct((rows, features), jnp.float32),
            half_shape,
            half_shape,
            jax.ShapeDtypeStruct((8, features), jnp.float32),
        ],
        compiler_params=pltpu.CompilerParams(vmem_limit_bytes=VMEM_ASK),
        cost_estimate=pl.CostEstimate(
            flops=40 * rows * features * features,
            bytes_accessed=24 * 1024 * 1024,
            transcendentals=0,
        ),
        name="attention_backward",
    )(place, tokens, cots, residual, blended, normed, qkv, weights, norms, *seconds)


def route_to(place):
    shards, ctxs, tps = (lax.axis_size(name) for name in axes)
    pairs = []
    for shard in range(shards):
        for ctx in range(ctxs):
            for tp in range(tps):
                other_shard, other_ctx, other_tp = place(shard, ctx, tp)
                pairs.append(
                    (
                        (shard * ctxs + ctx) * tps + tp,
                        (other_shard * ctxs + other_ctx) * tps + other_tp % tps,
                    )
                )
    return pairs


def swap_core(value):
    return lax.ppermute(value, axes, route_to(lambda s, c, t: (s ^ 1, c, t)))


def swap_chip(value, turn):
    return lax.ppermute(
        value, axes, route_to(lambda s, c, t: (s ^ (turn & 2), c ^ (turn & 1), t))
    )


def swap_tp(value, turn):
    return lax.ppermute(value, axes, route_to(lambda s, c, t: (s, c, t ^ turn)))


def pass_on(value):
    return lax.ppermute(value, axes, route_to(lambda s, c, t: (s, c, t + 1)))


def worker_route(source, target):
    shards, ctxs, tps = (lax.axis_size(name) for name in axes)
    pairs = []
    for shard in range(shards):
        for ctx in range(ctxs):
            for worker in range(tps):
                if worker // 2 == shard % 2:
                    base = (shard * ctxs + ctx) * tps
                    pairs.append((base + source(worker) % tps, base + target(worker) % tps))
    return pairs


def to_worker(value, turn):
    return lax.ppermute(value, axes, worker_route(lambda w: w + turn, lambda w: w))


def from_worker(value, turn):
    step = 1 if turn > 0 else -1
    return lax.ppermute(
        value, axes, worker_route(lambda w: w + turn - step, lambda w: w + turn)
    )


def pick(value, index, axis=0):
    return lax.dynamic_index_in_dim(value, index, axis, keepdims=False)


def relative(value, chip):
    return [pick(value, jnp.bitwise_xor(chip, turn)) for turn in range(4)]


def pass_by(value, steps):
    return lax.ppermute(value, axes, route_to(lambda s, c, t: (s, c, t + steps)))


def direct_gather(value):
    return [value] + [pass_by(value, steps) for steps in range(1, lax.axis_size("tp"))]


class Live:
    def __init__(self, values=None):
        vars(self).update(values or {})

    @property
    def drop(self):
        return Drop(vars(self))


class Drop:
    def __init__(self, values):
        self._values = values

    def __getattr__(self, name):
        return self._values.pop(name)


def hold(live):
    return Live(lax.optimization_barrier(vars(live)))


def by_tp(held, tp):
    count = len(held)
    stacked = jnp.stack(held)
    return jnp.stack([pick(stacked, (tp - place) % count) for place in range(count)])


def place_chips(pieces, chip):
    stacked = jnp.stack(pieces)
    return jnp.stack([pick(stacked, jnp.bitwise_xor(chip, place)) for place in range(4)])


def place_cores(own, other, core):
    return jnp.where(core == 0, jnp.stack([own, other]), jnp.stack([other, own]))


def low_dot(spec, left, right):
    return jnp.einsum(
        spec,
        left.astype(jnp.bfloat16),
        right.astype(jnp.bfloat16),
        preferred_element_type=jnp.float32,
    )


def plane_device(
    tokens,
    cotangent,
    routing,
    gating,
    inward,
    outward,
    scales,
    shifts,
    upward,
    downward,
    inward_moment,
    outward_moment,
    scales_moment,
    shifts_moment,
    upward_moment,
    downward_moment,
):
    rows_here = tokens.shape[1]
    features = tokens.shape[2]
    seqs = rows_here // LEN
    experts = upward.shape[0]
    half_experts = experts // 2
    shard = lax.axis_index("shard")
    core = shard % 2
    ctx = lax.axis_index("ctx")
    tp = lax.axis_index("tp")
    tps = lax.axis_size("tp")
    devices = lax.axis_size(axes)
    chip = (shard // 2) * 2 + ctx
    low = jnp.bfloat16
    rows_attn = inward.shape[1]
    rows_local = upward.shape[1]
    cols_local = upward.shape[2]

    v = Live()
    device = jnp.stack([chip, core, tp]).astype(jnp.int32)
    y_here, x_here = shard // 2, ctx
    padded = seqs * IMAGE
    half = tps // 2
    own_tokens, own_cot = (
        jnp.pad(
            value[0].reshape(seqs, LEN, features), ((0, 0), (0, IMAGE - LEN), (0, 0))
        ).reshape(padded, features)
        for value in (tokens, cotangent)
    )

    def halves(value):
        value = value.astype(low).reshape(2, half_experts, rows_local, cols_local)
        return pick(value, core), pick(value, 1 - core)

    def own_order(value):
        return jnp.stack([pick(value, jnp.bitwise_xor(chip, r)) for r in range(4)])

    up_kept, up_sent = halves(upward)
    down_kept, down_sent = halves(downward)
    v.up, v.down = [own_order(up_kept)], [own_order(down_kept)]
    v.up_x, v.down_y = [swap_chip(v.up[0], 1)], [swap_chip(v.down[0], 2)]
    v.column = direct_gather(jnp.concatenate([inward, outward[None]]))
    v.sent = jnp.stack([up_sent, down_sent])
    v.cots = [own_cot]

    packed = jnp.concatenate([routing[0].astype(jnp.float32).T, gating[0].T])
    packed = jnp.pad(
        packed.reshape(4, seqs, LEN), ((0, 0), (0, 0), (0, IMAGE - LEN)), constant_values=-1.0
    )
    norm_rows = jnp.concatenate([scales, shifts]).astype(jnp.float32)
    packed = jnp.concatenate(
        [packed.reshape(4, padded), jnp.pad(norm_rows, ((0, 0), (0, padded - rows_attn)))]
    )
    v.packs = direct_gather(packed)
    v = hold(v)

    column = by_tp(v.drop.column, tp).transpose(1, 0, 2, 3)
    column = column.reshape(4, tps * rows_attn, features)
    v.pieces = [column, swap_chip(column, 1), swap_chip(column, 2)]
    v.cots.append(pass_on(v.cots[-1]))
    v.got = swap_core(v.drop.sent)
    packs = jnp.stack(v.packs)
    v.packs = [packs, swap_core(packs)]
    v = hold(v)

    column, from_x, from_y = v.pieces
    v.far = [swap_chip(from_x[:2], 2), swap_chip(from_y[2:], 1)]
    v.others = [swap_core(jnp.stack(v.pieces[:2]))]
    got = v.drop.got
    v.up.append(own_order(got[0]))
    v.down.append(own_order(got[1]))
    own_packs, other_packs = v.drop.packs
    norms = [by_tp(list(each[:, 4:, :rows_attn]), tp) for each in (own_packs, other_packs)]
    norms = place_cores(*norms, core)
    v.norms = [norms, swap_chip(norms, 1)]
    packs = jnp.concatenate([own_packs, other_packs])
    mine = core * half_experts + jnp.bitwise_xor(chip, jnp.arange(4, dtype=jnp.int32))
    hits = packs[None, :, :2] == mine.astype(jnp.float32)[:, None, None, None]
    chosen = jnp.any(hits, axis=2)
    gate_tok = jnp.sum(jnp.where(hits, packs[None, :, 2:4], 0.0), axis=2)
    places = jnp.arange(padded)
    earlier = (places[:, None] < places[None, :]).astype(low)
    rank = jnp.einsum(
        "rbt,tu->rbu", chosen.astype(low), earlier, preferred_element_type=jnp.float32
    )
    rank = jnp.where(chosen, rank, -1.0).astype(jnp.int32)
    counts = jnp.sum(chosen.astype(jnp.int32), axis=2)
    counts = (counts + 15) // 16 * 16
    starts = jnp.cumsum(jnp.pad(counts, ((0, 0), (1, 0))), axis=1).astype(jnp.int32).reshape(-1)
    v.routes = (jnp.concatenate([starts, device[:2]]), rank, gate_tok)
    v = hold(v)
    far = jnp.concatenate(v.drop.far)
    v.pieces = v.pieces + [far]
    v.others.append(swap_core(jnp.stack(v.pieces[2:])))
    v.cots.append(pass_on(v.cots[-1]))
    v.up_x.append(swap_chip(v.up[1], 1))
    v.down_y.append(swap_chip(v.down[1], 2))
    norms = place_cores(*v.norms, ctx)
    v.norms = [norms, swap_chip(norms, 2)]
    v = hold(v)
    norms = place_cores(*v.drop.norms, y_here)
    norms = norms.transpose(4, 0, 2, 1, 3, 5).reshape(4, features)

    normed, qkv, blended, residual, second, full_weights = attention_forward(
        device, own_tokens, norms, v.drop.pieces, v.drop.others
    )
    v.seconds = [second]
    v.up_xy, v.down_xy = [swap_chip(v.up_x[0], 2)], [swap_chip(v.down_y[0], 1)]
    v.cots.append(pass_on(v.cots[-1]))
    v.cots_other = [swap_core(each) for each in v.cots[:2]]
    v = hold(v)

    v.seconds.append(pass_on(v.seconds[-1]))
    v.up_xy.append(swap_chip(v.up_x[1], 2))
    v.down_xy.append(swap_chip(v.down_y[1], 1))
    v.cots_other += [swap_core(each) for each in v.cots[2:]]
    v = hold(v)
    v.seconds.append(pass_on(v.seconds[-1]))
    v.down_x, v.up_y = [swap_chip(v.down[0], 1)], [swap_chip(v.up[0], 2)]
    v.seconds_other = [swap_core(v.seconds[0])]
    moments = halves(upward_moment) + halves(downward_moment)
    v.moments = moments[0], moments[2], swap_core(jnp.stack([moments[1], moments[3]]))
    v = hold(v)
    v.seconds.append(pass_on(v.seconds[-1]))
    v.down_x.append(swap_chip(v.down[1], 1))
    v.up_y.append(swap_chip(v.up[1], 2))
    v.seconds_other += [swap_core(each) for each in v.seconds[1:3]]
    moments = v.drop.moments
    moments = jnp.stack([moments[0], moments[2][0], moments[1], moments[2][1]])
    v.moments = [pick(moments, jnp.bitwise_xor(chip, turn), 1) for turn in range(4)]
    v = hold(v)
    v.seconds_other.append(swap_core(v.seconds[3]))
    v = hold(v)

    ups = v.drop.up + v.drop.up_x + v.drop.up_y + v.drop.up_xy
    downs = v.drop.down + v.drop.down_x + v.drop.down_y + v.drop.down_xy
    v.moments = [v.moments[0]] + [swap_chip(v.moments[turn], turn) for turn in range(1, 4)]
    hidden, before, v.own, v.near_x, v.near_y, v.far_x, v.far_y = experts_pass(
        *v.routes,
        v.drop.seconds + v.drop.seconds_other,
        v.drop.cots + v.drop.cots_other,
        ups, downs,
    )
    v.hidden, v.before = hidden, before
    v.ups, v.downs = ups, downs
    v = hold(v)

    v.part = tokens_pass(*v.routes, v.drop.before, v.drop.ups, False)
    v.far_x, v.far_y = swap_chip(v.far_x, 1), swap_chip(v.far_y, 2)
    v = hold(v)

    def join(own, other):
        return (own.astype(jnp.float32) + other.astype(jnp.float32)).astype(low)

    v.along_x = v.near_x.at[1].set(join(v.near_x[1], v.drop.far_y))
    v.along_y = v.near_y.at[0].set(join(v.near_y[0], v.drop.far_x))
    v.near_x = v.near_y = None
    v.part = [v.part[0], swap_core(v.part[1])]
    v = hold(v)
    kept = join(*v.drop.part)
    v.along_x, v.along_y = swap_chip(v.along_x, 1), swap_chip(v.along_y, 2)
    v.seconds = [kept[0]] + [pass_by(kept[turn], -turn) for turn in range(1, tps)]
    v.mixed = tokens_pass(*v.drop.routes, v.drop.hidden, v.drop.downs, True)
    v = hold(v)

    push, push_next, band0, band1, band2, *rows = push_rows(
        device, v.drop.own, (v.drop.along_x, v.drop.along_y), v.drop.moments
    )
    v.push, v.blocks, v.rows = [push, push_next], [band0, band1, band2], rows
    v.mixed = [v.mixed[0], swap_core(v.mixed[1])]
    v = hold(v)

    def rows_out(rows):
        return [rows[0]] + [swap_chip(rows[turn], turn) for turn in range(1, 4)]

    def rows_between(got):
        got = place_chips(got, chip)
        return pick(got, core, 2), swap_core(pick(got, 1 - core, 2))

    def rows_in(kept, got):
        joined = place_cores(kept, got, core).transpose(2, 0, 1, 3, 4)
        joined = joined.reshape(2, experts, rows_local, cols_local)
        return joined.astype(jnp.float32)

    v.joined = [v.push[0]] + [to_worker(v.push[1], turn) for turn in (1, 3)]
    v.rows = rows_out(v.rows)
    v.input_grad, v.own, v.gone, v.vectors = attention_backward(
        device, own_tokens, own_cot, residual, blended, normed, qkv,
        v.drop.seconds,
        full_weights, norms,
    )
    v = hold(v)

    def added(value, got):
        return value.astype(jnp.float32) + got.astype(jnp.float32)

    shape = (4, 2, 2, tps, rows_attn, features)
    v.gone = swap_core(v.gone)
    v.blocks[:2] = [to_worker(block, 2) for block in v.blocks[:2]]
    v.rows = rows_between(v.rows)
    vectors = v.vectors[:4]
    v.vectors = [vectors, swap_core(vectors)]
    v.input_grad = v.input_grad.reshape(seqs, IMAGE, features)[:, :LEN].reshape(rows_here, features)
    mixed = added(*v.mixed)
    v.mixed = [mixed[0]] + [mixed[turn].astype(low) for turn in range(1, tps)]
    v = hold(v)
    own, gone = v.drop.own.reshape(shape), v.drop.gone.reshape(shape)

    def first_part(x):
        return added(pick(own, x, 2)[:, :, :half], pick(gone, x, 2)[:, :, :half])

    def last_part(y):
        return added(pick(own, y, 1)[:, :, half:], pick(gone, y, 1)[:, :, half:])

    v.first = [first_part(x_here), swap_chip(first_part(1 - x_here).astype(low), 1)]
    v.last = [last_part(y_here), swap_chip(last_part(1 - y_here).astype(low), 2)]
    v.mixed.append(pass_by(v.mixed[2], -1))
    vectors = sum(v.vectors)
    v.vectors = [vectors, swap_chip(vectors, 1)]
    v = hold(v)
    first, last = added(*v.first), added(*v.last)
    v.first = [pick(first, y_here, 1), swap_chip(pick(first, 1 - y_here, 1).astype(low), 2)]
    v.last = [pick(last, x_here, 1), swap_chip(pick(last, 1 - x_here, 1).astype(low), 1)]
    v.blocks[2] = to_worker(v.blocks[2], 2)
    vectors = sum(v.vectors)
    v.vectors = [vectors, swap_chip(vectors, 2)]
    v = hold(v)

    sums = jnp.concatenate([added(*v.drop.first), added(*v.drop.last)], axis=1)
    vectors = jnp.pad(sum(v.drop.vectors)[:, None], ((0, 0), (0, 7), (0, 0)))
    parts = [
        jnp.concatenate([pick(sums, (tp - turn) % tps, 1), vectors], axis=1).astype(low)
        for turn in range(tps)
    ]
    v.sums = [parts[0]] + [pass_by(parts[turn], -turn) for turn in range(1, tps)]
    v.mixers = wide_first(v.drop.joined + v.drop.blocks)
    v = hold(v)
    sums = sum(part.astype(jnp.float32) for part in v.drop.sums)
    v.vectors = lax.dynamic_slice(
        sums[:, rows_attn], (0, lax.axis_index(axes) * rows_attn), (4, rows_attn)
    )
    sums = sums[:, :rows_attn]
    inward_grad, outward_grad = sums[:3], sums[3]
    inward_state, inward_push = advance(inward_grad, inward_moment)
    outward_state, outward_push = advance(outward_grad, outward_moment)
    v.column = direct_gather(jnp.concatenate([inward_push, outward_push[None]]).astype(low))
    v.mixers = [wide_last(*v.mixers)]
    v = hold(v)
    column = by_tp(v.drop.column, tp).transpose(1, 0, 2, 3)
    gone = relative(column, chip)
    v.pushes = [gone[0]] + [swap_chip(gone[turn], turn) for turn in range(1, 4)]
    upward_grad, downward_grad = rows_in(*v.drop.rows)
    v.states = [
        (upward_grad, advance(upward_grad, upward_moment)[0]),
        (downward_grad, advance(downward_grad, downward_moment)[0]),
    ]
    v.mixers.append(from_worker(v.mixers[0], 1))
    v.mixers.append(from_worker(v.mixers[0], -1))
    v = hold(v)
    pushes = place_chips(v.pushes, chip)
    v.pushes = [pushes, swap_core(pushes)]
    v.mixers.insert(2, from_worker(v.mixers[1], 2))
    v = hold(v)
    pushes = place_cores(*v.drop.pushes, core)
    pushes = pushes.reshape(2, 2, 2, tps, rows_attn, features).transpose(1, 0, 2, 3, 4, 5)
    v.pushes = pushes.reshape(features, features)
    v.new = apply_mixers(device, v.drop.mixers, v.drop.push, rows_local)
    v = hold(v)

    v.new = rows_out(v.new)
    own_part, next_part, unused, far_part, got = v.mixed
    v.mixed = [own_part, pass_by(added(next_part, got).astype(low), -1), pass_on(far_part)]
    v.moved = orthogonal_square(v.drop.pushes)
    v = hold(v)
    moved = v.drop.moved.reshape(2, 2, 2, tps, rows_attn, features)
    moved = pick(pick(moved, core, 1), tp, 2).reshape(4, rows_attn, features)
    gone = relative(moved, chip)
    v.moved = [gone[0]] + [swap_chip(gone[turn], turn) for turn in range(1, 4)]
    v.new = rows_between(v.new)
    v = hold(v)
    mixed = v.drop.mixed
    result = (residual + mixed[0] + added(mixed[1], mixed[2])).astype(low)
    result = result.reshape(seqs, IMAGE, features)[:, :LEN].reshape(rows_here, features)
    input_grad = v.input_grad
    scales_grad, shifts_grad = v.vectors[:2], v.vectors[2:]
    scales_state, scales_push = advance(scales_grad, scales_moment)
    shifts_state, shifts_push = advance(shifts_grad, shifts_moment)
    up_new, down_new = rows_in(*v.new)
    upward_new = upward.astype(jnp.float32) - 2.0 * up_new
    downward_new = downward.astype(jnp.float32) - down_new
    (upward_grad, upward_state), (downward_grad, downward_state) = v.states
    got = place_chips(v.moved, chip).astype(jnp.float32)
    inward_new = inward.astype(jnp.float32) - got[:3]
    outward_new = outward.astype(jnp.float32) - got[3]
    vector_rate = 0.6 / math.sqrt(devices * rows_here)
    scales_new = scales.astype(jnp.float32) - vector_rate * scales_push
    shifts_new = shifts.astype(jnp.float32) - vector_rate * shifts_push
    return (
        result[None],
        input_grad[None],
        inward_grad,
        outward_grad,
        scales_grad,
        shifts_grad,
        upward_grad,
        downward_grad,
        inward_state,
        outward_state,
        scales_state,
        shifts_state,
        upward_state,
        downward_state,
        inward_new,
        outward_new,
        scales_new,
        shifts_new,
        upward_new,
        downward_new,
    )


def solution(mesh):
    in_specs = (
        P(("shard", "tp"), "ctx", None),
        P(("shard", "tp"), "ctx", None),
        P(("shard", "tp"), "ctx", None),
        P(("shard", "tp"), "ctx", None),
        P(None, ("shard", "ctx", "tp"), None),
        P(("shard", "ctx", "tp"), None),
        P(None, ("shard", "ctx", "tp")),
        P(None, ("shard", "ctx", "tp")),
        P(None, ("shard", "ctx"), "tp"),
        P(None, ("shard", "ctx"), "tp"),
        P(None, ("shard", "ctx", "tp"), None),
        P(("shard", "ctx", "tp"), None),
        P(None, ("shard", "ctx", "tp")),
        P(None, ("shard", "ctx", "tp")),
        P(None, ("shard", "ctx"), "tp"),
        P(None, ("shard", "ctx"), "tp"),
    )
    out_specs = (
        P(("shard", "tp"), "ctx", None),
        P(("shard", "tp"), "ctx", None),
        P(None, ("shard", "ctx", "tp"), None),
        P(("shard", "ctx", "tp"), None),
        P(None, ("shard", "ctx", "tp")),
        P(None, ("shard", "ctx", "tp")),
        P(None, ("shard", "ctx"), "tp"),
        P(None, ("shard", "ctx"), "tp"),
        P(None, ("shard", "ctx", "tp"), None),
        P(("shard", "ctx", "tp"), None),
        P(None, ("shard", "ctx", "tp")),
        P(None, ("shard", "ctx", "tp")),
        P(None, ("shard", "ctx"), "tp"),
        P(None, ("shard", "ctx"), "tp"),
        P(None, ("shard", "ctx", "tp"), None),
        P(("shard", "ctx", "tp"), None),
        P(None, ("shard", "ctx", "tp")),
        P(None, ("shard", "ctx", "tp")),
        P(None, ("shard", "ctx"), "tp"),
        P(None, ("shard", "ctx"), "tp"),
    )
    body = plane_device if mesh.shape["shard"] == 4 and mesh.shape["ctx"] == 2 and mesh.shape["tp"] == 4 else on_device
    return jax.shard_map(
        body, mesh=mesh, in_specs=in_specs, out_specs=out_specs, check_vma=False
    )
```

```python
import functools
import math

import jax
import jax.numpy as jnp
import numpy as np
from jax import lax
from jax.experimental import pallas as pl
from jax.experimental.pallas import tpu as pltpu
from jax.sharding import PartitionSpec as P

HEAD_DIM = 64
LEN = 197


first_coef = 3.4445
second_coef = -4.775
third_coef = 2.0315
momentum_decay = 0.9
norm_epsilon = 1e-06
orth_epsilon = 1e-07
highest = lax.Precision.HIGHEST


def normalize(values, factor, offset):
    average = jnp.mean(values, axis=-1, keepdims=True)
    centred = values - average
    inverse = lax.rsqrt(jnp.mean(centred * centred, axis=-1, keepdims=True) + norm_epsilon)
    unit_rows = centred * inverse
    return (unit_rows * factor + offset, unit_rows, inverse)


def normalize_back(gradient, unit_rows, inverse, factor):
    inner = gradient * factor
    average = jnp.mean(inner, axis=-1, keepdims=True)
    along = jnp.mean(inner * unit_rows, axis=-1, keepdims=True)
    back = inverse * (inner - average - unit_rows * along)
    return (back, jnp.sum(gradient * unit_rows, axis=0), jnp.sum(gradient, axis=0))


def slot_sources(routes, experts, capacity):
    pairs = routes.shape[0] * routes.shape[1]
    chosen = routes.reshape(pairs)
    onehot = (chosen[:, None] == jnp.arange(experts, dtype=jnp.int32)[None, :]).astype(jnp.int32)
    earlier = jnp.cumsum(onehot, axis=0) - onehot
    placed = jnp.sum(earlier * onehot, axis=1) + chosen * capacity
    matches = placed[None, :] == jnp.arange(experts * capacity, dtype=jnp.int32)[:, None]
    source = jnp.sum(jnp.where(matches, jnp.arange(pairs, dtype=jnp.int32)[None, :], 0), axis=1)
    filled = jnp.any(matches, axis=1)
    return (placed, source, filled)


def orthogonal(matrix):
    summed = jnp.sqrt(jnp.sum(matrix * matrix))
    current = matrix / (summed + orth_epsilon)
    for repeat in range(5):
        square = lax.dot_general(
            current,
            current,
            (((1,), (1,)), ((), ())),
            precision=highest,
            preferred_element_type=jnp.float32,
        )
        power = jnp.dot(square, square, precision=highest, preferred_element_type=jnp.float32)
        mixer = second_coef * square + third_coef * power
        current = first_coef * current + jnp.dot(
            mixer, current, precision=highest, preferred_element_type=jnp.float32
        )
    return current


def advance(gradient, moment):
    current = momentum_decay * moment + (1.0 - momentum_decay) * gradient
    return (current, (1.0 - momentum_decay) * gradient + momentum_decay * current)


def expert_weights(upward, downward):
    return (
        lax.all_gather(upward, ("shard", "ctx"), axis=1, tiled=True),
        lax.all_gather(downward, ("shard", "ctx"), axis=1, tiled=True),
    )


def on_device(
    tokens,
    cotangent,
    routing,
    gating,
    inward,
    outward,
    scales,
    shifts,
    upward,
    downward,
    inward_moment,
    outward_moment,
    scales_moment,
    shifts_moment,
    upward_moment,
    downward_moment,
):
    rows_here = tokens.shape[1]
    features = tokens.shape[2]
    experts = upward.shape[0]
    top_count = routing.shape[2]
    capacity = 2 * top_count * rows_here // experts
    attn_scale = HEAD_DIM ** (-0.5)
    inputs = tokens[0].astype(jnp.float32)
    routes = routing[0]
    gate_pairs = gating[0].reshape(-1)
    zero_low = jnp.zeros((), jnp.bfloat16)
    full_in, full_out, all_scales, all_shifts = (
        lax.all_gather(inward, ("shard", "ctx", "tp"), axis=1, tiled=True),
        lax.all_gather(outward, ("shard", "ctx", "tp"), axis=0, tiled=True),
        lax.all_gather(scales, ("shard", "ctx", "tp"), axis=1, tiled=True),
        lax.all_gather(shifts, ("shard", "ctx", "tp"), axis=1, tiled=True),
    )
    factor = all_scales.astype(jnp.float32)
    offset = all_shifts.astype(jnp.float32)
    normed, unit_one, inverse_one = normalize(inputs, factor[0], offset[0])
    normed_low = normed.astype(jnp.bfloat16)
    projected = jnp.einsum(
        "td,kde->kte", normed_low, full_in, preferred_element_type=jnp.float32
    ).astype(jnp.bfloat16)
    head_rows = lax.all_to_all(projected, "ctx", split_axis=2, concat_axis=1, tiled=True)
    group_rows = head_rows.shape[1]
    head_width = head_rows.shape[2]
    seqs_here = group_rows // LEN
    shaped = head_rows.reshape(3, seqs_here, LEN, head_width // HEAD_DIM, HEAD_DIM)
    query_rows, key_rows, value_rows = (shaped[0], shaped[1], shaped[2])
    scores = (
        jnp.einsum("sqhd,skhd->shqk", query_rows, key_rows, preferred_element_type=jnp.float32)
        * attn_scale
    )
    top_score = jnp.max(scores, axis=-1, keepdims=True)
    logsum = top_score + jnp.log(jnp.sum(jnp.exp(scores - top_score), axis=-1, keepdims=True))
    soft_low = jnp.exp(scores - logsum).astype(jnp.bfloat16)
    blended = jnp.einsum(
        "shqk,skhd->sqhd", soft_low, value_rows, preferred_element_type=jnp.float32
    ).astype(jnp.bfloat16)
    blended_tokens = lax.all_to_all(
        blended.reshape(group_rows, head_width), "ctx", split_axis=0, concat_axis=1, tiled=True
    )
    residual = inputs + jnp.dot(blended_tokens, full_out, preferred_element_type=jnp.float32)
    second, unit_two, inverse_two = normalize(residual, factor[1], offset[1])
    second_low = second.astype(jnp.bfloat16)
    upstream = cotangent[0].astype(jnp.float32)
    placed, source, filled = slot_sources(routes, experts, capacity)
    slot_rows = jnp.where(filled[:, None], second_low[source // top_count], zero_low)
    slot_rows = slot_rows.reshape(experts, capacity, features)
    group_slots = lax.all_gather(slot_rows, "tp", axis=1, tiled=True)
    upper_full, lower_full = expert_weights(upward, downward)
    before = jnp.einsum("ecd,edf->ecf", group_slots, upper_full, preferred_element_type=jnp.float32)
    hidden = jax.nn.gelu(before).astype(jnp.bfloat16)
    partial_out = jnp.einsum("ecf,edf->ecd", hidden, lower_full, preferred_element_type=jnp.float32)
    own_out = lax.psum_scatter(
        partial_out.astype(jnp.bfloat16), "tp", scatter_dimension=1, tiled=True
    ).astype(jnp.float32)
    picked = own_out.reshape(experts * capacity, features)[placed].reshape(
        rows_here, top_count, features
    )
    mixture = jnp.sum(picked * gating[0][:, :, None], axis=1)
    result = (residual + mixture).astype(jnp.bfloat16)
    slot_grad = jnp.where(
        filled[:, None], upstream[source // top_count] * gate_pairs[source][:, None], 0.0
    )
    slot_grad = slot_grad.astype(jnp.bfloat16).reshape(experts, capacity, features)
    group_grad = lax.all_gather(slot_grad, "tp", axis=1, tiled=True)
    upper_full, lower_full = expert_weights(upward, downward)
    d_hidden = jnp.einsum(
        "ecd,edf->ecf", group_grad, lower_full, preferred_element_type=jnp.float32
    )
    unused, gelu_back = jax.vjp(jax.nn.gelu, before)
    d_before = gelu_back(d_hidden)[0].astype(jnp.bfloat16)
    lower_part = jnp.einsum("ecd,ecf->edf", group_grad, hidden, preferred_element_type=jnp.float32)
    upper_part = jnp.einsum(
        "ecd,ecf->edf", group_slots, d_before, preferred_element_type=jnp.float32
    )
    slot_input_part = jnp.einsum(
        "ecf,edf->ecd", d_before, upper_full, preferred_element_type=jnp.float32
    )
    slot_input = lax.psum_scatter(
        slot_input_part.astype(jnp.bfloat16), "tp", scatter_dimension=1, tiled=True
    ).astype(jnp.float32)
    d_second = jnp.sum(
        slot_input.reshape(experts * capacity, features)[placed].reshape(
            rows_here, top_count, features
        ),
        axis=1,
    )
    d_norm_two, scale_two, shift_two = normalize_back(d_second, unit_two, inverse_two, factor[1])
    d_residual = upstream + d_norm_two
    d_attended = d_residual.astype(jnp.bfloat16)
    outward_part = jnp.einsum(
        "td,te->de", blended_tokens, d_attended, preferred_element_type=jnp.float32
    )
    d_blended = jnp.einsum(
        "te,de->td", d_attended, full_out, preferred_element_type=jnp.float32
    ).astype(jnp.bfloat16)
    d_heads = lax.all_to_all(d_blended, "ctx", split_axis=1, concat_axis=0, tiled=True)
    d_heads = d_heads.reshape(seqs_here, LEN, head_width // HEAD_DIM, HEAD_DIM)
    soft_full = jnp.exp(
        jnp.einsum("sqhd,skhd->shqk", query_rows, key_rows, preferred_element_type=jnp.float32)
        * attn_scale
        - logsum
    )
    d_soft = jnp.einsum("sqhd,skhd->shqk", d_heads, value_rows, preferred_element_type=jnp.float32)
    value_grad = jnp.einsum(
        "shqk,sqhd->skhd", soft_low, d_heads, preferred_element_type=jnp.float32
    ).astype(jnp.bfloat16)
    row_inner = jnp.sum(soft_full * d_soft, axis=-1, keepdims=True)
    d_scores = (soft_full * (d_soft - row_inner)).astype(jnp.bfloat16)
    query_grad = (
        jnp.einsum("shqk,skhd->sqhd", d_scores, key_rows, preferred_element_type=jnp.float32)
        * attn_scale
    ).astype(jnp.bfloat16)
    key_grad = (
        jnp.einsum("shqk,sqhd->skhd", d_scores, query_rows, preferred_element_type=jnp.float32)
        * attn_scale
    ).astype(jnp.bfloat16)
    stacked_grad = jnp.stack([query_grad, key_grad, value_grad]).reshape(3, group_rows, head_width)
    token_grad = lax.all_to_all(stacked_grad, "ctx", split_axis=1, concat_axis=2, tiled=True)
    inward_part = jnp.einsum(
        "td,kte->kde", normed_low, token_grad, preferred_element_type=jnp.float32
    )
    d_normed = jnp.einsum("kte,kde->td", token_grad, full_in, preferred_element_type=jnp.float32)
    d_norm_one, scale_one, shift_one = normalize_back(d_normed, unit_one, inverse_one, factor[0])
    input_grad = d_residual + d_norm_one
    inward_grad, outward_grad, scales_grad, shifts_grad = (
        lax.psum_scatter(inward_part, ("shard", "ctx", "tp"), scatter_dimension=1, tiled=True),
        lax.psum_scatter(outward_part, ("shard", "ctx", "tp"), scatter_dimension=0, tiled=True),
        lax.psum_scatter(
            jnp.stack([scale_one, scale_two]),
            ("shard", "ctx", "tp"),
            scatter_dimension=1,
            tiled=True,
        ),
        lax.psum_scatter(
            jnp.stack([shift_one, shift_two]),
            ("shard", "ctx", "tp"),
            scatter_dimension=1,
            tiled=True,
        ),
    )
    upward_grad, downward_grad = (
        lax.psum_scatter(
            upper_part.astype(jnp.bfloat16), ("shard", "ctx"), scatter_dimension=1, tiled=True
        ).astype(jnp.float32),
        lax.psum_scatter(
            lower_part.astype(jnp.bfloat16), ("shard", "ctx"), scatter_dimension=1, tiled=True
        ).astype(jnp.float32),
    )
    inward_state, inward_push = advance(inward_grad, inward_moment)
    outward_state, outward_push = advance(outward_grad, outward_moment)
    scales_state, scales_push = advance(scales_grad, scales_moment)
    shifts_state, shifts_push = advance(shifts_grad, shifts_moment)
    upward_state, upward_push = advance(upward_grad, upward_moment)
    downward_state, downward_push = advance(downward_grad, downward_moment)
    devices = lax.axis_size(("shard", "ctx", "tp"))
    outer_count = lax.axis_size(("shard", "ctx"))
    inner_count = lax.axis_size("tp")
    rows_local = upward.shape[1]
    cols_local = upward.shape[2]
    slot_size = rows_local * cols_local
    attention_size = inward.shape[1] * features
    full_cols = inner_count * cols_local

    def flat_pad(portion):
        flatten = portion.reshape(portion.shape[0], -1)
        return jnp.pad(flatten, ((0, 0), (0, slot_size - flatten.shape[1])))

    matrices = jnp.concatenate(
        [
            flat_pad(inward_push),
            flat_pad(outward_push[None]),
            upward_push.reshape(experts, slot_size),
            downward_push.reshape(experts, slot_size),
        ]
    )
    matrix_count = matrices.shape[0]
    owner_table = np.arange(matrix_count) * devices // matrix_count
    outgoing = jnp.zeros((devices, slot_size), jnp.float32).at[owner_table].set(matrices)
    received = lax.all_to_all(
        outgoing.astype(jnp.bfloat16),
        ("shard", "ctx", "tp"),
        split_axis=0,
        concat_axis=0,
        tiled=True,
    ).astype(outgoing.dtype)
    myself = lax.axis_index(("shard", "ctx", "tp"))
    owned = (
        jnp.sum(
            jnp.where(
                jnp.asarray(owner_table, dtype=jnp.int32) == myself,
                jnp.arange(matrix_count, dtype=jnp.int32) + 1,
                0,
            )
        )
        - 1
    )
    attention_kind = jnp.logical_and(owned >= 0, owned < 4)
    expert_form = (
        received.reshape(outer_count, inner_count, rows_local, cols_local)
        .transpose(0, 2, 1, 3)
        .reshape(features, full_cols)
    )
    attention_form = jnp.pad(
        received[:, :attention_size].reshape(features, features),
        ((0, 0), (0, full_cols - features)),
    )
    orthogonal_form = orthogonal(jnp.where(attention_kind, attention_form, expert_form))
    back_expert = (
        orthogonal_form.reshape(outer_count, rows_local, inner_count, cols_local)
        .transpose(0, 2, 1, 3)
        .reshape(devices, slot_size)
    )
    back_attention = jnp.pad(
        orthogonal_form[:, :features].reshape(devices, attention_size),
        ((0, 0), (0, slot_size - attention_size)),
    )
    returned = lax.all_to_all(
        jnp.where(attention_kind, back_attention, back_expert).astype(jnp.bfloat16),
        ("shard", "ctx", "tp"),
        split_axis=0,
        concat_axis=0,
        tiled=True,
    ).astype(jnp.float32)
    mine_parts = returned[owner_table]
    inward_new = inward.astype(jnp.float32) - mine_parts[:3, :attention_size].reshape(inward.shape)
    outward_new = outward.astype(jnp.float32) - mine_parts[3, :attention_size].reshape(
        outward.shape
    )
    upward_new = upward.astype(jnp.float32) - 2.0 * mine_parts[4 : 4 + experts].reshape(
        upward.shape
    )
    downward_new = downward.astype(jnp.float32) - mine_parts[4 + experts :].reshape(downward.shape)
    total_tokens = lax.axis_size("shard") * lax.axis_size("ctx") * lax.axis_size("tp") * rows_here
    vector_rate = 0.6 / math.sqrt(total_tokens)
    scales_new = scales.astype(jnp.float32) - vector_rate * scales_push
    shifts_new = shifts.astype(jnp.float32) - vector_rate * shifts_push
    return (
        result[None],
        input_grad[None],
        inward_grad,
        outward_grad,
        scales_grad,
        shifts_grad,
        upward_grad,
        downward_grad,
        inward_state,
        outward_state,
        scales_state,
        shifts_state,
        upward_state,
        downward_state,
        inward_new,
        outward_new,
        scales_new,
        shifts_new,
        upward_new,
        downward_new,
    )


axes = ("shard", "ctx", "tp")
TILE = 256
SPAN = 208
VMEM_ASK = 60 * 1024 * 1024


def dot_nn(left, right):
    return lax.dot_general(
        left, right, (((1,), (0,)), ((), ())), preferred_element_type=jnp.float32
    )


def dot_nt(left, right):
    return lax.dot_general(
        left, right, (((1,), (1,)), ((), ())), preferred_element_type=jnp.float32
    )


def dot_tn(left, right):
    return lax.dot_general(
        left, right, (((0,), (0,)), ((), ())), preferred_element_type=jnp.float32
    )


def tile_pairs(count):
    return [(row, col) for row in range(count) for col in range(row, count)]


def wide_bands(size):
    return [pl.ds(start, TILE) for start in range(0, size, TILE)]


def wide_steps(count, gram, whole, low, whole_low, mixer):
    bands = wide_bands(gram.shape[0])

    def step(repeat, carry):
        wide_mix(gram, whole, low, whole_low, mixer)
        for band in bands:
            half = first_coef * gram[band, :] + dot_nn(mixer[band, :], low[...])
            gram[band, :] = first_coef * half + dot_nn(half.astype(jnp.bfloat16), mixer[...])
            whole[band, :] = first_coef * whole[band, :] + dot_nn(mixer[band, :], whole_low[...])
        return carry

    lax.fori_loop(0, count, step, 0)


def wide_mix(gram, whole, low, whole_low, mixer):
    low[...] = gram[...].astype(jnp.bfloat16)
    whole_low[...] = whole[...].astype(jnp.bfloat16)
    for band in wide_bands(gram.shape[0]):
        squared = dot_nn(low[band, :], low[...])
        mixer[band, :] = (second_coef * gram[band, :] + third_coef * squared).astype(jnp.bfloat16)


def wide_first_kernel(block0, block1, block3, part0, part1, part2, gram, whole, low, mixer, whole_low, block2):
    size = gram.shape[0]
    bands = wide_bands(size)
    rows = lax.broadcasted_iota(jnp.int32, (TILE, size), 0)
    cols = lax.broadcasted_iota(jnp.int32, (TILE, size), 1)
    for part, band in zip((part0, part1, part2), bands):
        block2[band, :] = part[...]
    trace = 0.0
    for place, band in enumerate(bands):
        part = dot_nt(block0[band, :], block0[...])
        for block in (block1, block2, block3):
            part = part + dot_nt(block[band, :], block[...])
        gram[band, :] = part
        trace = trace + jnp.sum(jnp.where(rows + place * TILE == cols, part, 0.0))
    factor = 1.0 / (jnp.sqrt(trace) + orth_epsilon)
    for place, band in enumerate(bands):
        gram[band, :] = gram[band, :] * (factor * factor)
        whole[band, :] = jnp.where(rows + place * TILE == cols, factor, 0.0)
    wide_steps(2, gram, whole, low, whole_low, mixer)


def wide_last_kernel(gram_in, whole_in, out, gram, whole, low, mixer, whole_low):
    bands = wide_bands(gram.shape[0])
    gram[...] = gram_in[...]
    whole[...] = whole_in[...]
    wide_steps(2, gram, whole, low, whole_low, mixer)
    wide_mix(gram, whole, low, whole_low, mixer)
    for row, band in enumerate(bands):
        last = first_coef * whole[band, :] + dot_nn(mixer[band, :], whole_low[...])
        for place, pair in enumerate(tile_pairs(len(bands))):
            if pair[0] == row:
                out[place] = last[:, pair[1] * TILE : (pair[1] + 1) * TILE].astype(out.dtype)


def wide_call(kernel, size, out_shape, kept, scratch, name, inputs):
    vmem = pl.BlockSpec(memory_space=pltpu.VMEM)
    square = (size, size)
    return pl.pallas_call(
        kernel,
        out_shape=out_shape,
        in_specs=[vmem] * len(inputs),
        out_specs=jax.tree.map(lambda shape: vmem, out_shape),
        scratch_shapes=[pltpu.VMEM(square, jnp.float32)] * kept
        + [pltpu.VMEM(square, jnp.bfloat16)] * scratch,
        compiler_params=pltpu.CompilerParams(vmem_limit_bytes=VMEM_ASK),
        cost_estimate=pl.CostEstimate(
            flops=20 * size**3, bytes_accessed=8 * size * size, transcendentals=0
        ),
        name=name,
    )(*inputs)


def wide_first(blocks):
    size = blocks[0].shape[0]
    shape = jax.ShapeDtypeStruct((size, size), jnp.float32)
    return wide_call(wide_first_kernel, size, [shape, shape], 0, 4, "wide_first", blocks)


def wide_last(gram, whole):
    size = gram.shape[0]
    pairs = len(tile_pairs(size // TILE))
    shape = jax.ShapeDtypeStruct((pairs, TILE, TILE), jnp.bfloat16)
    return wide_call(wide_last_kernel, size, shape, 2, 3, "wide_last", (gram, whole))


def store_rows(chip, value, outs, which):
    depth = outs[0].shape[2]
    for turn, out in enumerate(outs):
        other = jnp.bitwise_xor(chip, turn)
        for core in range(2):
            row = ((other // 2) * 2 + core) * 2 + other % 2
            out[which, core] = value[pl.ds(pl.multiple_of(row * depth, 16), depth), :].astype(
                out.dtype
            )


def apply_kernel(place, *refs):
    mixers, pushes, outs, (full, moved) = refs[:4], refs[4:6], refs[6:10], refs[10:]
    chip, core, tp = place[0], place[1], place[2]
    count = full.shape[0] // TILE
    for which in range(2):
        source = lax.rem(tp - 2 * core - which + 4, 4)
        for step in range(4):

            @pl.when(source == step)
            def _():
                for spot, (row, col) in enumerate(tile_pairs(count)):
                    tile = mixers[step][spot]
                    full[pl.ds(row * TILE, TILE), pl.ds(col * TILE, TILE)] = tile
                    if row != col:
                        full[pl.ds(col * TILE, TILE), pl.ds(row * TILE, TILE)] = tile.T

        for spot in range(2):

            @pl.when(lax.rem(tp + spot, 2) == which)
            def _():
                moved[...] = dot_nn(full[...], pushes[spot][...])

        store_rows(chip, moved, outs, which)


def apply_mixers(place, mixers, pushes, depth):
    size, width = pushes[0].shape
    vmem = pl.BlockSpec(memory_space=pltpu.VMEM)
    shape = jax.ShapeDtypeStruct((2, 2, depth, width), jnp.bfloat16)
    return pl.pallas_call(
        apply_kernel,
        in_specs=[pl.BlockSpec(memory_space=pltpu.SMEM)] + [vmem] * 6,
        out_specs=[vmem] * 4,
        out_shape=[shape] * 4,
        scratch_shapes=[
            pltpu.VMEM((size, size), jnp.bfloat16),
            pltpu.VMEM((size, width), jnp.float32),
        ],
        compiler_params=pltpu.CompilerParams(vmem_limit_bytes=VMEM_ASK),
        cost_estimate=pl.CostEstimate(
            flops=4 * size**3, bytes_accessed=10 * size * size, transcendentals=0
        ),
        name="apply_mixers",
    )(place, *mixers, *pushes)


def push_kernel(place, own, *refs):
    gots, moments, refs = refs[:2], refs[2:6], refs[6:]
    pushes, bands, outs, (total,) = refs[:2], refs[2:5], refs[5:9], refs[9:]
    chip, core, tp = place[0], place[1], place[2]
    keep = 1.0 - momentum_decay
    depth = outs[0].shape[2]
    for which in range(2):
        total[...] = (
            own[which].astype(jnp.float32)
            + gots[0][which].astype(jnp.float32)
            + gots[1][which].astype(jnp.float32)
        )
        store_rows(chip, total, outs, which)
        for turn, moment in enumerate(moments):
            other = jnp.bitwise_xor(chip, turn)
            for side in range(2):
                row = ((other // 2) * 2 + jnp.bitwise_xor(core, side)) * 2 + other % 2
                rows = pl.ds(pl.multiple_of(row * depth, 16), depth)
                pushed = (
                    (keep + momentum_decay * keep) * total[rows, :]
                    + momentum_decay * momentum_decay * moment[2 * which + side].astype(jnp.float32)
                ).astype(jnp.bfloat16)
                for spot in range(2):

                    @pl.when(lax.rem(tp + spot, 2) == which)
                    def _():
                        pushes[spot][rows, :] = pushed

    for place, band in enumerate(bands):
        band[...] = pushes[0][pl.ds(place * TILE, TILE), :]


def push_rows(place, own, gots, moments):
    size, width = own.shape[1:]
    depth = moments[0].shape[1]
    vmem = pl.BlockSpec(memory_space=pltpu.VMEM)
    rows = jax.ShapeDtypeStruct((2, 2, depth, width), jnp.bfloat16)
    return pl.pallas_call(
        push_kernel,
        in_specs=[pl.BlockSpec(memory_space=pltpu.SMEM)] + [vmem] * 7,
        out_specs=[vmem] * 9,
        out_shape=[jax.ShapeDtypeStruct((size, width), jnp.bfloat16)] * 2
        + [jax.ShapeDtypeStruct((TILE, width), jnp.bfloat16)] * 3
        + [rows] * 4,
        scratch_shapes=[pltpu.VMEM((size, width), jnp.float32)],
        compiler_params=pltpu.CompilerParams(vmem_limit_bytes=VMEM_ASK),
        cost_estimate=pl.CostEstimate(
            flops=20 * size * width, bytes_accessed=24 * size * width, transcendentals=0
        ),
        name="push_rows",
    )(place, own, *gots, *moments)


def square_kernel(matrix, out, current, low, square, square_low, mixer):
    size = current.shape[0]
    bands = [pl.ds(start, TILE) for start in range(0, size, TILE)]
    total = 0.0
    for band in bands:
        part = matrix[band, :].astype(jnp.float32)
        total = total + jnp.sum(part * part)
    factor = 1.0 / (jnp.sqrt(total) + orth_epsilon)
    for band in bands:
        current[band, :] = matrix[band, :].astype(jnp.float32) * factor

    def step(repeat, carry):
        low[...] = current[...].astype(jnp.bfloat16)
        for band in bands:
            part = dot_nt(low[band, :], low[...])
            square[band, :] = part
            square_low[band, :] = part.astype(jnp.bfloat16)
        for band in bands:
            mixed = second_coef * square[band, :] + third_coef * dot_nn(
                square_low[band, :], square_low[...]
            )
            mixer[band, :] = mixed.astype(jnp.bfloat16)
        for band in bands:
            current[band, :] = first_coef * current[band, :] + dot_nn(mixer[band, :], low[...])
        return carry

    lax.fori_loop(0, 5, step, 0)
    out[...] = current[...].astype(out.dtype)


def orthogonal_square(matrix):
    size = matrix.shape[0]
    return pl.pallas_call(
        square_kernel,
        out_shape=jax.ShapeDtypeStruct((size, size), jnp.bfloat16),
        in_specs=[pl.BlockSpec(memory_space=pltpu.VMEM)],
        out_specs=pl.BlockSpec(memory_space=pltpu.VMEM),
        scratch_shapes=[
            pltpu.VMEM((size, size), jnp.float32),
            pltpu.VMEM((size, size), jnp.bfloat16),
            pltpu.VMEM((size, size), jnp.float32),
            pltpu.VMEM((size, size), jnp.bfloat16),
            pltpu.VMEM((size, size), jnp.bfloat16),
        ],
        compiler_params=pltpu.CompilerParams(vmem_limit_bytes=VMEM_ASK),
        cost_estimate=pl.CostEstimate(
            flops=30 * size**3, bytes_accessed=4 * matrix.size, transcendentals=0
        ),
        name="square_orthogonal",
    )(matrix)


root = math.sqrt(2.0 / math.pi)


def gelu_pair(value):
    squared = value * value
    part = 0.5 * jnp.tanh(value * (root + (root * 0.044715) * squared)) + 0.5
    bend = value * (2.0 * root + (6.0 * root * 0.044715) * squared)
    return value * part, part + part * (1.0 - part) * bend


def one_hot(rank):
    return lax.broadcasted_iota(jnp.int32, (SPAN, rank.shape[1]), 0) == rank


def assemble(chip, core, pieces, whole):
    depth = pieces[0].shape[1]
    for place, piece in enumerate(pieces):
        other = jnp.bitwise_xor(chip, place // 2)
        row = ((other // 2) * 2 + jnp.bitwise_xor(core, place % 2)) * 2 + other % 2
        whole[pl.ds(pl.multiple_of(row * depth, 16), depth), :] = piece[0]


def each_band(count, work):
    wide = (count + 127) // 512

    def step(place, carry):
        work(pl.ds(pl.multiple_of(place * 512, 512), 512))
        return carry

    lax.fori_loop(0, wide, step, 0)
    rest = count - wide * 512
    start = wide * 512

    @pl.when(rest > 128)
    def _():
        work(pl.ds(pl.multiple_of(start, 512), 256))

    @pl.when(jnp.logical_or(rest > 256, jnp.logical_and(rest > 0, rest <= 128)))
    def _():
        work(pl.ds(pl.multiple_of(start + jnp.where(rest > 256, 256, 0), 128), 128))


def gate_of(hot, gate):
    return jnp.sum(jnp.where(hot, gate, 0.0), axis=1, keepdims=True)


def experts_kernel(
    starts, rank, gate, *refs
):
    blocks = rank.shape[1]
    ups, downs, refs = refs[:8], refs[8:16], refs[16:]
    tokens_hbm, refs = refs[: 2 * blocks], refs[2 * blocks :]
    hidden_out, before_out, *refs = refs
    outs, refs = refs[:5], refs[5:]
    rows, cots, upper, lower, slots, grads, upper_sum, lower_sum, leaving, sems, out_sems = refs
    targets = [(outs[turn].at[0], outs[turn].at[1]) for turn in range(3)] + [(outs[3], outs[4])]
    expert = pl.program_id(0)
    base = expert * (blocks + 1)
    chip = starts[pl.num_programs(0) * (blocks + 1)]
    core = starts[pl.num_programs(0) * (blocks + 1) + 1]
    low = jnp.bfloat16

    @pl.when(expert == 0)
    def _():
        copies = []
        for block in range(blocks):
            for which, held in enumerate((rows, cots)):
                place = which * blocks + block
                copies.append(
                    pltpu.make_async_copy(tokens_hbm[place], held.at[block], sems.at[place])
                )
        for copy in copies:
            copy.start()

    assemble(chip, core, ups, upper)
    assemble(chip, core, downs, lower)

    for block in range(blocks):

        @pl.when(expert == 0)
        def _():
            for which, held in enumerate((rows, cots)):
                place = which * blocks + block
                pltpu.make_async_copy(tokens_hbm[place], held.at[block], sems.at[place]).wait()

        start = pl.multiple_of(starts[base + block], 16)
        hot = one_hot(rank[0, block : block + 1, :])
        spread = jnp.where(hot, 1.0, 0.0).astype(low)
        weight = gate_of(hot, gate[0, block : block + 1, :])
        slots[pl.ds(start, SPAN), :] = dot_nn(spread, rows[block]).astype(low)
        grads[pl.ds(start, SPAN), :] = (dot_nn(spread, cots[block]) * weight).astype(low)

    end = pl.multiple_of(starts[base + blocks], 16)
    slots[pl.ds(end, TILE), :] = jnp.zeros((TILE, slots.shape[1]), low)
    grads[pl.ds(end, TILE), :] = jnp.zeros((TILE, slots.shape[1]), low)
    upper_sum[...] = jnp.zeros_like(upper_sum)
    lower_sum[...] = jnp.zeros_like(lower_sum)

    def work(band):
        slot_rows, slot_grads = slots[band, :], grads[band, :]
        hidden, slope = gelu_pair(dot_nn(slot_rows, upper[...]))
        hidden = hidden.astype(low)
        d_before = (dot_nn(slot_grads, lower[...]) * slope).astype(low)
        hidden_out[0, band, :] = hidden
        before_out[0, band, :] = d_before
        upper_sum[...] += dot_tn(slot_rows, d_before)
        lower_sum[...] += dot_tn(slot_grads, hidden)

    each_band(starts[base + blocks], work)

    for turn, target in enumerate(targets):

        @pl.when(expert == turn)
        def _():
            if turn > 0:
                for which in range(2):
                    pltpu.make_async_copy(
                        leaving.at[which], targets[turn - 1][which], out_sems.at[2 * turn - 2 + which]
                    ).wait()
            leaving[0] = upper_sum[...].astype(low)
            leaving[1] = lower_sum[...].astype(low)
            copies = [
                pltpu.make_async_copy(leaving.at[which], target[which], out_sems.at[2 * turn + which])
                for which in range(2)
            ]
            for copy in copies:
                copy.start()
            if turn == 3:
                for copy in copies:
                    copy.wait()


def tokens_kernel(
    gated, starts, rank, gate, acts, *refs
):
    pieces, (part_own, part_other, whole, moved, spread, found) = refs[:8], refs[8:]
    expert = pl.program_id(0)
    count, blocks = rank.shape[0], rank.shape[1]
    base = expert * (blocks + 1)
    chip, core = starts[count * (blocks + 1)], starts[count * (blocks + 1) + 1]
    low = jnp.bfloat16

    @pl.when(expert == 0)
    def _():
        moved[...] = jnp.zeros_like(moved)

    assemble(chip, core, pieces, whole)

    def work(band):
        moved[expert, band, :] = dot_nt(acts[0, band, :], whole[...]).astype(low)

    each_band(starts[base + blocks], work)

    @pl.when(expert == count - 1)
    def _():
        for side, part in enumerate((part_own, part_other)):
            for place in range(blocks // 2):
                block = side * (blocks // 2) + place
                ways, rows_of = spread.at[place % 2], found.at[place % 2]
                for each in range(count):
                    start = pl.multiple_of(starts[each * (blocks + 1) + block], 16)
                    hot = one_hot(rank[each, block : block + 1, :])
                    rows = moved[each, pl.ds(start, SPAN), :]
                    if gated:
                        weight = gate_of(hot, gate[each, block : block + 1, :])
                        rows = (rows.astype(jnp.float32) * weight).astype(low)
                    band = pl.ds(each * SPAN, SPAN)
                    ways[band, :] = jnp.where(hot, 1.0, 0.0).astype(low)
                    rows_of[band, :] = rows
                part[place] = dot_tn(ways[...], rows_of[...]).astype(low)


def pass_shapes(rank, pieces):
    count = pieces[0].shape[0]
    blocks, padded = rank.shape[1], rank.shape[2]
    tiles = -(-blocks * SPAN // TILE)

    def of_expert(expert, starts):
        return (expert, 0, 0)

    piece_specs = [
        pl.BlockSpec(
            (1,) + pieces[0].shape[1:],
            lambda expert, starts, turn=place // 2: (jnp.bitwise_xor(expert, turn), 0, 0),
        )
        for place in range(8)
    ]
    return count, blocks, padded, tiles, of_expert, piece_specs


def experts_pass(starts, rank, gate, rows, cots, ups, downs):
    count, blocks, padded, tiles, of_expert, piece_specs = pass_shapes(rank, ups)
    features = rows[0].shape[1]
    width = ups[0].shape[2]
    most = blocks * SPAN
    low = jnp.bfloat16
    vectors = pl.BlockSpec((1, blocks, padded), of_expert)
    acts = pl.BlockSpec((1, tiles * TILE, width), of_expert)
    acts_shape = jax.ShapeDtypeStruct((count, tiles * TILE, width), low)
    grad_shape = jax.ShapeDtypeStruct((features, width), low)
    pair_shape = jax.ShapeDtypeStruct((2, features, width), low)
    return pl.pallas_call(
        experts_kernel,
        grid_spec=pltpu.PrefetchScalarGridSpec(
            num_scalar_prefetch=1,
            grid=(count,),
            in_specs=[vectors, vectors]
            + piece_specs * 2
            + [pl.BlockSpec(memory_space=pl.ANY)] * (2 * blocks),
            out_specs=[acts, acts] + [pl.BlockSpec(memory_space=pl.ANY)] * 5,
            scratch_shapes=[
                pltpu.VMEM((blocks, padded, features), low),
                pltpu.VMEM((blocks, padded, features), low),
                pltpu.VMEM((features, width), low),
                pltpu.VMEM((features, width), low),
                pltpu.VMEM((most + TILE, features), low),
                pltpu.VMEM((most + TILE, features), low),
                pltpu.VMEM((features, width), jnp.float32),
                pltpu.VMEM((features, width), jnp.float32),
                pltpu.VMEM((2, features, width), low),
                pltpu.SemaphoreType.DMA((2 * blocks,)),
                pltpu.SemaphoreType.DMA((8,)),
            ],
        ),
        out_shape=[acts_shape, acts_shape] + [pair_shape] * 3 + [grad_shape] * 2,
        compiler_params=pltpu.CompilerParams(vmem_limit_bytes=VMEM_ASK),
        cost_estimate=pl.CostEstimate(
            flops=4 * count * most * features * width,
            bytes_accessed=60 * 1024 * 1024,
            transcendentals=count * most * width,
        ),
        name="experts_pass",
    )(starts, rank, gate, *ups, *downs, *rows, *cots)


def tokens_pass(starts, rank, gate, acts, pieces, gated):
    count, blocks, padded, tiles, of_expert, piece_specs = pass_shapes(rank, pieces)
    width = pieces[0].shape[2]
    features = 8 * pieces[0].shape[1]
    most = blocks * SPAN
    low = jnp.bfloat16
    vectors = pl.BlockSpec(rank.shape, lambda expert, starts: (0, 0, 0))
    parts = pl.BlockSpec((blocks // 2, padded, features), lambda expert, starts: (0, 0, 0))
    part_shape = jax.ShapeDtypeStruct((blocks // 2, padded, features), low)
    return pl.pallas_call(
        functools.partial(tokens_kernel, gated),
        grid_spec=pltpu.PrefetchScalarGridSpec(
            num_scalar_prefetch=1,
            grid=(count,),
            in_specs=[vectors, vectors, pl.BlockSpec((1,) + acts.shape[1:], of_expert)]
            + piece_specs,
            out_specs=[parts, parts],
            scratch_shapes=[
                pltpu.VMEM((features, width), low),
                pltpu.VMEM((count, most + TILE, features), low),
                pltpu.VMEM((2, count * SPAN, padded), low),
                pltpu.VMEM((2, count * SPAN, features), low),
            ],
        ),
        out_shape=[part_shape, part_shape],
        compiler_params=pltpu.CompilerParams(vmem_limit_bytes=VMEM_ASK),
        cost_estimate=pl.CostEstimate(
            flops=2 * count * most * features * width,
            bytes_accessed=30 * 1024 * 1024,
            transcendentals=0,
        ),
        name="tokens_gated" if gated else "tokens_plain",
    )(starts, rank, gate, acts, *pieces)


IMAGE = 208


def row_norm(values, factor, offset):
    width = values.shape[1]
    average = jnp.sum(values, axis=1, keepdims=True) / width
    centred = values - average
    spread = jnp.sum(centred * centred, axis=1, keepdims=True) / width
    inverse = lax.rsqrt(spread + norm_epsilon)
    unit = centred * inverse
    return unit * factor + offset, unit, inverse


def row_norm_back(gradient, unit, inverse, factor):
    width = gradient.shape[1]
    inner = gradient * factor
    average = jnp.sum(inner, axis=1, keepdims=True) / width
    along = jnp.sum(inner * unit, axis=1, keepdims=True) / width
    return inverse * (inner - average - unit * along)


def head_soft(query, key, here, keys_used):
    own = jnp.where(here, query, jnp.zeros_like(query))
    scores = dot_nt(own, key) * (HEAD_DIM ** (-0.5))
    scores = jnp.where(keys_used, scores, -1e30)
    powers = jnp.exp(scores - jnp.max(scores, axis=1, keepdims=True))
    return powers / jnp.sum(powers, axis=1, keepdims=True)


def forward_kernel(
    place, tokens, norms, w0, w1, w2, w3, others_near, others_far,
    normed_out, qkv_out, blended_out, residual_out, second_out, weights,
):
    features = tokens.shape[1]
    low = jnp.bfloat16

    chip, core = place[0], place[1]
    depth = features // 8
    others = (others_near.at[0], others_near.at[1], others_far.at[0], others_far.at[1])
    for side, pieces in enumerate(((w0, w1, w2, w3), others)):
        for turn, piece in enumerate(pieces):
            other = jnp.bitwise_xor(chip, turn)
            row = ((other // 2) * 2 + jnp.bitwise_xor(core, side)) * 2 + other % 2
            rows = pl.ds(pl.multiple_of(row * depth, 16), depth)
            for which in range(4):
                weights[which, rows, :] = piece[which]

    normed, unused, unused = row_norm(
        tokens[...].astype(jnp.float32), norms[0:1, :], norms[2:3, :]
    )
    normed_out[...] = normed.astype(low)
    for which in range(3):
        qkv_out[which] = dot_nn(normed_out[...], weights[which]).astype(low)
    keys_used = lax.broadcasted_iota(jnp.int32, (IMAGE, IMAGE), 1) < LEN
    first = lax.broadcasted_iota(jnp.int32, (IMAGE, 2 * HEAD_DIM), 1) < HEAD_DIM

    def attend(image, carry):
        rows = pl.ds(pl.multiple_of(image * IMAGE, 16), IMAGE)
        for start in range(0, features, 2 * HEAD_DIM):
            cols = pl.ds(start, 2 * HEAD_DIM)
            query, key, value = (qkv_out[which, rows, cols] for which in range(3))
            mixed = []
            for here in (first, jnp.logical_not(first)):
                soft = head_soft(query, key, here, keys_used).astype(low)
                mixed.append(dot_nn(soft, value))
            blended_out[rows, cols] = jnp.where(first, mixed[0], mixed[1]).astype(low)
        return carry

    lax.fori_loop(0, tokens.shape[0] // IMAGE, attend, 0)
    residual = tokens[...].astype(jnp.float32) + dot_nn(blended_out[...], weights[3])
    residual_out[...] = residual
    second, unused, unused = row_norm(residual, norms[1:2, :], norms[3:4, :])
    second_out[...] = second.astype(low)


def attention_forward(place, tokens, norms, pieces, others):
    rows, features = tokens.shape
    low = jnp.bfloat16
    vmem = pl.BlockSpec(memory_space=pltpu.VMEM)
    shape = jax.ShapeDtypeStruct((rows, features), low)
    return pl.pallas_call(
        forward_kernel,
        in_specs=[pl.BlockSpec(memory_space=pltpu.SMEM)] + [vmem] * 8,
        out_specs=[vmem] * 6,
        out_shape=[
            shape,
            jax.ShapeDtypeStruct((3, rows, features), low),
            shape,
            jax.ShapeDtypeStruct((rows, features), jnp.float32),
            shape,
            jax.ShapeDtypeStruct((4, features, features), low),
        ],
        compiler_params=pltpu.CompilerParams(vmem_limit_bytes=VMEM_ASK),
        cost_estimate=pl.CostEstimate(
            flops=10 * rows * features * features,
            bytes_accessed=16 * 1024 * 1024,
            transcendentals=0,
        ),
        name="attention_forward",
    )(place, tokens, norms, *pieces, *others)


def backward_kernel(
    place, tokens, cots, residual, blended, normed, qkv, weights, norms,
    second0, second1, second2, second3,
    input_grad, mine, theirs, vectors,
    part, d_heads, d_qkv, d_sum,
):
    rows_all, features = tokens.shape
    low = jnp.bfloat16
    chip, core = place[0], place[1]

    def store_part(which, value):
        part[...] = value
        slab = mine.shape[3]
        y_here, x_here = chip // 2, lax.rem(chip, 2)
        for out, side in ((mine, core), (theirs, 1 - core)):
            for kind in range(4):
                for turn in range(2):
                    if kind < 2:
                        y, x = jnp.bitwise_xor(y_here, turn), jnp.bitwise_xor(x_here, kind)
                    else:
                        y, x = jnp.bitwise_xor(y_here, kind - 2), jnp.bitwise_xor(x_here, turn)
                    row = (((y * 2 + side) * 2 + x) * 2 + kind // 2) * slab
                    rows = pl.ds(pl.multiple_of(row, 16), slab)
                    out[kind, which, turn] = part[rows, :].astype(low)

    d_second = second0[...].astype(jnp.float32)
    for piece in (second1, second2, second3):
        d_second = d_second + piece[...].astype(jnp.float32)
    unused, unit, inverse = row_norm(residual[...], norms[1:2, :], norms[3:4, :])
    vectors[...] = jnp.zeros_like(vectors)
    vectors[1:2, :] = jnp.sum(d_second * unit, axis=0, keepdims=True)
    vectors[3:4, :] = jnp.sum(d_second, axis=0, keepdims=True)
    d_sum[...] = cots[...].astype(jnp.float32) + row_norm_back(
        d_second, unit, inverse, norms[1:2, :]
    )
    d_attended = d_sum[...].astype(low)
    d_heads[...] = dot_nt(d_attended, weights[3]).astype(low)
    store_part(3, dot_tn(blended[...], d_attended))

    keys_used = lax.broadcasted_iota(jnp.int32, (IMAGE, IMAGE), 1) < LEN
    first = lax.broadcasted_iota(jnp.int32, (IMAGE, 2 * HEAD_DIM), 1) < HEAD_DIM
    scale = HEAD_DIM ** (-0.5)

    def attend(image, carry):
        rows = pl.ds(pl.multiple_of(image * IMAGE, 16), IMAGE)
        for start in range(0, features, 2 * HEAD_DIM):
            cols = pl.ds(start, 2 * HEAD_DIM)
            query, key, value = (qkv[which, rows, cols] for which in range(3))
            upper = d_heads[rows, cols]
            found = []
            for here in (first, jnp.logical_not(first)):
                soft = head_soft(query, key, here, keys_used)
                d_soft = dot_nt(jnp.where(here, upper, jnp.zeros_like(upper)), value)
                inner = jnp.sum(soft * d_soft, axis=1, keepdims=True)
                d_scores = (soft * (d_soft - inner)).astype(low)
                found.append(
                    (
                        dot_nn(d_scores, key) * scale,
                        dot_tn(d_scores, query) * scale,
                        dot_tn(soft.astype(low), upper),
                    )
                )
            for which in range(3):
                d_qkv[which, rows, cols] = jnp.where(
                    first, found[0][which], found[1][which]
                ).astype(low)
        return carry

    lax.fori_loop(0, rows_all // IMAGE, attend, 0)
    d_normed = dot_nt(d_qkv[0], weights[0])
    for which in range(1, 3):
        d_normed = d_normed + dot_nt(d_qkv[which], weights[which])
    for which in range(3):
        store_part(which, dot_tn(normed[...], d_qkv[which]))
    unused, unit, inverse = row_norm(
        tokens[...].astype(jnp.float32), norms[0:1, :], norms[2:3, :]
    )
    vectors[0:1, :] = jnp.sum(d_normed * unit, axis=0, keepdims=True)
    vectors[2:3, :] = jnp.sum(d_normed, axis=0, keepdims=True)
    input_grad[...] = d_sum[...] + row_norm_back(d_normed, unit, inverse, norms[0:1, :])


def attention_backward(place, tokens, cots, residual, blended, normed, qkv, seconds, weights, norms):
    rows, features = tokens.shape
    low = jnp.bfloat16
    vmem = pl.BlockSpec(memory_space=pltpu.VMEM)
    half_shape = jax.ShapeDtypeStruct((4, 4, 2, features // 16, features), low)
    return pl.pallas_call(
        backward_kernel,
        in_specs=[pl.BlockSpec(memory_space=pltpu.SMEM)] + [vmem] * 12,
        out_specs=[vmem] * 4,
        scratch_shapes=[
            pltpu.VMEM((features, features), jnp.float32),
            pltpu.VMEM((rows, features), low),
            pltpu.VMEM((3, rows, features), low),
            pltpu.VMEM((rows, features), jnp.float32),
        ],
        out_shape=[
            jax.ShapeDtypeStruct((rows, features), jnp.float32),
            half_shape,
            half_shape,
            jax.ShapeDtypeStruct((8, features), jnp.float32),
        ],
        compiler_params=pltpu.CompilerParams(vmem_limit_bytes=VMEM_ASK),
        cost_estimate=pl.CostEstimate(
            flops=40 * rows * features * features,
            bytes_accessed=24 * 1024 * 1024,
            transcendentals=0,
        ),
        name="attention_backward",
    )(place, tokens, cots, residual, blended, normed, qkv, weights, norms, *seconds)


def route_to(place):
    shards, ctxs, tps = (lax.axis_size(name) for name in axes)
    pairs = []
    for shard in range(shards):
        for ctx in range(ctxs):
            for tp in range(tps):
                other_shard, other_ctx, other_tp = place(shard, ctx, tp)
                pairs.append(
                    (
                        (shard * ctxs + ctx) * tps + tp,
                        (other_shard * ctxs + other_ctx) * tps + other_tp % tps,
                    )
                )
    return pairs


def swap_core(value):
    return lax.ppermute(value, axes, route_to(lambda s, c, t: (s ^ 1, c, t)))


def swap_chip(value, turn):
    return lax.ppermute(
        value, axes, route_to(lambda s, c, t: (s ^ (turn & 2), c ^ (turn & 1), t))
    )


def swap_tp(value, turn):
    return lax.ppermute(value, axes, route_to(lambda s, c, t: (s, c, t ^ turn)))


def pass_on(value):
    return lax.ppermute(value, axes, route_to(lambda s, c, t: (s, c, t + 1)))


def worker_route(source, target):
    shards, ctxs, tps = (lax.axis_size(name) for name in axes)
    pairs = []
    for shard in range(shards):
        for ctx in range(ctxs):
            for worker in range(tps):
                if worker // 2 == shard % 2:
                    base = (shard * ctxs + ctx) * tps
                    pairs.append((base + source(worker) % tps, base + target(worker) % tps))
    return pairs


def to_worker(value, turn):
    return lax.ppermute(value, axes, worker_route(lambda w: w + turn, lambda w: w))


def from_worker(value, turn):
    step = 1 if turn > 0 else -1
    return lax.ppermute(
        value, axes, worker_route(lambda w: w + turn - step, lambda w: w + turn)
    )


def pick(value, index, axis=0):
    return lax.dynamic_index_in_dim(value, index, axis, keepdims=False)


def relative(value, chip):
    return [pick(value, jnp.bitwise_xor(chip, turn)) for turn in range(4)]


def pass_by(value, steps):
    return lax.ppermute(value, axes, route_to(lambda s, c, t: (s, c, t + steps)))


def direct_gather(value):
    return [value] + [pass_by(value, steps) for steps in range(1, lax.axis_size("tp"))]


class Live:
    def __init__(self, values=None):
        vars(self).update(values or {})

    @property
    def drop(self):
        return Drop(vars(self))


class Drop:
    def __init__(self, values):
        self._values = values

    def __getattr__(self, name):
        return self._values.pop(name)


def hold(live):
    return Live(lax.optimization_barrier(vars(live)))


def by_tp(held, tp):
    count = len(held)
    stacked = jnp.stack(held)
    return jnp.stack([pick(stacked, (tp - place) % count) for place in range(count)])


def place_chips(pieces, chip):
    stacked = jnp.stack(pieces)
    return jnp.stack([pick(stacked, jnp.bitwise_xor(chip, place)) for place in range(4)])


def place_cores(own, other, core):
    return jnp.where(core == 0, jnp.stack([own, other]), jnp.stack([other, own]))


def low_dot(spec, left, right):
    return jnp.einsum(
        spec,
        left.astype(jnp.bfloat16),
        right.astype(jnp.bfloat16),
        preferred_element_type=jnp.float32,
    )


def plane_device(
    tokens,
    cotangent,
    routing,
    gating,
    inward,
    outward,
    scales,
    shifts,
    upward,
    downward,
    inward_moment,
    outward_moment,
    scales_moment,
    shifts_moment,
    upward_moment,
    downward_moment,
):
    rows_here = tokens.shape[1]
    features = tokens.shape[2]
    seqs = rows_here // LEN
    experts = upward.shape[0]
    half_experts = experts // 2
    shard = lax.axis_index("shard")
    core = shard % 2
    ctx = lax.axis_index("ctx")
    tp = lax.axis_index("tp")
    tps = lax.axis_size("tp")
    devices = lax.axis_size(axes)
    chip = (shard // 2) * 2 + ctx
    low = jnp.bfloat16
    rows_attn = inward.shape[1]
    rows_local = upward.shape[1]
    cols_local = upward.shape[2]

    v = Live()
    device = jnp.stack([chip, core, tp]).astype(jnp.int32)
    y_here, x_here = shard // 2, ctx
    padded = seqs * IMAGE
    own_tokens, own_cot = (
        jnp.pad(
            value[0].reshape(seqs, LEN, features), ((0, 0), (0, IMAGE - LEN), (0, 0))
        ).reshape(padded, features)
        for value in (tokens, cotangent)
    )

    def halves(value):
        value = value.astype(low).reshape(2, half_experts, rows_local, cols_local)
        return pick(value, core), pick(value, 1 - core)

    def own_order(value):
        return jnp.stack([pick(value, jnp.bitwise_xor(chip, r)) for r in range(4)])

    up_kept, up_sent = halves(upward)
    down_kept, down_sent = halves(downward)
    v.up, v.down = [own_order(up_kept)], [own_order(down_kept)]
    v.up_x, v.down_y = [swap_chip(v.up[0], 1)], [swap_chip(v.down[0], 2)]
    v.column = direct_gather(jnp.concatenate([inward, outward[None]]))
    v.sent = jnp.stack([up_sent, down_sent])
    v.cots = [own_cot]

    packed = jnp.concatenate([routing[0].astype(jnp.float32).T, gating[0].T])
    packed = jnp.pad(
        packed.reshape(4, seqs, LEN), ((0, 0), (0, 0), (0, IMAGE - LEN)), constant_values=-1.0
    )
    norm_rows = jnp.concatenate([scales, shifts]).astype(jnp.float32)
    packed = jnp.concatenate(
        [packed.reshape(4, padded), jnp.pad(norm_rows, ((0, 0), (0, padded - rows_attn)))]
    )
    v.packs = direct_gather(packed)
    v = hold(v)

    column = by_tp(v.drop.column, tp).transpose(1, 0, 2, 3)
    column = column.reshape(4, tps * rows_attn, features)
    v.pieces = [column, swap_chip(column, 1), swap_chip(column, 2)]
    v.cots.append(pass_on(v.cots[-1]))
    v.got = swap_core(v.drop.sent)
    packs = jnp.stack(v.packs)
    v.packs = [packs, swap_core(packs)]
    v = hold(v)

    column, from_x, from_y = v.pieces
    v.far = [swap_chip(from_x[:2], 2), swap_chip(from_y[2:], 1)]
    v.others = [swap_core(jnp.stack(v.pieces[:2]))]
    got = v.drop.got
    v.up.append(own_order(got[0]))
    v.down.append(own_order(got[1]))
    own_packs, other_packs = v.drop.packs
    norms = [by_tp(list(each[:, 4:, :rows_attn]), tp) for each in (own_packs, other_packs)]
    norms = place_cores(*norms, core)
    v.norms = [norms, swap_chip(norms, 1)]
    packs = jnp.concatenate([own_packs, other_packs])
    mine = core * half_experts + jnp.bitwise_xor(chip, jnp.arange(4, dtype=jnp.int32))
    hits = packs[None, :, :2] == mine.astype(jnp.float32)[:, None, None, None]
    chosen = jnp.any(hits, axis=2)
    gate_tok = jnp.sum(jnp.where(hits, packs[None, :, 2:4], 0.0), axis=2)
    places = jnp.arange(padded)
    earlier = (places[:, None] < places[None, :]).astype(low)
    rank = jnp.einsum(
        "rbt,tu->rbu", chosen.astype(low), earlier, preferred_element_type=jnp.float32
    )
    rank = jnp.where(chosen, rank, -1.0).astype(jnp.int32)
    counts = jnp.sum(chosen.astype(jnp.int32), axis=2)
    counts = (counts + 15) // 16 * 16
    starts = jnp.cumsum(jnp.pad(counts, ((0, 0), (1, 0))), axis=1).astype(jnp.int32).reshape(-1)
    v.routes = (jnp.concatenate([starts, device[:2]]), rank, gate_tok)
    v = hold(v)
    far = jnp.concatenate(v.drop.far)
    v.pieces = v.pieces + [far]
    v.others.append(swap_core(jnp.stack(v.pieces[2:])))
    v.cots.append(pass_on(v.cots[-1]))
    v.up_x.append(swap_chip(v.up[1], 1))
    v.down_y.append(swap_chip(v.down[1], 2))
    norms = place_cores(*v.norms, ctx)
    v.norms = [norms, swap_chip(norms, 2)]
    v = hold(v)
    norms = place_cores(*v.drop.norms, y_here)
    norms = norms.transpose(4, 0, 2, 1, 3, 5).reshape(4, features)

    normed, qkv, blended, residual, second, full_weights = attention_forward(
        device, own_tokens, norms, v.drop.pieces, v.drop.others
    )
    v.seconds = [second]
    v.up_xy, v.down_xy = [swap_chip(v.up_x[0], 2)], [swap_chip(v.down_y[0], 1)]
    v.cots.append(pass_on(v.cots[-1]))
    v.cots_other = [swap_core(each) for each in v.cots[:2]]
    v = hold(v)

    v.seconds.append(pass_on(v.seconds[-1]))
    v.up_xy.append(swap_chip(v.up_x[1], 2))
    v.down_xy.append(swap_chip(v.down_y[1], 1))
    v.cots_other += [swap_core(each) for each in v.cots[2:]]
    v = hold(v)
    v.seconds.append(pass_on(v.seconds[-1]))
    v.down_x, v.up_y = [swap_chip(v.down[0], 1)], [swap_chip(v.up[0], 2)]
    v.seconds_other = [swap_core(v.seconds[0])]
    moments = halves(upward_moment) + halves(downward_moment)
    v.moments = moments[0], moments[2], swap_core(jnp.stack([moments[1], moments[3]]))
    v = hold(v)
    v.seconds.append(pass_on(v.seconds[-1]))
    v.down_x.append(swap_chip(v.down[1], 1))
    v.up_y.append(swap_chip(v.up[1], 2))
    v.seconds_other += [swap_core(each) for each in v.seconds[1:3]]
    moments = v.drop.moments
    moments = jnp.stack([moments[0], moments[2][0], moments[1], moments[2][1]])
    v.moments = [pick(moments, jnp.bitwise_xor(chip, turn), 1) for turn in range(4)]
    v = hold(v)
    v.seconds_other.append(swap_core(v.seconds[3]))
    v = hold(v)

    ups = v.drop.up + v.drop.up_x + v.drop.up_y + v.drop.up_xy
    downs = v.drop.down + v.drop.down_x + v.drop.down_y + v.drop.down_xy
    v.moments = [v.moments[0]] + [swap_chip(v.moments[turn], turn) for turn in range(1, 4)]
    hidden, before, v.own, v.near_x, v.near_y, v.far_x, v.far_y = experts_pass(
        *v.routes,
        v.drop.seconds + v.drop.seconds_other,
        v.drop.cots + v.drop.cots_other,
        ups, downs,
    )
    v.hidden, v.before = hidden, before
    v.ups, v.downs = ups, downs
    v = hold(v)

    v.part = tokens_pass(*v.routes, v.drop.before, v.drop.ups, False)
    v.far_x, v.far_y = swap_chip(v.far_x, 1), swap_chip(v.far_y, 2)
    v = hold(v)

    def join(own, other):
        return (own.astype(jnp.float32) + other.astype(jnp.float32)).astype(low)

    v.along_x = v.near_x.at[1].set(join(v.near_x[1], v.drop.far_y))
    v.along_y = v.near_y.at[0].set(join(v.near_y[0], v.drop.far_x))
    v.near_x = v.near_y = None
    v.part = [v.part[0], swap_core(v.part[1])]
    v = hold(v)
    kept = join(*v.drop.part)
    v.along_x, v.along_y = swap_chip(v.along_x, 1), swap_chip(v.along_y, 2)
    v.seconds = [kept[0]] + [pass_by(kept[turn], -turn) for turn in range(1, tps)]
    v.summed = tokens_pass(*v.drop.routes, v.drop.hidden, v.drop.downs, True)
    v = hold(v)

    push, push_next, band0, band1, band2, *rows = push_rows(
        device, v.drop.own, (v.drop.along_x, v.drop.along_y), v.drop.moments
    )
    v.push, v.blocks, v.rows = [push, push_next], [band0, band1, band2], rows
    v.summed = [v.summed[0], swap_core(v.summed[1])]
    v = hold(v)

    def rows_out(rows):
        return [rows[0]] + [swap_chip(rows[turn], turn) for turn in range(1, 4)]

    def rows_between(got):
        got = place_chips(got, chip)
        return pick(got, core, 2), swap_core(pick(got, 1 - core, 2))

    def rows_in(kept, got):
        joined = place_cores(kept, got, core).transpose(2, 0, 1, 3, 4)
        joined = joined.reshape(2, experts, rows_local, cols_local)
        return joined.astype(jnp.float32)

    v.joined = [v.push[0]] + [to_worker(v.push[1], turn) for turn in (1, 3)]
    v.rows = rows_out(v.rows)
    v.input_grad, v.own, v.gone, v.vectors = attention_backward(
        device, own_tokens, own_cot, residual, blended, normed, qkv,
        v.drop.seconds,
        full_weights, norms,
    )
    v = hold(v)

    def added(value, got):
        return value.astype(jnp.float32) + got.astype(jnp.float32)

    v.gone = swap_core(v.gone)
    v.blocks[:2] = [to_worker(block, 2) for block in v.blocks[:2]]
    v.rows = rows_between(v.rows)
    vectors = v.vectors[:4]
    v.vectors = [vectors, swap_core(vectors)]
    input_grad = v.drop.input_grad
    input_grad = input_grad.reshape(seqs, IMAGE, features)[:, :LEN].reshape(rows_here, features)
    mixed = added(*v.summed)
    v.summed = [mixed[0]] + [mixed[turn].astype(low) for turn in range(1, tps)]
    v = hold(v)
    own, gone = v.drop.own, v.drop.gone
    v.first = [added(own[0], gone[0]), swap_chip(added(own[1], gone[1]).astype(low), 1)]
    v.last = [added(own[2], gone[2]), swap_chip(added(own[3], gone[3]).astype(low), 2)]
    v.summed.append(pass_by(v.summed[2], -1))
    vectors = sum(v.vectors)
    v.vectors = [vectors, swap_chip(vectors, 1)]
    v = hold(v)
    first, last = added(*v.first), added(*v.last)
    v.first = [first[:, 0], swap_chip(first[:, 1].astype(low), 2)]
    v.last = [last[:, 0], swap_chip(last[:, 1].astype(low), 1)]
    v.blocks[2] = to_worker(v.blocks[2], 2)
    vectors = sum(v.vectors)
    v.vectors = [vectors, swap_chip(vectors, 2)]
    v = hold(v)

    sums = jnp.concatenate([added(*v.drop.first), added(*v.drop.last)], axis=1)
    sums = sums.reshape(4, tps, rows_attn, features)
    vectors = jnp.pad(sum(v.drop.vectors)[:, None], ((0, 0), (0, 7), (0, 0)))
    parts = [
        jnp.concatenate([pick(sums, (tp - turn) % tps, 1), vectors], axis=1).astype(low)
        for turn in range(tps)
    ]
    v.sums = [parts[0]] + [pass_by(parts[turn], -turn) for turn in range(1, tps)]
    v.mixers = wide_first(v.drop.joined + v.drop.blocks)
    v = hold(v)
    sums = sum(part.astype(jnp.float32) for part in v.drop.sums)
    v.vectors = lax.dynamic_slice(
        sums[:, rows_attn], (0, lax.axis_index(axes) * rows_attn), (4, rows_attn)
    )
    sums = sums[:, :rows_attn]
    inward_grad, outward_grad = sums[:3], sums[3]
    inward_state, inward_push = advance(inward_grad, inward_moment)
    outward_state, outward_push = advance(outward_grad, outward_moment)
    v.column = direct_gather(jnp.concatenate([inward_push, outward_push[None]]).astype(low))
    v.mixers = [wide_last(*v.mixers)]
    v = hold(v)
    column = by_tp(v.drop.column, tp).transpose(1, 0, 2, 3)
    gone = relative(column, chip)
    v.pushes = [gone[0]] + [swap_chip(gone[turn], turn) for turn in range(1, 4)]
    upward_grad, downward_grad = rows_in(*v.drop.rows)
    v.states = [
        (upward_grad, advance(upward_grad, upward_moment)[0]),
        (downward_grad, advance(downward_grad, downward_moment)[0]),
    ]
    v.mixers.append(from_worker(v.mixers[0], 1))
    v.mixers.append(from_worker(v.mixers[0], -1))
    v = hold(v)
    pushes = place_chips(v.pushes, chip)
    v.pushes = [pushes, swap_core(pushes)]
    v.mixers.insert(2, from_worker(v.mixers[1], 2))
    v = hold(v)
    pushes = place_cores(*v.drop.pushes, core)
    pushes = pushes.reshape(2, 2, 2, tps, rows_attn, features).transpose(1, 0, 2, 3, 4, 5)
    v.pushes = pushes.reshape(features, features)
    v.new = apply_mixers(device, v.drop.mixers, v.drop.push, rows_local)
    v = hold(v)

    v.new = rows_out(v.new)
    own_part, next_part, unused, far_part, got = v.summed
    v.summed = [own_part, pass_by(added(next_part, got).astype(low), -1), pass_on(far_part)]
    v.moved = orthogonal_square(v.drop.pushes)
    v = hold(v)
    moved = v.drop.moved.reshape(2, 2, 2, tps, rows_attn, features)
    moved = pick(pick(moved, core, 1), tp, 2).reshape(4, rows_attn, features)
    gone = relative(moved, chip)
    v.moved = [gone[0]] + [swap_chip(gone[turn], turn) for turn in range(1, 4)]
    v.new = rows_between(v.new)
    v = hold(v)
    mixed = v.drop.summed
    result = (residual + mixed[0] + added(mixed[1], mixed[2])).astype(low)
    result = result.reshape(seqs, IMAGE, features)[:, :LEN].reshape(rows_here, features)
    scales_grad, shifts_grad = v.vectors[:2], v.vectors[2:]
    scales_state, scales_push = advance(scales_grad, scales_moment)
    shifts_state, shifts_push = advance(shifts_grad, shifts_moment)
    up_new, down_new = rows_in(*v.new)
    upward_new = upward.astype(jnp.float32) - 2.0 * up_new
    downward_new = downward.astype(jnp.float32) - down_new
    (upward_grad, upward_state), (downward_grad, downward_state) = v.states
    got = place_chips(v.moved, chip).astype(jnp.float32)
    inward_new = inward.astype(jnp.float32) - got[:3]
    outward_new = outward.astype(jnp.float32) - got[3]
    vector_rate = 0.6 / math.sqrt(devices * rows_here)
    scales_new = scales.astype(jnp.float32) - vector_rate * scales_push
    shifts_new = shifts.astype(jnp.float32) - vector_rate * shifts_push
    return (
        result[None],
        input_grad[None],
        inward_grad,
        outward_grad,
        scales_grad,
        shifts_grad,
        upward_grad,
        downward_grad,
        inward_state,
        outward_state,
        scales_state,
        shifts_state,
        upward_state,
        downward_state,
        inward_new,
        outward_new,
        scales_new,
        shifts_new,
        upward_new,
        downward_new,
    )


def solution(mesh):
    in_specs = (
        P(("shard", "tp"), "ctx", None),
        P(("shard", "tp"), "ctx", None),
        P(("shard", "tp"), "ctx", None),
        P(("shard", "tp"), "ctx", None),
        P(None, ("shard", "ctx", "tp"), None),
        P(("shard", "ctx", "tp"), None),
        P(None, ("shard", "ctx", "tp")),
        P(None, ("shard", "ctx", "tp")),
        P(None, ("shard", "ctx"), "tp"),
        P(None, ("shard", "ctx"), "tp"),
        P(None, ("shard", "ctx", "tp"), None),
        P(("shard", "ctx", "tp"), None),
        P(None, ("shard", "ctx", "tp")),
        P(None, ("shard", "ctx", "tp")),
        P(None, ("shard", "ctx"), "tp"),
        P(None, ("shard", "ctx"), "tp"),
    )
    out_specs = (
        P(("shard", "tp"), "ctx", None),
        P(("shard", "tp"), "ctx", None),
        P(None, ("shard", "ctx", "tp"), None),
        P(("shard", "ctx", "tp"), None),
        P(None, ("shard", "ctx", "tp")),
        P(None, ("shard", "ctx", "tp")),
        P(None, ("shard", "ctx"), "tp"),
        P(None, ("shard", "ctx"), "tp"),
        P(None, ("shard", "ctx", "tp"), None),
        P(("shard", "ctx", "tp"), None),
        P(None, ("shard", "ctx", "tp")),
        P(None, ("shard", "ctx", "tp")),
        P(None, ("shard", "ctx"), "tp"),
        P(None, ("shard", "ctx"), "tp"),
        P(None, ("shard", "ctx", "tp"), None),
        P(("shard", "ctx", "tp"), None),
        P(None, ("shard", "ctx", "tp")),
        P(None, ("shard", "ctx", "tp")),
        P(None, ("shard", "ctx"), "tp"),
        P(None, ("shard", "ctx"), "tp"),
    )
    body = plane_device if mesh.shape["shard"] == 4 and mesh.shape["ctx"] == 2 and mesh.shape["tp"] == 4 else on_device
    return jax.shard_map(
        body, mesh=mesh, in_specs=in_specs, out_specs=out_specs, check_vma=False
    )
```

```python
import functools
import math

import jax
import jax.numpy as jnp
import numpy as np
from jax import lax
from jax.experimental import pallas as pl
from jax.experimental.pallas import tpu as pltpu
from jax.sharding import PartitionSpec as P

HEAD_DIM = 64
LEN = 197


first_coef = 3.4445
second_coef = -4.775
third_coef = 2.0315
momentum_decay = 0.9
norm_epsilon = 1e-06
orth_epsilon = 1e-07
highest = lax.Precision.HIGHEST


def normalize(values, factor, offset):
    average = jnp.mean(values, axis=-1, keepdims=True)
    centred = values - average
    inverse = lax.rsqrt(jnp.mean(centred * centred, axis=-1, keepdims=True) + norm_epsilon)
    unit_rows = centred * inverse
    return (unit_rows * factor + offset, unit_rows, inverse)


def normalize_back(gradient, unit_rows, inverse, factor):
    inner = gradient * factor
    average = jnp.mean(inner, axis=-1, keepdims=True)
    along = jnp.mean(inner * unit_rows, axis=-1, keepdims=True)
    back = inverse * (inner - average - unit_rows * along)
    return (back, jnp.sum(gradient * unit_rows, axis=0), jnp.sum(gradient, axis=0))


def slot_sources(routes, experts, capacity):
    pairs = routes.shape[0] * routes.shape[1]
    chosen = routes.reshape(pairs)
    onehot = (chosen[:, None] == jnp.arange(experts, dtype=jnp.int32)[None, :]).astype(jnp.int32)
    earlier = jnp.cumsum(onehot, axis=0) - onehot
    placed = jnp.sum(earlier * onehot, axis=1) + chosen * capacity
    matches = placed[None, :] == jnp.arange(experts * capacity, dtype=jnp.int32)[:, None]
    source = jnp.sum(jnp.where(matches, jnp.arange(pairs, dtype=jnp.int32)[None, :], 0), axis=1)
    filled = jnp.any(matches, axis=1)
    return (placed, source, filled)


def orthogonal(matrix):
    summed = jnp.sqrt(jnp.sum(matrix * matrix))
    current = matrix / (summed + orth_epsilon)
    for repeat in range(5):
        square = lax.dot_general(
            current,
            current,
            (((1,), (1,)), ((), ())),
            precision=highest,
            preferred_element_type=jnp.float32,
        )
        power = jnp.dot(square, square, precision=highest, preferred_element_type=jnp.float32)
        mixer = second_coef * square + third_coef * power
        current = first_coef * current + jnp.dot(
            mixer, current, precision=highest, preferred_element_type=jnp.float32
        )
    return current


def advance(gradient, moment):
    current = momentum_decay * moment + (1.0 - momentum_decay) * gradient
    return (current, (1.0 - momentum_decay) * gradient + momentum_decay * current)


def expert_weights(upward, downward):
    return (
        lax.all_gather(upward, ("shard", "ctx"), axis=1, tiled=True),
        lax.all_gather(downward, ("shard", "ctx"), axis=1, tiled=True),
    )


def on_device(
    tokens,
    cotangent,
    routing,
    gating,
    inward,
    outward,
    scales,
    shifts,
    upward,
    downward,
    inward_moment,
    outward_moment,
    scales_moment,
    shifts_moment,
    upward_moment,
    downward_moment,
):
    rows_here = tokens.shape[1]
    features = tokens.shape[2]
    experts = upward.shape[0]
    top_count = routing.shape[2]
    capacity = 2 * top_count * rows_here // experts
    attn_scale = HEAD_DIM ** (-0.5)
    inputs = tokens[0].astype(jnp.float32)
    routes = routing[0]
    gate_pairs = gating[0].reshape(-1)
    zero_low = jnp.zeros((), jnp.bfloat16)
    full_in, full_out, all_scales, all_shifts = (
        lax.all_gather(inward, ("shard", "ctx", "tp"), axis=1, tiled=True),
        lax.all_gather(outward, ("shard", "ctx", "tp"), axis=0, tiled=True),
        lax.all_gather(scales, ("shard", "ctx", "tp"), axis=1, tiled=True),
        lax.all_gather(shifts, ("shard", "ctx", "tp"), axis=1, tiled=True),
    )
    factor = all_scales.astype(jnp.float32)
    offset = all_shifts.astype(jnp.float32)
    normed, unit_one, inverse_one = normalize(inputs, factor[0], offset[0])
    normed_low = normed.astype(jnp.bfloat16)
    projected = jnp.einsum(
        "td,kde->kte", normed_low, full_in, preferred_element_type=jnp.float32
    ).astype(jnp.bfloat16)
    head_rows = lax.all_to_all(projected, "ctx", split_axis=2, concat_axis=1, tiled=True)
    group_rows = head_rows.shape[1]
    head_width = head_rows.shape[2]
    seqs_here = group_rows // LEN
    shaped = head_rows.reshape(3, seqs_here, LEN, head_width // HEAD_DIM, HEAD_DIM)
    query_rows, key_rows, value_rows = (shaped[0], shaped[1], shaped[2])
    scores = (
        jnp.einsum("sqhd,skhd->shqk", query_rows, key_rows, preferred_element_type=jnp.float32)
        * attn_scale
    )
    top_score = jnp.max(scores, axis=-1, keepdims=True)
    logsum = top_score + jnp.log(jnp.sum(jnp.exp(scores - top_score), axis=-1, keepdims=True))
    soft_low = jnp.exp(scores - logsum).astype(jnp.bfloat16)
    blended = jnp.einsum(
        "shqk,skhd->sqhd", soft_low, value_rows, preferred_element_type=jnp.float32
    ).astype(jnp.bfloat16)
    blended_tokens = lax.all_to_all(
        blended.reshape(group_rows, head_width), "ctx", split_axis=0, concat_axis=1, tiled=True
    )
    residual = inputs + jnp.dot(blended_tokens, full_out, preferred_element_type=jnp.float32)
    second, unit_two, inverse_two = normalize(residual, factor[1], offset[1])
    second_low = second.astype(jnp.bfloat16)
    upstream = cotangent[0].astype(jnp.float32)
    placed, source, filled = slot_sources(routes, experts, capacity)
    slot_rows = jnp.where(filled[:, None], second_low[source // top_count], zero_low)
    slot_rows = slot_rows.reshape(experts, capacity, features)
    group_slots = lax.all_gather(slot_rows, "tp", axis=1, tiled=True)
    upper_full, lower_full = expert_weights(upward, downward)
    before = jnp.einsum("ecd,edf->ecf", group_slots, upper_full, preferred_element_type=jnp.float32)
    hidden = jax.nn.gelu(before).astype(jnp.bfloat16)
    partial_out = jnp.einsum("ecf,edf->ecd", hidden, lower_full, preferred_element_type=jnp.float32)
    own_out = lax.psum_scatter(
        partial_out.astype(jnp.bfloat16), "tp", scatter_dimension=1, tiled=True
    ).astype(jnp.float32)
    picked = own_out.reshape(experts * capacity, features)[placed].reshape(
        rows_here, top_count, features
    )
    mixture = jnp.sum(picked * gating[0][:, :, None], axis=1)
    result = (residual + mixture).astype(jnp.bfloat16)
    slot_grad = jnp.where(
        filled[:, None], upstream[source // top_count] * gate_pairs[source][:, None], 0.0
    )
    slot_grad = slot_grad.astype(jnp.bfloat16).reshape(experts, capacity, features)
    group_grad = lax.all_gather(slot_grad, "tp", axis=1, tiled=True)
    upper_full, lower_full = expert_weights(upward, downward)
    d_hidden = jnp.einsum(
        "ecd,edf->ecf", group_grad, lower_full, preferred_element_type=jnp.float32
    )
    unused, gelu_back = jax.vjp(jax.nn.gelu, before)
    d_before = gelu_back(d_hidden)[0].astype(jnp.bfloat16)
    lower_part = jnp.einsum("ecd,ecf->edf", group_grad, hidden, preferred_element_type=jnp.float32)
    upper_part = jnp.einsum(
        "ecd,ecf->edf", group_slots, d_before, preferred_element_type=jnp.float32
    )
    slot_input_part = jnp.einsum(
        "ecf,edf->ecd", d_before, upper_full, preferred_element_type=jnp.float32
    )
    slot_input = lax.psum_scatter(
        slot_input_part.astype(jnp.bfloat16), "tp", scatter_dimension=1, tiled=True
    ).astype(jnp.float32)
    d_second = jnp.sum(
        slot_input.reshape(experts * capacity, features)[placed].reshape(
            rows_here, top_count, features
        ),
        axis=1,
    )
    d_norm_two, scale_two, shift_two = normalize_back(d_second, unit_two, inverse_two, factor[1])
    d_residual = upstream + d_norm_two
    d_attended = d_residual.astype(jnp.bfloat16)
    outward_part = jnp.einsum(
        "td,te->de", blended_tokens, d_attended, preferred_element_type=jnp.float32
    )
    d_blended = jnp.einsum(
        "te,de->td", d_attended, full_out, preferred_element_type=jnp.float32
    ).astype(jnp.bfloat16)
    d_heads = lax.all_to_all(d_blended, "ctx", split_axis=1, concat_axis=0, tiled=True)
    d_heads = d_heads.reshape(seqs_here, LEN, head_width // HEAD_DIM, HEAD_DIM)
    soft_full = jnp.exp(
        jnp.einsum("sqhd,skhd->shqk", query_rows, key_rows, preferred_element_type=jnp.float32)
        * attn_scale
        - logsum
    )
    d_soft = jnp.einsum("sqhd,skhd->shqk", d_heads, value_rows, preferred_element_type=jnp.float32)
    value_grad = jnp.einsum(
        "shqk,sqhd->skhd", soft_low, d_heads, preferred_element_type=jnp.float32
    ).astype(jnp.bfloat16)
    row_inner = jnp.sum(soft_full * d_soft, axis=-1, keepdims=True)
    d_scores = (soft_full * (d_soft - row_inner)).astype(jnp.bfloat16)
    query_grad = (
        jnp.einsum("shqk,skhd->sqhd", d_scores, key_rows, preferred_element_type=jnp.float32)
        * attn_scale
    ).astype(jnp.bfloat16)
    key_grad = (
        jnp.einsum("shqk,sqhd->skhd", d_scores, query_rows, preferred_element_type=jnp.float32)
        * attn_scale
    ).astype(jnp.bfloat16)
    stacked_grad = jnp.stack([query_grad, key_grad, value_grad]).reshape(3, group_rows, head_width)
    token_grad = lax.all_to_all(stacked_grad, "ctx", split_axis=1, concat_axis=2, tiled=True)
    inward_part = jnp.einsum(
        "td,kte->kde", normed_low, token_grad, preferred_element_type=jnp.float32
    )
    d_normed = jnp.einsum("kte,kde->td", token_grad, full_in, preferred_element_type=jnp.float32)
    d_norm_one, scale_one, shift_one = normalize_back(d_normed, unit_one, inverse_one, factor[0])
    input_grad = d_residual + d_norm_one
    inward_grad, outward_grad, scales_grad, shifts_grad = (
        lax.psum_scatter(inward_part, ("shard", "ctx", "tp"), scatter_dimension=1, tiled=True),
        lax.psum_scatter(outward_part, ("shard", "ctx", "tp"), scatter_dimension=0, tiled=True),
        lax.psum_scatter(
            jnp.stack([scale_one, scale_two]),
            ("shard", "ctx", "tp"),
            scatter_dimension=1,
            tiled=True,
        ),
        lax.psum_scatter(
            jnp.stack([shift_one, shift_two]),
            ("shard", "ctx", "tp"),
            scatter_dimension=1,
            tiled=True,
        ),
    )
    upward_grad, downward_grad = (
        lax.psum_scatter(
            upper_part.astype(jnp.bfloat16), ("shard", "ctx"), scatter_dimension=1, tiled=True
        ).astype(jnp.float32),
        lax.psum_scatter(
            lower_part.astype(jnp.bfloat16), ("shard", "ctx"), scatter_dimension=1, tiled=True
        ).astype(jnp.float32),
    )
    inward_state, inward_push = advance(inward_grad, inward_moment)
    outward_state, outward_push = advance(outward_grad, outward_moment)
    scales_state, scales_push = advance(scales_grad, scales_moment)
    shifts_state, shifts_push = advance(shifts_grad, shifts_moment)
    upward_state, upward_push = advance(upward_grad, upward_moment)
    downward_state, downward_push = advance(downward_grad, downward_moment)
    devices = lax.axis_size(("shard", "ctx", "tp"))
    outer_count = lax.axis_size(("shard", "ctx"))
    inner_count = lax.axis_size("tp")
    rows_local = upward.shape[1]
    cols_local = upward.shape[2]
    slot_size = rows_local * cols_local
    attention_size = inward.shape[1] * features
    full_cols = inner_count * cols_local

    def flat_pad(portion):
        flatten = portion.reshape(portion.shape[0], -1)
        return jnp.pad(flatten, ((0, 0), (0, slot_size - flatten.shape[1])))

    matrices = jnp.concatenate(
        [
            flat_pad(inward_push),
            flat_pad(outward_push[None]),
            upward_push.reshape(experts, slot_size),
            downward_push.reshape(experts, slot_size),
        ]
    )
    matrix_count = matrices.shape[0]
    owner_table = np.arange(matrix_count) * devices // matrix_count
    outgoing = jnp.zeros((devices, slot_size), jnp.float32).at[owner_table].set(matrices)
    received = lax.all_to_all(
        outgoing.astype(jnp.bfloat16),
        ("shard", "ctx", "tp"),
        split_axis=0,
        concat_axis=0,
        tiled=True,
    ).astype(outgoing.dtype)
    myself = lax.axis_index(("shard", "ctx", "tp"))
    owned = (
        jnp.sum(
            jnp.where(
                jnp.asarray(owner_table, dtype=jnp.int32) == myself,
                jnp.arange(matrix_count, dtype=jnp.int32) + 1,
                0,
            )
        )
        - 1
    )
    attention_kind = jnp.logical_and(owned >= 0, owned < 4)
    expert_form = (
        received.reshape(outer_count, inner_count, rows_local, cols_local)
        .transpose(0, 2, 1, 3)
        .reshape(features, full_cols)
    )
    attention_form = jnp.pad(
        received[:, :attention_size].reshape(features, features),
        ((0, 0), (0, full_cols - features)),
    )
    orthogonal_form = orthogonal(jnp.where(attention_kind, attention_form, expert_form))
    back_expert = (
        orthogonal_form.reshape(outer_count, rows_local, inner_count, cols_local)
        .transpose(0, 2, 1, 3)
        .reshape(devices, slot_size)
    )
    back_attention = jnp.pad(
        orthogonal_form[:, :features].reshape(devices, attention_size),
        ((0, 0), (0, slot_size - attention_size)),
    )
    returned = lax.all_to_all(
        jnp.where(attention_kind, back_attention, back_expert).astype(jnp.bfloat16),
        ("shard", "ctx", "tp"),
        split_axis=0,
        concat_axis=0,
        tiled=True,
    ).astype(jnp.float32)
    mine_parts = returned[owner_table]
    inward_new = inward.astype(jnp.float32) - mine_parts[:3, :attention_size].reshape(inward.shape)
    outward_new = outward.astype(jnp.float32) - mine_parts[3, :attention_size].reshape(
        outward.shape
    )
    upward_new = upward.astype(jnp.float32) - 2.0 * mine_parts[4 : 4 + experts].reshape(
        upward.shape
    )
    downward_new = downward.astype(jnp.float32) - mine_parts[4 + experts :].reshape(downward.shape)
    total_tokens = lax.axis_size("shard") * lax.axis_size("ctx") * lax.axis_size("tp") * rows_here
    vector_rate = 0.6 / math.sqrt(total_tokens)
    scales_new = scales.astype(jnp.float32) - vector_rate * scales_push
    shifts_new = shifts.astype(jnp.float32) - vector_rate * shifts_push
    return (
        result[None],
        input_grad[None],
        inward_grad,
        outward_grad,
        scales_grad,
        shifts_grad,
        upward_grad,
        downward_grad,
        inward_state,
        outward_state,
        scales_state,
        shifts_state,
        upward_state,
        downward_state,
        inward_new,
        outward_new,
        scales_new,
        shifts_new,
        upward_new,
        downward_new,
    )


axes = ("shard", "ctx", "tp")
TILE = 256
SPAN = 208
VMEM_ASK = 60 * 1024 * 1024


def dot_nn(left, right):
    return lax.dot_general(
        left, right, (((1,), (0,)), ((), ())), preferred_element_type=jnp.float32
    )


def dot_nt(left, right):
    return lax.dot_general(
        left, right, (((1,), (1,)), ((), ())), preferred_element_type=jnp.float32
    )


def dot_tn(left, right):
    return lax.dot_general(
        left, right, (((0,), (0,)), ((), ())), preferred_element_type=jnp.float32
    )


def tile_pairs(count):
    return [(row, col) for row in range(count) for col in range(row, count)]


def wide_bands(size):
    return [pl.ds(start, TILE) for start in range(0, size, TILE)]


def wide_steps(count, gram, whole, low, whole_low, mixer):
    bands = wide_bands(gram.shape[0])

    def step(repeat, carry):
        wide_mix(gram, whole, low, whole_low, mixer)
        for band in bands:
            half = first_coef * gram[band, :] + dot_nn(mixer[band, :], low[...])
            gram[band, :] = first_coef * half + dot_nn(half.astype(jnp.bfloat16), mixer[...])
            whole[band, :] = first_coef * whole[band, :] + dot_nn(mixer[band, :], whole_low[...])
        return carry

    lax.fori_loop(0, count, step, 0)


def wide_mix(gram, whole, low, whole_low, mixer):
    low[...] = gram[...].astype(jnp.bfloat16)
    whole_low[...] = whole[...].astype(jnp.bfloat16)
    for band in wide_bands(gram.shape[0]):
        squared = dot_nn(low[band, :], low[...])
        mixer[band, :] = (second_coef * gram[band, :] + third_coef * squared).astype(jnp.bfloat16)


def wide_first_kernel(block0, block1, block3, part0, part1, part2, gram, whole, low, mixer, whole_low, block2):
    size = gram.shape[0]
    bands = wide_bands(size)
    rows = lax.broadcasted_iota(jnp.int32, (TILE, size), 0)
    cols = lax.broadcasted_iota(jnp.int32, (TILE, size), 1)
    for part, band in zip((part0, part1, part2), bands):
        block2[band, :] = part[...]
    trace = 0.0
    for place, band in enumerate(bands):
        part = dot_nt(block0[band, :], block0[...])
        for block in (block1, block2, block3):
            part = part + dot_nt(block[band, :], block[...])
        gram[band, :] = part
        trace = trace + jnp.sum(jnp.where(rows + place * TILE == cols, part, 0.0))
    factor = 1.0 / (jnp.sqrt(trace) + orth_epsilon)
    for place, band in enumerate(bands):
        gram[band, :] = gram[band, :] * (factor * factor)
        whole[band, :] = jnp.where(rows + place * TILE == cols, factor, 0.0)
    wide_mix(gram, whole, low, whole_low, mixer)
    for band in bands:
        half = first_coef * gram[band, :] + dot_nn(mixer[band, :], low[...])
        gram[band, :] = first_coef * half + dot_nn(half.astype(jnp.bfloat16), mixer[...])
        whole[band, :] = first_coef * whole[band, :] + factor * mixer[band, :].astype(jnp.float32)
    wide_steps(1, gram, whole, low, whole_low, mixer)


def wide_last_kernel(gram_in, whole_in, out, gram, whole, low, mixer, whole_low):
    bands = wide_bands(gram.shape[0])
    gram[...] = gram_in[...]
    whole[...] = whole_in[...]
    wide_steps(2, gram, whole, low, whole_low, mixer)
    wide_mix(gram, whole, low, whole_low, mixer)
    for row, band in enumerate(bands):
        last = first_coef * whole[band, :] + dot_nn(mixer[band, :], whole_low[...])
        for place, pair in enumerate(tile_pairs(len(bands))):
            if pair[0] == row:
                out[place] = last[:, pair[1] * TILE : (pair[1] + 1) * TILE].astype(out.dtype)


def wide_call(kernel, size, out_shape, kept, scratch, name, inputs):
    vmem = pl.BlockSpec(memory_space=pltpu.VMEM)
    square = (size, size)
    return pl.pallas_call(
        kernel,
        out_shape=out_shape,
        in_specs=[vmem] * len(inputs),
        out_specs=jax.tree.map(lambda shape: vmem, out_shape),
        scratch_shapes=[pltpu.VMEM(square, jnp.float32)] * kept
        + [pltpu.VMEM(square, jnp.bfloat16)] * scratch,
        compiler_params=pltpu.CompilerParams(vmem_limit_bytes=VMEM_ASK),
        cost_estimate=pl.CostEstimate(
            flops=20 * size**3, bytes_accessed=8 * size * size, transcendentals=0
        ),
        name=name,
    )(*inputs)


def wide_first(blocks):
    size = blocks[0].shape[0]
    shape = jax.ShapeDtypeStruct((size, size), jnp.float32)
    return wide_call(wide_first_kernel, size, [shape, shape], 0, 4, "wide_first", blocks)


def wide_last(gram, whole):
    size = gram.shape[0]
    pairs = len(tile_pairs(size // TILE))
    shape = jax.ShapeDtypeStruct((pairs, TILE, TILE), jnp.bfloat16)
    return wide_call(wide_last_kernel, size, shape, 2, 3, "wide_last", (gram, whole))


def store_rows(chip, value, outs, which):
    depth = outs[0].shape[2]
    for turn, out in enumerate(outs):
        other = jnp.bitwise_xor(chip, turn)
        for core in range(2):
            row = ((other // 2) * 2 + core) * 2 + other % 2
            out[which, core] = value[pl.ds(pl.multiple_of(row * depth, 16), depth), :].astype(
                out.dtype
            )


def apply_kernel(place, *refs):
    mixers, pushes, outs, (full, moved) = refs[:4], refs[4:6], refs[6:10], refs[10:]
    chip, core, tp = place[0], place[1], place[2]
    count = full.shape[0] // TILE
    for which in range(2):
        source = lax.rem(tp - 2 * core - which + 4, 4)
        for step in range(4):

            @pl.when(source == step)
            def _():
                for spot, (row, col) in enumerate(tile_pairs(count)):
                    tile = mixers[step][spot]
                    full[pl.ds(row * TILE, TILE), pl.ds(col * TILE, TILE)] = tile
                    if row != col:
                        full[pl.ds(col * TILE, TILE), pl.ds(row * TILE, TILE)] = tile.T

        for spot in range(2):

            @pl.when(lax.rem(tp + spot, 2) == which)
            def _():
                moved[...] = dot_nn(full[...], pushes[spot][...])

        store_rows(chip, moved, outs, which)


def apply_mixers(place, mixers, pushes, depth):
    size, width = pushes[0].shape
    vmem = pl.BlockSpec(memory_space=pltpu.VMEM)
    shape = jax.ShapeDtypeStruct((2, 2, depth, width), jnp.bfloat16)
    return pl.pallas_call(
        apply_kernel,
        in_specs=[pl.BlockSpec(memory_space=pltpu.SMEM)] + [vmem] * 6,
        out_specs=[vmem] * 4,
        out_shape=[shape] * 4,
        scratch_shapes=[
            pltpu.VMEM((size, size), jnp.bfloat16),
            pltpu.VMEM((size, width), jnp.float32),
        ],
        compiler_params=pltpu.CompilerParams(vmem_limit_bytes=VMEM_ASK),
        cost_estimate=pl.CostEstimate(
            flops=4 * size**3, bytes_accessed=10 * size * size, transcendentals=0
        ),
        name="apply_mixers",
    )(place, *mixers, *pushes)


def push_kernel(place, own, *refs):
    gots, moments, refs = refs[:2], refs[2:6], refs[6:]
    pushes, bands, outs, (total,) = refs[:2], refs[2:5], refs[5:9], refs[9:]
    chip, core, tp = place[0], place[1], place[2]
    keep = 1.0 - momentum_decay
    depth = outs[0].shape[2]
    for which in range(2):
        total[...] = (
            own[which].astype(jnp.float32)
            + gots[0][which].astype(jnp.float32)
            + gots[1][which].astype(jnp.float32)
        )
        store_rows(chip, total, outs, which)
        for turn, moment in enumerate(moments):
            other = jnp.bitwise_xor(chip, turn)
            for side in range(2):
                row = ((other // 2) * 2 + jnp.bitwise_xor(core, side)) * 2 + other % 2
                rows = pl.ds(pl.multiple_of(row * depth, 16), depth)
                pushed = (
                    (keep + momentum_decay * keep) * total[rows, :]
                    + momentum_decay * momentum_decay * moment[2 * which + side].astype(jnp.float32)
                ).astype(jnp.bfloat16)
                for spot in range(2):

                    @pl.when(lax.rem(tp + spot, 2) == which)
                    def _():
                        pushes[spot][rows, :] = pushed

    for place, band in enumerate(bands):
        band[...] = pushes[0][pl.ds(place * TILE, TILE), :]


def push_rows(place, own, gots, moments):
    size, width = own.shape[1:]
    depth = moments[0].shape[1]
    vmem = pl.BlockSpec(memory_space=pltpu.VMEM)
    rows = jax.ShapeDtypeStruct((2, 2, depth, width), jnp.bfloat16)
    return pl.pallas_call(
        push_kernel,
        in_specs=[pl.BlockSpec(memory_space=pltpu.SMEM)] + [vmem] * 7,
        out_specs=[vmem] * 9,
        out_shape=[jax.ShapeDtypeStruct((size, width), jnp.bfloat16)] * 2
        + [jax.ShapeDtypeStruct((TILE, width), jnp.bfloat16)] * 3
        + [rows] * 4,
        scratch_shapes=[pltpu.VMEM((size, width), jnp.float32)],
        compiler_params=pltpu.CompilerParams(vmem_limit_bytes=VMEM_ASK),
        cost_estimate=pl.CostEstimate(
            flops=20 * size * width, bytes_accessed=24 * size * width, transcendentals=0
        ),
        name="push_rows",
    )(place, own, *gots, *moments)


def square_kernel(matrix, out, current, low, square, square_low, mixer):
    size = current.shape[0]
    bands = [pl.ds(start, TILE) for start in range(0, size, TILE)]
    total = 0.0
    for band in bands:
        part = matrix[band, :].astype(jnp.float32)
        total = total + jnp.sum(part * part)
    factor = 1.0 / (jnp.sqrt(total) + orth_epsilon)
    for band in bands:
        current[band, :] = matrix[band, :].astype(jnp.float32) * factor

    def step(repeat, carry):
        low[...] = current[...].astype(jnp.bfloat16)
        for band in bands:
            part = dot_nt(low[band, :], low[...])
            square[band, :] = part
            square_low[band, :] = part.astype(jnp.bfloat16)
        for band in bands:
            mixed = second_coef * square[band, :] + third_coef * dot_nn(
                square_low[band, :], square_low[...]
            )
            mixer[band, :] = mixed.astype(jnp.bfloat16)
        for band in bands:
            current[band, :] = first_coef * current[band, :] + dot_nn(mixer[band, :], low[...])
        return carry

    lax.fori_loop(0, 5, step, 0)
    out[...] = current[...].astype(out.dtype)


def orthogonal_square(matrix):
    size = matrix.shape[0]
    return pl.pallas_call(
        square_kernel,
        out_shape=jax.ShapeDtypeStruct((size, size), jnp.bfloat16),
        in_specs=[pl.BlockSpec(memory_space=pltpu.VMEM)],
        out_specs=pl.BlockSpec(memory_space=pltpu.VMEM),
        scratch_shapes=[
            pltpu.VMEM((size, size), jnp.float32),
            pltpu.VMEM((size, size), jnp.bfloat16),
            pltpu.VMEM((size, size), jnp.float32),
            pltpu.VMEM((size, size), jnp.bfloat16),
            pltpu.VMEM((size, size), jnp.bfloat16),
        ],
        compiler_params=pltpu.CompilerParams(vmem_limit_bytes=VMEM_ASK),
        cost_estimate=pl.CostEstimate(
            flops=30 * size**3, bytes_accessed=4 * matrix.size, transcendentals=0
        ),
        name="square_orthogonal",
    )(matrix)


root = math.sqrt(2.0 / math.pi)


def gelu_pair(value):
    squared = value * value
    part = 0.5 * jnp.tanh(value * (root + (root * 0.044715) * squared)) + 0.5
    bend = value * (2.0 * root + (6.0 * root * 0.044715) * squared)
    return value * part, part + part * (1.0 - part) * bend


def one_hot(rank):
    return lax.broadcasted_iota(jnp.int32, (SPAN, rank.shape[1]), 0) == rank


def assemble(chip, core, pieces, whole):
    depth = pieces[0].shape[1]
    for place, piece in enumerate(pieces):
        other = jnp.bitwise_xor(chip, place // 2)
        row = ((other // 2) * 2 + jnp.bitwise_xor(core, place % 2)) * 2 + other % 2
        whole[pl.ds(pl.multiple_of(row * depth, 16), depth), :] = piece[0]


def each_band(count, work):
    wide = (count + 127) // 512

    def step(place, carry):
        work(pl.ds(pl.multiple_of(place * 512, 512), 512))
        return carry

    lax.fori_loop(0, wide, step, 0)
    rest = count - wide * 512
    start = wide * 512

    @pl.when(rest > 128)
    def _():
        work(pl.ds(pl.multiple_of(start, 512), 256))

    @pl.when(jnp.logical_or(rest > 256, jnp.logical_and(rest > 0, rest <= 128)))
    def _():
        work(pl.ds(pl.multiple_of(start + jnp.where(rest > 256, 256, 0), 128), 128))


def gate_of(hot, gate):
    return jnp.sum(jnp.where(hot, gate, 0.0), axis=1, keepdims=True)


def experts_kernel(
    starts, rank, gate, *refs
):
    blocks = rank.shape[1]
    ups, downs, refs = refs[:8], refs[8:16], refs[16:]
    tokens_hbm, refs = refs[: 2 * blocks], refs[2 * blocks :]
    hidden_out, before_out, *refs = refs
    outs, refs = refs[:5], refs[5:]
    rows, cots, upper, lower, slots, grads, upper_sum, lower_sum, leaving, sems, out_sems = refs
    targets = [(outs[turn].at[0], outs[turn].at[1]) for turn in range(3)] + [(outs[3], outs[4])]
    expert = pl.program_id(0)
    base = expert * (blocks + 1)
    chip = starts[pl.num_programs(0) * (blocks + 1)]
    core = starts[pl.num_programs(0) * (blocks + 1) + 1]
    low = jnp.bfloat16

    @pl.when(expert == 0)
    def _():
        copies = []
        for block in range(blocks):
            for which, held in enumerate((rows, cots)):
                place = which * blocks + block
                copies.append(
                    pltpu.make_async_copy(tokens_hbm[place], held.at[block], sems.at[place])
                )
        for copy in copies:
            copy.start()

    assemble(chip, core, ups, upper)
    assemble(chip, core, downs, lower)

    for block in range(blocks):

        @pl.when(expert == 0)
        def _():
            for which, held in enumerate((rows, cots)):
                place = which * blocks + block
                pltpu.make_async_copy(tokens_hbm[place], held.at[block], sems.at[place]).wait()

        start = pl.multiple_of(starts[base + block], 16)
        hot = one_hot(rank[0, block : block + 1, :])
        spread = jnp.where(hot, 1.0, 0.0).astype(low)
        weight = gate_of(hot, gate[0, block : block + 1, :])
        slots[pl.ds(start, SPAN), :] = dot_nn(spread, rows[block]).astype(low)
        grads[pl.ds(start, SPAN), :] = (dot_nn(spread, cots[block]) * weight).astype(low)

    end = pl.multiple_of(starts[base + blocks], 16)
    slots[pl.ds(end, TILE), :] = jnp.zeros((TILE, slots.shape[1]), low)
    grads[pl.ds(end, TILE), :] = jnp.zeros((TILE, slots.shape[1]), low)
    upper_sum[...] = jnp.zeros_like(upper_sum)
    lower_sum[...] = jnp.zeros_like(lower_sum)

    def work(band):
        slot_rows, slot_grads = slots[band, :], grads[band, :]
        hidden, slope = gelu_pair(dot_nn(slot_rows, upper[...]))
        hidden = hidden.astype(low)
        d_before = (dot_nn(slot_grads, lower[...]) * slope).astype(low)
        hidden_out[0, band, :] = hidden
        before_out[0, band, :] = d_before
        upper_sum[...] += dot_tn(slot_rows, d_before)
        lower_sum[...] += dot_tn(slot_grads, hidden)

    each_band(starts[base + blocks], work)

    for turn, target in enumerate(targets):

        @pl.when(expert == turn)
        def _():
            if turn > 0:
                for which in range(2):
                    pltpu.make_async_copy(
                        leaving.at[which], targets[turn - 1][which], out_sems.at[2 * turn - 2 + which]
                    ).wait()
            leaving[0] = upper_sum[...].astype(low)
            leaving[1] = lower_sum[...].astype(low)
            copies = [
                pltpu.make_async_copy(leaving.at[which], target[which], out_sems.at[2 * turn + which])
                for which in range(2)
            ]
            for copy in copies:
                copy.start()
            if turn == 3:
                for copy in copies:
                    copy.wait()


def tokens_kernel(
    gated, starts, rank, gate, acts, *refs
):
    pieces, (part_own, part_other, whole, moved, spread, found) = refs[:8], refs[8:]
    expert = pl.program_id(0)
    count, blocks = rank.shape[0], rank.shape[1]
    base = expert * (blocks + 1)
    chip, core = starts[count * (blocks + 1)], starts[count * (blocks + 1) + 1]
    low = jnp.bfloat16

    @pl.when(expert == 0)
    def _():
        moved[...] = jnp.zeros_like(moved)

    assemble(chip, core, pieces, whole)

    def work(band):
        moved[expert, band, :] = dot_nt(acts[0, band, :], whole[...]).astype(low)

    each_band(starts[base + blocks], work)

    @pl.when(expert == count - 1)
    def _():
        for side, part in enumerate((part_own, part_other)):
            for place in range(blocks // 2):
                block = side * (blocks // 2) + place
                ways, rows_of = spread.at[place % 2], found.at[place % 2]
                for each in range(count):
                    start = pl.multiple_of(starts[each * (blocks + 1) + block], 16)
                    hot = one_hot(rank[each, block : block + 1, :])
                    rows = moved[each, pl.ds(start, SPAN), :]
                    if gated:
                        weight = gate_of(hot, gate[each, block : block + 1, :])
                        rows = (rows.astype(jnp.float32) * weight).astype(low)
                    band = pl.ds(each * SPAN, SPAN)
                    ways[band, :] = jnp.where(hot, 1.0, 0.0).astype(low)
                    rows_of[band, :] = rows
                part[place] = dot_tn(ways[...], rows_of[...]).astype(low)


def pass_shapes(rank, pieces):
    count = pieces[0].shape[0]
    blocks, padded = rank.shape[1], rank.shape[2]
    tiles = -(-blocks * SPAN // TILE)

    def of_expert(expert, starts):
        return (expert, 0, 0)

    piece_specs = [
        pl.BlockSpec(
            (1,) + pieces[0].shape[1:],
            lambda expert, starts, turn=place // 2: (jnp.bitwise_xor(expert, turn), 0, 0),
        )
        for place in range(8)
    ]
    return count, blocks, padded, tiles, of_expert, piece_specs


def experts_pass(starts, rank, gate, rows, cots, ups, downs):
    count, blocks, padded, tiles, of_expert, piece_specs = pass_shapes(rank, ups)
    features = rows[0].shape[1]
    width = ups[0].shape[2]
    most = blocks * SPAN
    low = jnp.bfloat16
    vectors = pl.BlockSpec((1, blocks, padded), of_expert)
    acts = pl.BlockSpec((1, tiles * TILE, width), of_expert)
    acts_shape = jax.ShapeDtypeStruct((count, tiles * TILE, width), low)
    grad_shape = jax.ShapeDtypeStruct((features, width), low)
    pair_shape = jax.ShapeDtypeStruct((2, features, width), low)
    return pl.pallas_call(
        experts_kernel,
        grid_spec=pltpu.PrefetchScalarGridSpec(
            num_scalar_prefetch=1,
            grid=(count,),
            in_specs=[vectors, vectors]
            + piece_specs * 2
            + [pl.BlockSpec(memory_space=pl.ANY)] * (2 * blocks),
            out_specs=[acts, acts] + [pl.BlockSpec(memory_space=pl.ANY)] * 5,
            scratch_shapes=[
                pltpu.VMEM((blocks, padded, features), low),
                pltpu.VMEM((blocks, padded, features), low),
                pltpu.VMEM((features, width), low),
                pltpu.VMEM((features, width), low),
                pltpu.VMEM((most + TILE, features), low),
                pltpu.VMEM((most + TILE, features), low),
                pltpu.VMEM((features, width), jnp.float32),
                pltpu.VMEM((features, width), jnp.float32),
                pltpu.VMEM((2, features, width), low),
                pltpu.SemaphoreType.DMA((2 * blocks,)),
                pltpu.SemaphoreType.DMA((8,)),
            ],
        ),
        out_shape=[acts_shape, acts_shape] + [pair_shape] * 3 + [grad_shape] * 2,
        compiler_params=pltpu.CompilerParams(vmem_limit_bytes=VMEM_ASK),
        cost_estimate=pl.CostEstimate(
            flops=4 * count * most * features * width,
            bytes_accessed=60 * 1024 * 1024,
            transcendentals=count * most * width,
        ),
        name="experts_pass",
    )(starts, rank, gate, *ups, *downs, *rows, *cots)


def tokens_pass(starts, rank, gate, acts, pieces, gated):
    count, blocks, padded, tiles, of_expert, piece_specs = pass_shapes(rank, pieces)
    width = pieces[0].shape[2]
    features = 8 * pieces[0].shape[1]
    most = blocks * SPAN
    low = jnp.bfloat16
    vectors = pl.BlockSpec(rank.shape, lambda expert, starts: (0, 0, 0))
    parts = pl.BlockSpec((blocks // 2, padded, features), lambda expert, starts: (0, 0, 0))
    part_shape = jax.ShapeDtypeStruct((blocks // 2, padded, features), low)
    return pl.pallas_call(
        functools.partial(tokens_kernel, gated),
        grid_spec=pltpu.PrefetchScalarGridSpec(
            num_scalar_prefetch=1,
            grid=(count,),
            in_specs=[vectors, vectors, pl.BlockSpec((1,) + acts.shape[1:], of_expert)]
            + piece_specs,
            out_specs=[parts, parts],
            scratch_shapes=[
                pltpu.VMEM((features, width), low),
                pltpu.VMEM((count, most + TILE, features), low),
                pltpu.VMEM((2, count * SPAN, padded), low),
                pltpu.VMEM((2, count * SPAN, features), low),
            ],
        ),
        out_shape=[part_shape, part_shape],
        compiler_params=pltpu.CompilerParams(vmem_limit_bytes=VMEM_ASK),
        cost_estimate=pl.CostEstimate(
            flops=2 * count * most * features * width,
            bytes_accessed=30 * 1024 * 1024,
            transcendentals=0,
        ),
        name="tokens_gated" if gated else "tokens_plain",
    )(starts, rank, gate, acts, *pieces)


IMAGE = 208


def row_norm(values, factor, offset):
    width = values.shape[1]
    average = jnp.sum(values, axis=1, keepdims=True) / width
    centred = values - average
    spread = jnp.sum(centred * centred, axis=1, keepdims=True) / width
    inverse = lax.rsqrt(spread + norm_epsilon)
    unit = centred * inverse
    return unit * factor + offset, unit, inverse


def row_norm_back(gradient, unit, inverse, factor):
    width = gradient.shape[1]
    inner = gradient * factor
    average = jnp.sum(inner, axis=1, keepdims=True) / width
    along = jnp.sum(inner * unit, axis=1, keepdims=True) / width
    return inverse * (inner - average - unit * along)


def head_soft(query, key, here, keys_used):
    own = jnp.where(here, query, jnp.zeros_like(query))
    scores = dot_nt(own, key) * (HEAD_DIM ** (-0.5))
    scores = jnp.where(keys_used, scores, -1e30)
    powers = jnp.exp(scores - jnp.max(scores, axis=1, keepdims=True))
    return powers / jnp.sum(powers, axis=1, keepdims=True)


def forward_kernel(
    place, tokens, norms, w0, w1, w2, w3, others_near, others_far,
    normed_out, qkv_out, blended_out, residual_out, second_out, weights,
):
    features = tokens.shape[1]
    low = jnp.bfloat16

    chip, core = place[0], place[1]
    depth = features // 8
    others = (others_near.at[0], others_near.at[1], others_far.at[0], others_far.at[1])
    for side, pieces in enumerate(((w0, w1, w2, w3), others)):
        for turn, piece in enumerate(pieces):
            other = jnp.bitwise_xor(chip, turn)
            row = ((other // 2) * 2 + jnp.bitwise_xor(core, side)) * 2 + other % 2
            rows = pl.ds(pl.multiple_of(row * depth, 16), depth)
            for which in range(4):
                weights[which, rows, :] = piece[which]

    normed, unused, unused = row_norm(
        tokens[...].astype(jnp.float32), norms[0:1, :], norms[2:3, :]
    )
    normed_out[...] = normed.astype(low)
    for which in range(3):
        qkv_out[which] = dot_nn(normed_out[...], weights[which]).astype(low)
    keys_used = lax.broadcasted_iota(jnp.int32, (IMAGE, IMAGE), 1) < LEN
    first = lax.broadcasted_iota(jnp.int32, (IMAGE, 2 * HEAD_DIM), 1) < HEAD_DIM

    def attend(image, carry):
        rows = pl.ds(pl.multiple_of(image * IMAGE, 16), IMAGE)
        for start in range(0, features, 2 * HEAD_DIM):
            cols = pl.ds(start, 2 * HEAD_DIM)
            query, key, value = (qkv_out[which, rows, cols] for which in range(3))
            mixed = []
            for here in (first, jnp.logical_not(first)):
                soft = head_soft(query, key, here, keys_used).astype(low)
                mixed.append(dot_nn(soft, value))
            blended_out[rows, cols] = jnp.where(first, mixed[0], mixed[1]).astype(low)
        return carry

    lax.fori_loop(0, tokens.shape[0] // IMAGE, attend, 0)
    residual = tokens[...].astype(jnp.float32) + dot_nn(blended_out[...], weights[3])
    residual_out[...] = residual
    second, unused, unused = row_norm(residual, norms[1:2, :], norms[3:4, :])
    second_out[...] = second.astype(low)


def attention_forward(place, tokens, norms, pieces, others):
    rows, features = tokens.shape
    low = jnp.bfloat16
    vmem = pl.BlockSpec(memory_space=pltpu.VMEM)
    shape = jax.ShapeDtypeStruct((rows, features), low)
    return pl.pallas_call(
        forward_kernel,
        in_specs=[pl.BlockSpec(memory_space=pltpu.SMEM)] + [vmem] * 8,
        out_specs=[vmem] * 6,
        out_shape=[
            shape,
            jax.ShapeDtypeStruct((3, rows, features), low),
            shape,
            jax.ShapeDtypeStruct((rows, features), jnp.float32),
            shape,
            jax.ShapeDtypeStruct((4, features, features), low),
        ],
        compiler_params=pltpu.CompilerParams(vmem_limit_bytes=VMEM_ASK),
        cost_estimate=pl.CostEstimate(
            flops=10 * rows * features * features,
            bytes_accessed=16 * 1024 * 1024,
            transcendentals=0,
        ),
        name="attention_forward",
    )(place, tokens, norms, *pieces, *others)


def backward_kernel(
    place, tokens, cots, residual, blended, normed, qkv, weights, norms,
    second0, second1, second2, second3,
    input_grad, mine, theirs, vectors,
    part, d_heads, d_qkv, d_sum,
):
    rows_all, features = tokens.shape
    low = jnp.bfloat16
    chip, core = place[0], place[1]

    def store_part(which, value):
        part[...] = value
        slab = mine.shape[3]
        y_here, x_here = chip // 2, lax.rem(chip, 2)
        for out, side in ((mine, core), (theirs, 1 - core)):
            for kind in range(4):
                for turn in range(2):
                    if kind < 2:
                        y, x = jnp.bitwise_xor(y_here, turn), jnp.bitwise_xor(x_here, kind)
                    else:
                        y, x = jnp.bitwise_xor(y_here, kind - 2), jnp.bitwise_xor(x_here, turn)
                    row = (((y * 2 + side) * 2 + x) * 2 + kind // 2) * slab
                    rows = pl.ds(pl.multiple_of(row, 16), slab)
                    out[kind, which, turn] = part[rows, :].astype(low)

    d_second = second0[...].astype(jnp.float32)
    for piece in (second1, second2, second3):
        d_second = d_second + piece[...].astype(jnp.float32)
    unused, unit, inverse = row_norm(residual[...], norms[1:2, :], norms[3:4, :])
    vectors[...] = jnp.zeros_like(vectors)
    vectors[1:2, :] = jnp.sum(d_second * unit, axis=0, keepdims=True)
    vectors[3:4, :] = jnp.sum(d_second, axis=0, keepdims=True)
    d_sum[...] = cots[...].astype(jnp.float32) + row_norm_back(
        d_second, unit, inverse, norms[1:2, :]
    )
    d_attended = d_sum[...].astype(low)
    d_heads[...] = dot_nt(d_attended, weights[3]).astype(low)
    store_part(3, dot_tn(blended[...], d_attended))

    keys_used = lax.broadcasted_iota(jnp.int32, (IMAGE, IMAGE), 1) < LEN
    first = lax.broadcasted_iota(jnp.int32, (IMAGE, 2 * HEAD_DIM), 1) < HEAD_DIM
    scale = HEAD_DIM ** (-0.5)

    def attend(image, carry):
        rows = pl.ds(pl.multiple_of(image * IMAGE, 16), IMAGE)
        for start in range(0, features, 2 * HEAD_DIM):
            cols = pl.ds(start, 2 * HEAD_DIM)
            query, key, value = (qkv[which, rows, cols] for which in range(3))
            upper = d_heads[rows, cols]
            found = []
            for here in (first, jnp.logical_not(first)):
                soft = head_soft(query, key, here, keys_used)
                d_soft = dot_nt(jnp.where(here, upper, jnp.zeros_like(upper)), value)
                inner = jnp.sum(soft * d_soft, axis=1, keepdims=True)
                d_scores = (soft * (d_soft - inner)).astype(low)
                found.append(
                    (
                        dot_nn(d_scores, key) * scale,
                        dot_tn(d_scores, query) * scale,
                        dot_tn(soft.astype(low), upper),
                    )
                )
            for which in range(3):
                d_qkv[which, rows, cols] = jnp.where(
                    first, found[0][which], found[1][which]
                ).astype(low)
        return carry

    lax.fori_loop(0, rows_all // IMAGE, attend, 0)
    d_normed = dot_nt(d_qkv[0], weights[0])
    for which in range(1, 3):
        d_normed = d_normed + dot_nt(d_qkv[which], weights[which])
    for which in range(3):
        store_part(which, dot_tn(normed[...], d_qkv[which]))
    unused, unit, inverse = row_norm(
        tokens[...].astype(jnp.float32), norms[0:1, :], norms[2:3, :]
    )
    vectors[0:1, :] = jnp.sum(d_normed * unit, axis=0, keepdims=True)
    vectors[2:3, :] = jnp.sum(d_normed, axis=0, keepdims=True)
    input_grad[...] = d_sum[...] + row_norm_back(d_normed, unit, inverse, norms[0:1, :])


def attention_backward(place, tokens, cots, residual, blended, normed, qkv, seconds, weights, norms):
    rows, features = tokens.shape
    low = jnp.bfloat16
    vmem = pl.BlockSpec(memory_space=pltpu.VMEM)
    half_shape = jax.ShapeDtypeStruct((4, 4, 2, features // 16, features), low)
    return pl.pallas_call(
        backward_kernel,
        in_specs=[pl.BlockSpec(memory_space=pltpu.SMEM)] + [vmem] * 12,
        out_specs=[vmem] * 4,
        scratch_shapes=[
            pltpu.VMEM((features, features), jnp.float32),
            pltpu.VMEM((rows, features), low),
            pltpu.VMEM((3, rows, features), low),
            pltpu.VMEM((rows, features), jnp.float32),
        ],
        out_shape=[
            jax.ShapeDtypeStruct((rows, features), jnp.float32),
            half_shape,
            half_shape,
            jax.ShapeDtypeStruct((8, features), jnp.float32),
        ],
        compiler_params=pltpu.CompilerParams(vmem_limit_bytes=VMEM_ASK),
        cost_estimate=pl.CostEstimate(
            flops=40 * rows * features * features,
            bytes_accessed=24 * 1024 * 1024,
            transcendentals=0,
        ),
        name="attention_backward",
    )(place, tokens, cots, residual, blended, normed, qkv, weights, norms, *seconds)


def route_to(place):
    shards, ctxs, tps = (lax.axis_size(name) for name in axes)
    pairs = []
    for shard in range(shards):
        for ctx in range(ctxs):
            for tp in range(tps):
                other_shard, other_ctx, other_tp = place(shard, ctx, tp)
                pairs.append(
                    (
                        (shard * ctxs + ctx) * tps + tp,
                        (other_shard * ctxs + other_ctx) * tps + other_tp % tps,
                    )
                )
    return pairs


def swap_core(value):
    return lax.ppermute(value, axes, route_to(lambda s, c, t: (s ^ 1, c, t)))


def swap_chip(value, turn):
    return lax.ppermute(
        value, axes, route_to(lambda s, c, t: (s ^ (turn & 2), c ^ (turn & 1), t))
    )


def swap_tp(value, turn):
    return lax.ppermute(value, axes, route_to(lambda s, c, t: (s, c, t ^ turn)))


def pass_on(value):
    return lax.ppermute(value, axes, route_to(lambda s, c, t: (s, c, t + 1)))


def worker_route(source, target):
    shards, ctxs, tps = (lax.axis_size(name) for name in axes)
    pairs = []
    for shard in range(shards):
        for ctx in range(ctxs):
            for worker in range(tps):
                if worker // 2 == shard % 2:
                    base = (shard * ctxs + ctx) * tps
                    pairs.append((base + source(worker) % tps, base + target(worker) % tps))
    return pairs


def to_worker(value, turn):
    return lax.ppermute(value, axes, worker_route(lambda w: w + turn, lambda w: w))


def from_worker(value, turn):
    step = 1 if turn > 0 else -1
    return lax.ppermute(
        value, axes, worker_route(lambda w: w + turn - step, lambda w: w + turn)
    )


def pick(value, index, axis=0):
    return lax.dynamic_index_in_dim(value, index, axis, keepdims=False)


def relative(value, chip):
    return [pick(value, jnp.bitwise_xor(chip, turn)) for turn in range(4)]


def pass_by(value, steps):
    return lax.ppermute(value, axes, route_to(lambda s, c, t: (s, c, t + steps)))


def direct_gather(value):
    return [value] + [pass_by(value, steps) for steps in range(1, lax.axis_size("tp"))]


class Live:
    def __init__(self, values=None):
        vars(self).update(values or {})

    @property
    def drop(self):
        return Drop(vars(self))


class Drop:
    def __init__(self, values):
        self._values = values

    def __getattr__(self, name):
        return self._values.pop(name)


def hold(live):
    return Live(lax.optimization_barrier(vars(live)))


def by_tp(held, tp):
    count = len(held)
    stacked = jnp.stack(held)
    return jnp.stack([pick(stacked, (tp - place) % count) for place in range(count)])


def place_chips(pieces, chip):
    stacked = jnp.stack(pieces)
    return jnp.stack([pick(stacked, jnp.bitwise_xor(chip, place)) for place in range(4)])


def place_cores(own, other, core):
    return jnp.where(core == 0, jnp.stack([own, other]), jnp.stack([other, own]))


def low_dot(spec, left, right):
    return jnp.einsum(
        spec,
        left.astype(jnp.bfloat16),
        right.astype(jnp.bfloat16),
        preferred_element_type=jnp.float32,
    )


def plane_device(
    tokens,
    cotangent,
    routing,
    gating,
    inward,
    outward,
    scales,
    shifts,
    upward,
    downward,
    inward_moment,
    outward_moment,
    scales_moment,
    shifts_moment,
    upward_moment,
    downward_moment,
):
    rows_here = tokens.shape[1]
    features = tokens.shape[2]
    seqs = rows_here // LEN
    experts = upward.shape[0]
    half_experts = experts // 2
    shard = lax.axis_index("shard")
    core = shard % 2
    ctx = lax.axis_index("ctx")
    tp = lax.axis_index("tp")
    tps = lax.axis_size("tp")
    devices = lax.axis_size(axes)
    chip = (shard // 2) * 2 + ctx
    low = jnp.bfloat16
    rows_attn = inward.shape[1]
    rows_local = upward.shape[1]
    cols_local = upward.shape[2]

    v = Live()
    device = jnp.stack([chip, core, tp]).astype(jnp.int32)
    y_here, x_here = shard // 2, ctx
    padded = seqs * IMAGE
    own_tokens, own_cot = (
        jnp.pad(
            value[0].reshape(seqs, LEN, features), ((0, 0), (0, IMAGE - LEN), (0, 0))
        ).reshape(padded, features)
        for value in (tokens, cotangent)
    )

    def halves(value):
        value = value.astype(low).reshape(2, half_experts, rows_local, cols_local)
        return pick(value, core), pick(value, 1 - core)

    def own_order(value):
        return jnp.stack([pick(value, jnp.bitwise_xor(chip, r)) for r in range(4)])

    up_kept, up_sent = halves(upward)
    down_kept, down_sent = halves(downward)
    v.up, v.down = [own_order(up_kept)], [own_order(down_kept)]
    v.up_x, v.down_y = [swap_chip(v.up[0], 1)], [swap_chip(v.down[0], 2)]
    v.column = direct_gather(jnp.concatenate([inward, outward[None]]))
    v.sent = jnp.stack([up_sent, down_sent])
    v.cots = [own_cot]

    packed = jnp.concatenate([routing[0].astype(jnp.float32).T, gating[0].T])
    packed = jnp.pad(
        packed.reshape(4, seqs, LEN), ((0, 0), (0, 0), (0, IMAGE - LEN)), constant_values=-1.0
    )
    norm_rows = jnp.concatenate([scales, shifts]).astype(jnp.float32)
    packed = jnp.concatenate(
        [packed.reshape(4, padded), jnp.pad(norm_rows, ((0, 0), (0, padded - rows_attn)))]
    )
    v.packs = direct_gather(packed)
    v = hold(v)

    column = by_tp(v.drop.column, tp).transpose(1, 0, 2, 3)
    column = column.reshape(4, tps * rows_attn, features)
    v.pieces = [column, swap_chip(column, 1), swap_chip(column, 2)]
    v.cots.append(pass_on(v.cots[-1]))
    v.got = swap_core(v.drop.sent)
    packs = jnp.stack(v.packs)
    v.packs = [packs, swap_core(packs)]
    v = hold(v)

    column, from_x, from_y = v.pieces
    v.far = [swap_chip(from_x[:2], 2), swap_chip(from_y[2:], 1)]
    v.others = [swap_core(jnp.stack(v.pieces[:2]))]
    got = v.drop.got
    v.up.append(own_order(got[0]))
    v.down.append(own_order(got[1]))
    own_packs, other_packs = v.drop.packs
    norms = [by_tp(list(each[:, 4:, :rows_attn]), tp) for each in (own_packs, other_packs)]
    norms = place_cores(*norms, core)
    v.norms = [norms, swap_chip(norms, 1)]
    packs = jnp.concatenate([own_packs, other_packs])
    mine = core * half_experts + jnp.bitwise_xor(chip, jnp.arange(4, dtype=jnp.int32))
    hits = packs[None, :, :2] == mine.astype(jnp.float32)[:, None, None, None]
    chosen = jnp.any(hits, axis=2)
    gate_tok = jnp.sum(jnp.where(hits, packs[None, :, 2:4], 0.0), axis=2)
    places = jnp.arange(padded)
    earlier = (places[:, None] < places[None, :]).astype(low)
    rank = jnp.einsum(
        "rbt,tu->rbu", chosen.astype(low), earlier, preferred_element_type=jnp.float32
    )
    rank = jnp.where(chosen, rank, -1.0).astype(jnp.int32)
    counts = jnp.sum(chosen.astype(jnp.int32), axis=2)
    counts = (counts + 15) // 16 * 16
    starts = jnp.cumsum(jnp.pad(counts, ((0, 0), (1, 0))), axis=1).astype(jnp.int32).reshape(-1)
    v.routes = (jnp.concatenate([starts, device[:2]]), rank, gate_tok)
    v = hold(v)
    far = jnp.concatenate(v.drop.far)
    v.pieces = v.pieces + [far]
    v.others.append(swap_core(jnp.stack(v.pieces[2:])))
    v.cots.append(pass_on(v.cots[-1]))
    v.up_x.append(swap_chip(v.up[1], 1))
    v.down_y.append(swap_chip(v.down[1], 2))
    norms = place_cores(*v.norms, ctx)
    v.norms = [norms, swap_chip(norms, 2)]
    v = hold(v)
    norms = place_cores(*v.drop.norms, y_here)
    norms = norms.transpose(4, 0, 2, 1, 3, 5).reshape(4, features)

    normed, qkv, blended, residual, second, full_weights = attention_forward(
        device, own_tokens, norms, v.drop.pieces, v.drop.others
    )
    v.seconds = [second]
    v.up_xy, v.down_xy = [swap_chip(v.up_x[0], 2)], [swap_chip(v.down_y[0], 1)]
    v.cots.append(pass_on(v.cots[-1]))
    v.cots_other = [swap_core(each) for each in v.cots[:2]]
    v = hold(v)

    v.seconds.append(pass_on(v.seconds[-1]))
    v.up_xy.append(swap_chip(v.up_x[1], 2))
    v.down_xy.append(swap_chip(v.down_y[1], 1))
    v.cots_other += [swap_core(each) for each in v.cots[2:]]
    v = hold(v)
    v.seconds.append(pass_on(v.seconds[-1]))
    v.down_x, v.up_y = [swap_chip(v.down[0], 1)], [swap_chip(v.up[0], 2)]
    v.seconds_other = [swap_core(v.seconds[0])]
    moments = halves(upward_moment) + halves(downward_moment)
    v.moments = moments[0], moments[2], swap_core(jnp.stack([moments[1], moments[3]]))
    v = hold(v)
    v.seconds.append(pass_on(v.seconds[-1]))
    v.down_x.append(swap_chip(v.down[1], 1))
    v.up_y.append(swap_chip(v.up[1], 2))
    v.seconds_other += [swap_core(each) for each in v.seconds[1:3]]
    moments = v.drop.moments
    moments = jnp.stack([moments[0], moments[2][0], moments[1], moments[2][1]])
    v.moments = [pick(moments, jnp.bitwise_xor(chip, turn), 1) for turn in range(4)]
    v = hold(v)
    v.seconds_other.append(swap_core(v.seconds[3]))
    v = hold(v)

    ups = v.drop.up + v.drop.up_x + v.drop.up_y + v.drop.up_xy
    downs = v.drop.down + v.drop.down_x + v.drop.down_y + v.drop.down_xy
    v.moments = [v.moments[0]] + [swap_chip(v.moments[turn], turn) for turn in range(1, 4)]
    hidden, before, v.own, v.near_x, v.near_y, v.far_x, v.far_y = experts_pass(
        *v.routes,
        v.drop.seconds + v.drop.seconds_other,
        v.drop.cots + v.drop.cots_other,
        ups, downs,
    )
    v.hidden, v.before = hidden, before
    v.ups, v.downs = ups, downs
    v = hold(v)

    v.part = tokens_pass(*v.routes, v.drop.before, v.drop.ups, False)
    v.far_x, v.far_y = swap_chip(v.far_x, 1), swap_chip(v.far_y, 2)
    v = hold(v)

    def join(own, other):
        return (own.astype(jnp.float32) + other.astype(jnp.float32)).astype(low)

    v.along_x = v.near_x.at[1].set(join(v.near_x[1], v.drop.far_y))
    v.along_y = v.near_y.at[0].set(join(v.near_y[0], v.drop.far_x))
    v.near_x = v.near_y = None
    v.part = [v.part[0], swap_core(v.part[1])]
    v = hold(v)
    kept = join(*v.drop.part)
    v.along_x, v.along_y = swap_chip(v.along_x, 1), swap_chip(v.along_y, 2)
    v.seconds = [kept[0]] + [pass_by(kept[turn], -turn) for turn in range(1, tps)]
    v.summed = tokens_pass(*v.drop.routes, v.drop.hidden, v.drop.downs, True)
    v = hold(v)

    push, push_next, band0, band1, band2, *rows = push_rows(
        device, v.drop.own, (v.drop.along_x, v.drop.along_y), v.drop.moments
    )
    v.push, v.blocks, v.rows = [push, push_next], [band0, band1, band2], rows
    v.summed = [v.summed[0], swap_core(v.summed[1])]
    v = hold(v)

    def rows_out(rows):
        return [rows[0]] + [swap_chip(rows[turn], turn) for turn in range(1, 4)]

    def rows_between(got):
        got = place_chips(got, chip)
        return pick(got, core, 2), swap_core(pick(got, 1 - core, 2))

    def rows_in(kept, got):
        joined = place_cores(kept, got, core).transpose(2, 0, 1, 3, 4)
        joined = joined.reshape(2, experts, rows_local, cols_local)
        return joined.astype(jnp.float32)

    v.joined = [v.push[0]] + [to_worker(v.push[1], turn) for turn in (1, 3)]
    v.rows = rows_out(v.rows)
    v.input_grad, v.own, v.gone, v.vectors = attention_backward(
        device, own_tokens, own_cot, residual, blended, normed, qkv,
        v.drop.seconds,
        full_weights, norms,
    )
    v = hold(v)

    def added(value, got):
        return value.astype(jnp.float32) + got.astype(jnp.float32)

    v.gone = swap_core(v.gone)
    v.blocks[:2] = [to_worker(block, 2) for block in v.blocks[:2]]
    v.rows = rows_between(v.rows)
    vectors = v.vectors[:4]
    v.vectors = [vectors, swap_core(vectors)]
    input_grad = v.drop.input_grad
    input_grad = input_grad.reshape(seqs, IMAGE, features)[:, :LEN].reshape(rows_here, features)
    mixed = added(*v.summed)
    v.summed = [mixed[0]] + [mixed[turn].astype(low) for turn in range(1, tps)]
    v = hold(v)
    own, gone = v.drop.own, v.drop.gone
    v.first = [added(own[0], gone[0]), swap_chip(added(own[1], gone[1]).astype(low), 1)]
    v.last = [added(own[2], gone[2]), swap_chip(added(own[3], gone[3]).astype(low), 2)]
    v.summed.append(pass_by(v.summed[2], -1))
    vectors = sum(v.vectors)
    v.vectors = [vectors, swap_chip(vectors, 1)]
    v = hold(v)
    first, last = added(*v.first), added(*v.last)
    v.first = [first[:, 0], swap_chip(first[:, 1].astype(low), 2)]
    v.last = [last[:, 0], swap_chip(last[:, 1].astype(low), 1)]
    v.blocks[2] = to_worker(v.blocks[2], 2)
    vectors = sum(v.vectors)
    v.vectors = [vectors, swap_chip(vectors, 2)]
    v = hold(v)

    sums = jnp.concatenate([added(*v.drop.first), added(*v.drop.last)], axis=1)
    sums = sums.reshape(4, tps, rows_attn, features)
    vectors = jnp.pad(sum(v.drop.vectors)[:, None], ((0, 0), (0, 7), (0, 0)))
    parts = [
        jnp.concatenate([pick(sums, (tp - turn) % tps, 1), vectors], axis=1).astype(low)
        for turn in range(tps)
    ]
    v.sums = [parts[0]] + [pass_by(parts[turn], -turn) for turn in range(1, tps)]
    v.mixers = wide_first(v.drop.joined + v.drop.blocks)
    v = hold(v)
    sums = sum(part.astype(jnp.float32) for part in v.drop.sums)
    v.vectors = lax.dynamic_slice(
        sums[:, rows_attn], (0, lax.axis_index(axes) * rows_attn), (4, rows_attn)
    )
    sums = sums[:, :rows_attn]
    inward_grad, outward_grad = sums[:3], sums[3]
    inward_state, inward_push = advance(inward_grad, inward_moment)
    outward_state, outward_push = advance(outward_grad, outward_moment)
    v.column = direct_gather(jnp.concatenate([inward_push, outward_push[None]]).astype(low))
    v.mixers = [wide_last(*v.mixers)]
    v = hold(v)
    column = by_tp(v.drop.column, tp).transpose(1, 0, 2, 3)
    gone = relative(column, chip)
    v.pushes = [gone[0]] + [swap_chip(gone[turn], turn) for turn in range(1, 4)]
    upward_grad, downward_grad = rows_in(*v.drop.rows)
    v.states = [
        (upward_grad, advance(upward_grad, upward_moment)[0]),
        (downward_grad, advance(downward_grad, downward_moment)[0]),
    ]
    v.mixers.append(from_worker(v.mixers[0], 1))
    v.mixers.append(from_worker(v.mixers[0], -1))
    v = hold(v)
    pushes = place_chips(v.pushes, chip)
    v.pushes = [pushes, swap_core(pushes)]
    v.mixers.insert(2, from_worker(v.mixers[1], 2))
    v = hold(v)
    pushes = place_cores(*v.drop.pushes, core)
    pushes = pushes.reshape(2, 2, 2, tps, rows_attn, features).transpose(1, 0, 2, 3, 4, 5)
    v.pushes = pushes.reshape(features, features)
    v.new = apply_mixers(device, v.drop.mixers, v.drop.push, rows_local)
    v = hold(v)

    v.new = rows_out(v.new)
    own_part, next_part, unused, far_part, got = v.summed
    v.summed = [own_part, pass_by(added(next_part, got).astype(low), -1), pass_on(far_part)]
    v.moved = orthogonal_square(v.drop.pushes)
    v = hold(v)
    moved = v.drop.moved.reshape(2, 2, 2, tps, rows_attn, features)
    moved = pick(pick(moved, core, 1), tp, 2).reshape(4, rows_attn, features)
    gone = relative(moved, chip)
    v.moved = [gone[0]] + [swap_chip(gone[turn], turn) for turn in range(1, 4)]
    v.new = rows_between(v.new)
    v = hold(v)
    mixed = v.drop.summed
    result = (residual + mixed[0] + added(mixed[1], mixed[2])).astype(low)
    result = result.reshape(seqs, IMAGE, features)[:, :LEN].reshape(rows_here, features)
    scales_grad, shifts_grad = v.vectors[:2], v.vectors[2:]
    scales_state, scales_push = advance(scales_grad, scales_moment)
    shifts_state, shifts_push = advance(shifts_grad, shifts_moment)
    up_new, down_new = rows_in(*v.new)
    upward_new = upward.astype(jnp.float32) - 2.0 * up_new
    downward_new = downward.astype(jnp.float32) - down_new
    (upward_grad, upward_state), (downward_grad, downward_state) = v.states
    got = place_chips(v.moved, chip).astype(jnp.float32)
    inward_new = inward.astype(jnp.float32) - got[:3]
    outward_new = outward.astype(jnp.float32) - got[3]
    vector_rate = 0.6 / math.sqrt(devices * rows_here)
    scales_new = scales.astype(jnp.float32) - vector_rate * scales_push
    shifts_new = shifts.astype(jnp.float32) - vector_rate * shifts_push
    return (
        result[None],
        input_grad[None],
        inward_grad,
        outward_grad,
        scales_grad,
        shifts_grad,
        upward_grad,
        downward_grad,
        inward_state,
        outward_state,
        scales_state,
        shifts_state,
        upward_state,
        downward_state,
        inward_new,
        outward_new,
        scales_new,
        shifts_new,
        upward_new,
        downward_new,
    )


def solution(mesh):
    in_specs = (
        P(("shard", "tp"), "ctx", None),
        P(("shard", "tp"), "ctx", None),
        P(("shard", "tp"), "ctx", None),
        P(("shard", "tp"), "ctx", None),
        P(None, ("shard", "ctx", "tp"), None),
        P(("shard", "ctx", "tp"), None),
        P(None, ("shard", "ctx", "tp")),
        P(None, ("shard", "ctx", "tp")),
        P(None, ("shard", "ctx"), "tp"),
        P(None, ("shard", "ctx"), "tp"),
        P(None, ("shard", "ctx", "tp"), None),
        P(("shard", "ctx", "tp"), None),
        P(None, ("shard", "ctx", "tp")),
        P(None, ("shard", "ctx", "tp")),
        P(None, ("shard", "ctx"), "tp"),
        P(None, ("shard", "ctx"), "tp"),
    )
    out_specs = (
        P(("shard", "tp"), "ctx", None),
        P(("shard", "tp"), "ctx", None),
        P(None, ("shard", "ctx", "tp"), None),
        P(("shard", "ctx", "tp"), None),
        P(None, ("shard", "ctx", "tp")),
        P(None, ("shard", "ctx", "tp")),
        P(None, ("shard", "ctx"), "tp"),
        P(None, ("shard", "ctx"), "tp"),
        P(None, ("shard", "ctx", "tp"), None),
        P(("shard", "ctx", "tp"), None),
        P(None, ("shard", "ctx", "tp")),
        P(None, ("shard", "ctx", "tp")),
        P(None, ("shard", "ctx"), "tp"),
        P(None, ("shard", "ctx"), "tp"),
        P(None, ("shard", "ctx", "tp"), None),
        P(("shard", "ctx", "tp"), None),
        P(None, ("shard", "ctx", "tp")),
        P(None, ("shard", "ctx", "tp")),
        P(None, ("shard", "ctx"), "tp"),
        P(None, ("shard", "ctx"), "tp"),
    )
    body = plane_device if mesh.shape["shard"] == 4 and mesh.shape["ctx"] == 2 and mesh.shape["tp"] == 4 else on_device
    return jax.shard_map(
        body, mesh=mesh, in_specs=in_specs, out_specs=out_specs, check_vma=False
    )
```
